32 devices in a mesh: dp: 8 (over y, x, core), mp: 4 (over z).
Axes of the slice: x: 2, y: 2, z: 4, core: 2. Of those that a mesh axis runs over, the one named last changes fastest.
Arguments:
- tokens: bfloat16 [32768, 768], P('dp'), may hold values from -18 to 18, as said below
- cotangent: bfloat16 [32768, 768], P('dp'), may hold values from -20 to 20, as said below
- counts: int32 [8, 32], P('dp'), may hold values from 0 to 128, as said below
- attend_in: float32 [3, 2, 768, 2304], P(None, None, 'dp', 'mp'), as said below
- attend_out: float32 [3, 2, 768, 768], P(None, None, ('mp', 'dp')), as said below
- expand_in: float32 [3, 2, 768, 3072], P(None, None, 'dp', 'mp'), as said below
- expand_bias: float32 [3, 2, 3072], P(None, None, ('mp', 'dp')), as said below
- expand_out: float32 [3, 2, 3072, 768], P(None, None, ('mp', 'dp')), as said below
- affine_state: float32 [3, 2, 6, 768], P(None, None, None, 'dp'), as said below
- position_state: float32 [3, 32, 768], P(None, None, 'dp'), as said below
Outputs:
- out_tokens: bfloat16 [32768, 768], P('dp')
- input_grad: float32 [32768, 768], P('dp')
- grad_norm: float32 [], replicated
- new_attend_in: float32 [2, 768, 2304], P(None, 'dp', 'mp')
- new_attend_out: float32 [2, 768, 768], P(None, ('mp', 'dp'))
- new_expand_in: float32 [2, 768, 3072], P(None, 'dp', 'mp')
- new_expand_bias: float32 [2, 3072], P(None, ('mp', 'dp'))
- new_expand_out: float32 [2, 3072, 768], P(None, ('mp', 'dp'))
- new_affine_state: float32 [2, 6, 768], P(None, None, 'dp')
- new_position_state: float32 [32, 768], P(None, 'dp')
- first_attend_in: float32 [2, 768, 2304], P(None, 'dp', 'mp')
- first_attend_out: float32 [2, 768, 768], P(None, ('mp', 'dp'))
- first_expand_in: float32 [2, 768, 3072], P(None, 'dp', 'mp')
- first_expand_bias: float32 [2, 3072], P(None, ('mp', 'dp'))
- first_expand_out: float32 [2, 3072, 768], P(None, ('mp', 'dp'))
- first_affine_state: float32 [2, 6, 768], P(None, None, 'dp')
- first_position_state: float32 [32, 768], P(None, 'dp')
- second_attend_in: float32 [2, 768, 2304], P(None, 'dp', 'mp')
- second_attend_out: float32 [2, 768, 768], P(None, ('mp', 'dp'))
- second_expand_in: float32 [2, 768, 3072], P(None, 'dp', 'mp')
- second_expand_bias: float32 [2, 3072], P(None, ('mp', 'dp'))
- second_expand_out: float32 [2, 3072, 768], P(None, ('mp', 'dp'))
- second_affine_state: float32 [2, 6, 768], P(None, None, 'dp')
- second_position_state: float32 [32, 768], P(None, 'dp')
The draws below stay inside these ranges and needn't reach their ends.
Inputs may be any that keep to these rules, and one draw needn't show every extreme that they name: counts[d, s] = min(128, max(0, L - 128 * s)) for a document length L of 512 tokens or more; in every draw some document is full and some has an empty last segment. `tokens`: real values. `cotangent`: real values. `attend_in`: along the first dimension: master weight, first moment, second moment; second moments are positive. `attend_out`: along the first dimension: master weight, first moment, second moment; second moments are positive. `expand_in`: along the first dimension: master weight, first moment, second moment; second moments are positive. `expand_bias`: along the first dimension: master weight, first moment, second moment; second moments are positive. `expand_out`: along the first dimension: master weight, first moment, second moment; second moments are positive. `affine_state`: along the first dimension: master, first moment, second moment; second moments are positive. `position_state`: along the first dimension: master, first moment, second moment; second moments are positive.
All inputs are finite; a program needn't handle non-finite values.
Results may differ from the reference program's by a relative error of at most 0.024.
Values may be sent and summed in bfloat16 or wider, within the bound.
No kernel may reach another device: no remote copies, remote signals or barrier semaphores. Data moves between devices by JAX's collectives and lax.ppermute only.
A program may use at most 320 MiB of HBM per device.

```python
import jax
import jax.numpy as jnp
from jax import lax

D = 768
HEAD_DIM = 64
FF = 3072
SEG = 128
NSEG = 32
DOCS = 8
TOKENS = 32768
PARAMS = 14195712
N_MP = 4


def scaled_normal(key, shape, scale):
    return jax.random.truncated_normal(jax.random.fold_in(key, 5), -4.0, 4.0, shape, jnp.float32) * scale


def rising(key, lower, upper):
    place = jnp.arange(D, dtype=jnp.float32) / (D - 1.0)
    jitter = jax.random.uniform(jax.random.fold_in(key, 31), (D,), jnp.float32, 0.85, 1.15)
    return (lower + (upper - lower) * place) * jitter


def with_moments(key, master, factor):
    grad_size = factor * PARAMS ** (-0.5)
    first = jax.random.truncated_normal(jax.random.fold_in(key, 11), -4.0, 4.0, master.shape, jnp.float32) * (0.11 * grad_size)
    least = 0.001 * grad_size * grad_size
    level = jax.random.uniform(jax.random.fold_in(key, 12), master.shape, jnp.float32, 0.0, 1.0)
    second = least * jnp.exp(level * jnp.log(4.0))
    return jnp.stack([master, first, second])


def draw_tokens(key, part):
    columns = rising(key, 0.6, 1.8)
    base = jax.random.truncated_normal(jax.random.fold_in(key, 41), -6.0, 6.0, (TOKENS, D), jnp.float32)
    return (base * columns[None, :]).astype(jnp.bfloat16)


def draw_cotangent(key, part):
    base = jax.random.truncated_normal(jax.random.fold_in(key, 51), -6.0, 6.0, (DOCS, SEG * NSEG, D), jnp.float32)
    level = jax.random.uniform(jax.random.fold_in(key, 52), (DOCS, 1, 1), jnp.float32, jnp.log(0.7), jnp.log(1.4))
    place = jnp.arange(SEG * NSEG, dtype=jnp.int32)
    lift = jnp.where(place % SEG == 0, 2.0, 1.0).astype(jnp.float32)
    return (base * jnp.exp(level) * lift[None, :, None]).reshape(TOKENS, D).astype(jnp.bfloat16)


def draw_attend_in(key, part):
    return with_moments(key, scaled_normal(key, (2, D, 3 * D), D ** (-0.5)), 1.0)


def draw_attend_out(key, part):
    return with_moments(key, scaled_normal(key, (2, D, D), (D // 8) ** (-0.5)), 1.0)


def draw_expand_in(key, part):
    return with_moments(key, scaled_normal(key, (2, D, FF), D ** (-0.5)), 1.0)


def draw_expand_bias(key, part):
    return with_moments(key, scaled_normal(key, (2, FF), 0.5), 2.0)


def draw_expand_out(key, part):
    return with_moments(key, scaled_normal(key, (2, FF, D), FF ** (-0.5)), 1.0)


def draw_affine_state(key, part):
    which = jnp.arange(6).reshape(1, 6, 1) + jnp.zeros((2, 6, D), jnp.int32)
    ramp = rising(jax.random.fold_in(key, 61), 0.5, 1.5)
    gains = ramp[None, None, :] * jax.random.uniform(jax.random.fold_in(key, 6), (2, 6, D), jnp.float32, 0.9, 1.1)
    shifts = scaled_normal(key, (2, 6, D), 0.3)
    master = jnp.where((which == 0) | (which == 2), gains, shifts)
    return with_moments(key, master, 4.0)


def draw_position_state(key, part):
    return with_moments(key, scaled_normal(key, (NSEG, D), 0.5), 2.0)


def draw_counts(key, part):
    full = SEG * NSEG
    lengths = jax.random.randint(jax.random.fold_in(key, 21), (DOCS,), full // 8, full + 1)
    chosen = jax.random.randint(jax.random.fold_in(key, 22), (), 0, DOCS)
    other = (chosen + 1 + jax.random.randint(jax.random.fold_in(key, 23), (), 0, DOCS - 1)) % DOCS
    short = jax.random.randint(jax.random.fold_in(key, 24), (), full // 8, full // 2 + 1)
    index = jnp.arange(DOCS)
    lengths = jnp.where(index == chosen, full, lengths)
    lengths = jnp.where(index == other, short, lengths)
    starts = SEG * jnp.arange(NSEG)
    return jnp.clip(lengths[:, None] - starts[None, :], 0, SEG).astype(jnp.int32)


def setup_inputs(seed: int = 0) -> dict:
    seeds = jax.random.split(jax.random.key(seed), 11)
    return {
        "tokens": draw_tokens(jax.random.fold_in(seeds[10], 71), 0),
        "cotangent": draw_cotangent(jax.random.fold_in(seeds[10], 71), 0),
        "counts": draw_counts(jax.random.fold_in(seeds[10], 71), 0),
        "attend_in": draw_attend_in(jax.random.fold_in(seeds[10], 71), 0),
        "attend_out": draw_attend_out(jax.random.fold_in(seeds[10], 71), 0),
        "expand_in": draw_expand_in(jax.random.fold_in(seeds[10], 71), 0),
        "expand_bias": draw_expand_bias(jax.random.fold_in(seeds[10], 71), 0),
        "expand_out": draw_expand_out(jax.random.fold_in(seeds[10], 71), 0),
        "affine_state": draw_affine_state(jax.random.fold_in(seeds[10], 71), 0),
        "position_state": draw_position_state(jax.random.fold_in(seeds[10], 71), 0),
    }


HIGH = lax.Precision.HIGHEST
norm_eps = 1e-05
clip_level = 1.0
rate = 0.02
decay = 0.01
beta_one = 0.9
beta_two = 0.999
adam_eps = 1e-08
adam_step = 10

@jax.custom_vjp
def low(v):
    return lax.optimization_barrier(v.astype(jnp.bfloat16)).astype(jnp.float32)

@jax.custom_vjp
def low_back(v):
    return v

def low_keep(v):
    return (low(v), None)

def low_pass(kept, grad):
    return (grad,)

def back_keep(v):
    return (v, None)

def back_low(kept, grad):
    return (low(grad),)
low.defvjp(low_keep, low_pass)
low_back.defvjp(back_keep, back_low)

def layer_norm(values, gain, shift):
    mean = lax.optimization_barrier(jnp.mean(values, axis=-1, keepdims=True))
    centred = values - mean
    spread = lax.optimization_barrier(jnp.mean(centred * centred, axis=-1, keepdims=True))
    return centred * lax.rsqrt(spread + norm_eps) * gain + shift

def attend(triple, keep, span):
    rows = triple.shape[0]
    heads = triple.shape[1] // (3 * HEAD_DIM)
    parts = triple.reshape(rows // span, span, heads, 3, HEAD_DIM)
    query = parts[:, :, :, 0] * HEAD_DIM ** (-0.5)
    key = parts[:, :, :, 1]
    value = parts[:, :, :, 2]
    scores = jnp.einsum('bqhe,bkhe->bhqk', query, key, precision=HIGH)
    live = keep.reshape(rows // span, 1, 1, span) > 0.5
    scores = low_back(jnp.where(live, scores, -1e+30))
    top = lax.optimization_barrier(jnp.max(scores, axis=-1, keepdims=True))
    weights = jnp.exp(scores - top)
    probs = low(weights / lax.optimization_barrier(jnp.sum(weights, axis=-1, keepdims=True)))
    context = jnp.einsum('bhqk,bkhe->bqhe', probs, value, precision=HIGH)
    return context.reshape(rows, heads * HEAD_DIM)

def layer(inputs, keep, span, attend_in, attend_out, expand_in, expand_bias, expand_out, affine):
    unit = low(inputs)
    in_cols = attend_in.shape[1] // N_MP
    head_rows = attend_out.shape[0] // N_MP
    units = expand_in.shape[1] // N_MP
    mixed = jnp.zeros_like(inputs)
    for group in range(N_MP):
        piece = low_back(unit)
        triple = low_back(low(jnp.dot(piece, attend_in[:, group * in_cols:(group + 1) * in_cols], precision=HIGH)))
        context = low_back(low(attend(triple, keep, span)))
        mixed = mixed + low(jnp.dot(context, attend_out[group * head_rows:(group + 1) * head_rows], precision=HIGH))
    resid = inputs + low_back(mixed) + affine[4]
    hidden = layer_norm(resid, affine[0], affine[1])
    hid_low = low(hidden)
    returned = jnp.zeros_like(inputs)
    for group in range(N_MP):
        piece = low_back(hid_low)
        lower = group * units
        upper = (group + 1) * units
        expanded = low_back(jnp.dot(piece, expand_in[:, lower:upper], precision=HIGH)) + expand_bias[lower:upper]
        activated = low(jax.nn.gelu(expanded))
        returned = returned + low(jnp.dot(activated, expand_out[lower:upper], precision=HIGH))
    resid_two = hidden + low_back(returned) + affine[5]
    return layer_norm(resid_two, affine[2], affine[3])

def adam(state, grad, factor):
    clipped = grad * factor
    first = beta_one * state[1] + (1.0 - beta_one) * clipped
    second = beta_two * state[2] + (1.0 - beta_two) * clipped * clipped
    fixed_first = first / (1.0 - beta_one ** adam_step)
    fixed_second = second / (1.0 - beta_two ** adam_step)
    master = state[0] - rate * (fixed_first / (jnp.sqrt(fixed_second) + adam_eps) + decay * state[0])
    return (master, first, second)

def reference(tokens, cotangent, counts, attend_in, attend_out, expand_in, expand_bias, expand_out, affine_state, position_state):
    states = (attend_in, attend_out, expand_in, expand_bias, expand_out, affine_state, position_state)
    working = tuple((state[0].astype(jnp.bfloat16).astype(jnp.float32) for state in states))
    doc_tokens = tokens.reshape(DOCS, NSEG * SEG, D)
    doc_pulls = cotangent.reshape(DOCS, NSEG * SEG, D)
    spot = jnp.arange(SEG, dtype=jnp.int32)

    def one_doc(total, item):
        this_doc, this_pull, this_count = item
        keep_tok = (spot[None, :] < this_count[:, None]).astype(jnp.float32).reshape(NSEG * SEG)
        keep_seg = (this_count > 0).astype(jnp.float32)

        def model(values, params):
            w_in, w_out, w_up, b_up, w_down, affine, position = params
            first = layer(values, keep_tok, SEG, w_in[0], w_out[0], w_up[0], b_up[0], w_down[0], affine[0])
            grid = first.reshape(NSEG, SEG, D)
            heads_in = grid[:, 0] + position
            second = layer(heads_in, keep_seg, NSEG, w_in[1], w_out[1], w_up[1], b_up[1], w_down[1], affine[1])
            merged = grid.at[:, 0].set(second).reshape(NSEG * SEG, D)
            return merged * keep_tok[:, None]
        result, pull = jax.vjp(model, this_doc.astype(jnp.float32), working)
        grad_doc, grad_params = pull(this_pull.astype(jnp.float32))
        total = tuple((left + right for left, right in zip(total, grad_params)))
        return (total, (result.astype(jnp.bfloat16), grad_doc))
    zeros = tuple((jnp.zeros_like(value) for value in working))
    grads, (results, grad_docs) = lax.scan(one_doc, zeros, (doc_tokens, doc_pulls, counts))
    squares = jnp.sum(grads[0] * grads[0])
    for grad in grads[1:]:
        squares = squares + jnp.sum(grad * grad)
    grad_norm = jnp.sqrt(squares)
    factor = jnp.minimum(1.0, clip_level / grad_norm)
    updated = [adam(state, grad, factor) for state, grad in zip(states, grads)]
    out_tokens = results.reshape(TOKENS, D)
    input_grad = grad_docs.reshape(TOKENS, D)
    return (out_tokens, input_grad, grad_norm, updated[0][0], updated[1][0], updated[2][0], updated[3][0], updated[4][0], updated[5][0], updated[6][0], updated[0][1], updated[1][1], updated[2][1], updated[3][1], updated[4][1], updated[5][1], updated[6][1], updated[0][2], updated[1][2], updated[2][2], updated[3][2], updated[4][2], updated[5][2], updated[6][2])
```

```python
import jax
import jax.numpy as jnp
from jax import lax
from jax.sharding import PartitionSpec as P

HEAD_DIM = 64
SEG = 128
NSEG = 32


norm_eps = 1e-05
clip_level = 1.0
rate = 0.02
decay = 0.01
beta_one = 0.9
beta_two = 0.999
adam_eps = 1e-08
adam_step = 10


def layer_norm(values, gain, shift):
    mean = jnp.mean(values, axis=-1, keepdims=True)
    centred = values - mean
    spread = jnp.mean(centred * centred, axis=-1, keepdims=True)
    return centred * lax.rsqrt(spread + norm_eps) * gain + shift


def matmul(left, right):
    return jnp.dot(left, right, preferred_element_type=jnp.float32)


def matmul_tn(left, right):
    return lax.dot_general(
        left, right, (((0,), (0,)), ((), ())), preferred_element_type=jnp.float32
    )


def matmul_nt(left, right):
    return lax.dot_general(
        left, right, (((1,), (1,)), ((), ())), preferred_element_type=jnp.float32
    )


def split_heads(triple, span):
    rows = triple.shape[0]
    heads = triple.shape[1] // (3 * HEAD_DIM)
    parts = triple.reshape(rows // span, span, heads, 3, HEAD_DIM)
    return (parts[:, :, :, 0], parts[:, :, :, 1], parts[:, :, :, 2])


def scores_of(query, key, keep, span):
    raw = jnp.einsum(
        "bqhe,bkhe->bhqk", query, key, preferred_element_type=jnp.float32
    ) * HEAD_DIM ** (-0.5)
    live = keep.reshape(-1, 1, 1, span) > 0.5
    return jnp.where(live, raw, -1e30)


def attend(triple, keep, span):
    query, key, value = split_heads(triple, span)
    scores = scores_of(query, key, keep, span)
    top = jnp.max(scores, axis=-1, keepdims=True)
    weights = jnp.exp(scores - top)
    total = jnp.sum(weights, axis=-1, keepdims=True)
    probs = (weights / total).astype(jnp.bfloat16)
    context = jnp.einsum("bhqk,bkhe->bqhe", probs, value, preferred_element_type=jnp.float32)
    return (context.reshape(triple.shape[0], -1).astype(jnp.bfloat16), top, total)


def attend_back(triple, keep, span, top, total, grad_context):
    query, key, value = split_heads(triple, span)
    scores = scores_of(query, key, keep, span)
    probs = jnp.exp(scores - top) / total
    grad_ctx = grad_context.reshape(query.shape)
    grad_probs = jnp.einsum("bqhe,bkhe->bhqk", grad_ctx, value, preferred_element_type=jnp.float32)
    inner = jnp.sum(probs * grad_probs, axis=-1, keepdims=True)
    grad_scores = (probs * (grad_probs - inner)).astype(jnp.bfloat16)
    scale = HEAD_DIM ** (-0.5)
    grad_query = (
        jnp.einsum("bhqk,bkhe->bqhe", grad_scores, key, preferred_element_type=jnp.float32) * scale
    )
    grad_key = (
        jnp.einsum("bhqk,bqhe->bkhe", grad_scores, query, preferred_element_type=jnp.float32)
        * scale
    )
    grad_value = jnp.einsum(
        "bhqk,bqhe->bkhe", probs.astype(jnp.bfloat16), grad_ctx, preferred_element_type=jnp.float32
    )
    stacked = jnp.stack([grad_query, grad_key, grad_value], axis=3)
    return stacked.reshape(triple.shape).astype(jnp.bfloat16)


def share_sum(value, axis):
    if axis is None:
        return value
    return lax.psum(value.astype(jnp.bfloat16), axis).astype(jnp.float32)


def forward(inputs, keep, span, weights, axis):
    w_in, w_out, w_up, b_up, w_down, affine = weights
    affine = affine.astype(jnp.float32)
    unit = inputs.astype(jnp.bfloat16)
    triple = matmul(unit, w_in).astype(jnp.bfloat16)
    context, top, total = attend(triple, keep, span)
    mixed = share_sum(matmul(context, w_out), axis)
    resid = inputs + mixed + affine[4]
    hidden = layer_norm(resid, affine[0], affine[1])
    hid_low = hidden.astype(jnp.bfloat16)
    expanded = matmul(hid_low, w_up) + b_up.astype(jnp.float32)
    activated = jax.nn.gelu(expanded).astype(jnp.bfloat16)
    returned = share_sum(matmul(activated, w_down), axis)
    resid_two = hidden + returned + affine[5]
    output = layer_norm(resid_two, affine[2], affine[3])
    cache = (unit, triple, top, total, context, resid, hid_low, expanded, activated, resid_two)
    return (output, cache)


def backward(grad_out, cache, keep, span, weights, axis):
    w_in, w_out, w_up, b_up, w_down, affine = weights
    affine = affine.astype(jnp.float32)
    unit, triple, top, total, context, resid, hid_low, expanded, activated, resid_two = cache
    pull_two = jax.vjp(layer_norm, resid_two, affine[2], affine[3])[1]
    grad_resid_two, grad_gain_two, grad_shift_two = pull_two(grad_out)
    grad_returned = grad_resid_two.astype(jnp.bfloat16)
    grad_down = matmul_tn(activated, grad_returned)
    grad_act = matmul_nt(grad_returned, w_down)
    pull_act = jax.vjp(jax.nn.gelu, expanded)[1]
    grad_expanded = pull_act(grad_act)[0]
    grad_exp_low = grad_expanded.astype(jnp.bfloat16)
    grad_up = matmul_tn(hid_low, grad_exp_low)
    grad_hidden = grad_resid_two + share_sum(matmul_nt(grad_exp_low, w_up), axis)
    pull_one = jax.vjp(layer_norm, resid, affine[0], affine[1])[1]
    grad_resid, grad_gain_one, grad_shift_one = pull_one(grad_hidden)
    grad_mixed = grad_resid.astype(jnp.bfloat16)
    grad_wout = matmul_tn(context, grad_mixed)
    grad_context = matmul_nt(grad_mixed, w_out).astype(jnp.bfloat16)
    grad_triple = attend_back(triple, keep, span, top, total, grad_context)
    grad_win = matmul_tn(unit, grad_triple)
    grad_inputs = grad_resid + share_sum(matmul_nt(grad_triple, w_in), axis)
    grad_affine = jnp.stack(
        [
            grad_gain_one,
            grad_shift_one,
            grad_gain_two,
            grad_shift_two,
            jnp.sum(grad_resid, axis=0),
            jnp.sum(grad_resid_two, axis=0),
        ]
    )
    return (
        grad_inputs,
        (grad_win, grad_wout, grad_up, jnp.sum(grad_expanded, axis=0), grad_down, grad_affine),
    )


def adam(state, grad, factor):
    clipped = grad * factor
    first = beta_one * state[1] + (1.0 - beta_one) * clipped
    second = beta_two * state[2] + (1.0 - beta_two) * clipped * clipped
    fixed_first = first / (1.0 - beta_one**adam_step)
    fixed_second = second / (1.0 - beta_two**adam_step)
    master = state[0] - rate * (
        fixed_first / (jnp.sqrt(fixed_second) + adam_eps) + decay * state[0]
    )
    return (master, first, second)


def shards(
    tokens,
    cotangent,
    counts,
    attend_in,
    attend_out,
    expand_in,
    expand_bias,
    expand_out,
    affine_state,
    position_state,
):
    low = jnp.bfloat16
    groups = lax.axis_size("mp")
    mine = lax.axis_index("mp")

    def spread(state, layer, axes, dim):
        value = state[0, layer].astype(low)
        for axis in axes:
            value = lax.all_gather(value, axis, axis=dim[axis], tiled=True)
        return value

    cols = {"dp": 0, "mp": 1}
    rows = {"dp": 0, "mp": 0}
    affine = lax.all_gather(affine_state[0].astype(low), "dp", axis=2, tiled=True)
    position = lax.all_gather(position_state[0].astype(low), "dp", axis=1, tiled=True)
    position = position.astype(jnp.float32)
    layers = []
    for layer, axes in enumerate([("dp", "mp"), ("dp",)]):
        layers.append(
            (
                spread(attend_in, layer, axes, cols),
                spread(attend_out, layer, axes, rows),
                spread(expand_in, layer, axes, cols),
                spread(expand_bias, layer, axes, rows),
                spread(expand_out, layer, axes, rows),
                affine[layer],
            )
        )
    layer_one, layer_two = layers
    docs_here = counts.shape[0]
    segments = docs_here * NSEG
    here = segments // groups
    spot = lax.broadcasted_iota(jnp.int32, (docs_here, NSEG, SEG), 2)
    keep_tokens = (spot < counts[:, :, None]).astype(jnp.float32).reshape(-1)
    keep_heads = (counts > 0).astype(jnp.float32).reshape(-1)

    def part(value):
        size = value.shape[0] // groups
        return lax.dynamic_slice_in_dim(value, mine * size, size)

    keep_part = part(keep_tokens)
    inputs = part(tokens).astype(jnp.float32)
    first, cache_one = forward(inputs, keep_part, SEG, layer_one, None)
    grid = first.reshape(here, SEG, -1)
    heads = lax.all_gather(grid[:, 0], "mp", axis=0, tiled=True)
    heads_in = (heads.reshape(docs_here, NSEG, -1) + position[None]).reshape(segments, -1)
    second, cache_two = forward(heads_in, keep_heads, NSEG, layer_two, "mp")
    merged = grid.at[:, 0].set(part(second)).reshape(first.shape) * keep_part[:, None]
    merged = lax.all_gather(merged.astype(low), "mp", axis=0, tiled=True)
    grad_out = part(cotangent).astype(jnp.float32) * keep_part[:, None]
    top_grad = cotangent.reshape(segments, SEG, -1)[:, 0].astype(jnp.float32) * keep_heads[:, None]
    grad_heads, grads_two = backward(top_grad, cache_two, keep_heads, NSEG, layer_two, "mp")
    grad_position = jnp.sum(grad_heads.reshape(docs_here, NSEG, -1), axis=0)
    grad_grid = grad_out.reshape(here, SEG, -1)
    grad_first = grad_grid.at[:, 0].set(part(grad_heads)).reshape(grad_out.shape)
    grad_inputs, grads_one = backward(grad_first, cache_one, keep_part, SEG, layer_one, None)
    grad_inputs = lax.all_gather(
        (grad_inputs * keep_part[:, None]).astype(low), "mp", axis=0, tiled=True
    ).astype(jnp.float32)

    def collect(value, axes, dim):
        value = value.astype(low)
        for axis in axes:
            value = lax.psum_scatter(value, axis, scatter_dimension=dim[axis], tiled=True)
        return value.astype(jnp.float32)

    shares = []
    for which, dim in enumerate([cols, rows, cols, rows, rows]):
        shares.append(
            jnp.stack(
                [
                    collect(grads_one[which], ("mp", "dp"), dim),
                    collect(grads_two[which], ("dp",), dim),
                ]
            )
        )
    grad_affine = jnp.stack([lax.psum(grads_one[5], "mp"), grads_two[5]])
    shares.append(collect(grad_affine, ("dp",), {"dp": 2}))
    shares.append(collect(grad_position, ("dp",), {"dp": 1}))
    matrix_squares = jnp.sum(shares[0] * shares[0])
    for member in shares[1:5]:
        matrix_squares = matrix_squares + jnp.sum(member * member)
    small_squares = jnp.sum(shares[5] * shares[5]) + jnp.sum(shares[6] * shares[6])
    leader = (lax.axis_index("mp") == 0).astype(jnp.float32)
    total_squares = lax.psum(matrix_squares + leader * small_squares, ("dp", "mp"))
    grad_norm = jnp.sqrt(total_squares)
    factor = jnp.minimum(1.0, clip_level / grad_norm)
    states = (
        attend_in,
        attend_out,
        expand_in,
        expand_bias,
        expand_out,
        affine_state,
        position_state,
    )
    updated = [adam(state, share, factor) for state, share in zip(states, shares)]
    masters = [item[0] for item in updated]
    firsts = [item[1] for item in updated]
    seconds = [item[2] for item in updated]
    head = [merged, grad_inputs, grad_norm]
    return tuple(head + masters + firsts + seconds)


def solution(mesh):
    in_specs = (
        P("dp", None),
        P("dp", None),
        P("dp", None),
        P(None, None, "dp", "mp"),
        P(None, None, ("mp", "dp"), None),
        P(None, None, "dp", "mp"),
        P(None, None, ("mp", "dp")),
        P(None, None, ("mp", "dp"), None),
        P(None, None, None, "dp"),
        P(None, None, "dp"),
    )
    out_specs = (
        P("dp", None),
        P("dp", None),
        P(),
        P(None, "dp", "mp"),
        P(None, ("mp", "dp"), None),
        P(None, "dp", "mp"),
        P(None, ("mp", "dp")),
        P(None, ("mp", "dp"), None),
        P(None, None, "dp"),
        P(None, "dp"),
        P(None, "dp", "mp"),
        P(None, ("mp", "dp"), None),
        P(None, "dp", "mp"),
        P(None, ("mp", "dp")),
        P(None, ("mp", "dp"), None),
        P(None, None, "dp"),
        P(None, "dp"),
        P(None, "dp", "mp"),
        P(None, ("mp", "dp"), None),
        P(None, "dp", "mp"),
        P(None, ("mp", "dp")),
        P(None, ("mp", "dp"), None),
        P(None, None, "dp"),
        P(None, "dp"),
    )
    return jax.shard_map(shards, mesh=mesh, in_specs=in_specs, out_specs=out_specs, check_vma=False)
```

```python
import functools

import jax
import jax.numpy as jnp
from jax import lax
from jax.experimental import pallas as pl
from jax.experimental.pallas import tpu as pltpu
from jax.sharding import PartitionSpec as P

LOW = jnp.bfloat16
FULL = jnp.float32
HEAD_DIM = 64
SEG = 128
NSEG = 32
norm_eps = 1e-05
clip_level = 1.0
rate = 0.02
decay = 0.01
beta_one = 0.9
beta_two = 0.999
adam_eps = 1e-08
adam_step = 10
LANES = 2 * HEAD_DIM
TANH_A = 0.7978845608028654
TANH_B = 0.044715
VMEM_BYTES = 60 * 1024 * 1024
FLOPS = 1.15e9


def dot_nn(a, b):
    return lax.dot_general(a, b, (((1,), (0,)), ((), ())), preferred_element_type=FULL)


def dot_nt(a, b):
    return lax.dot_general(a, b, (((1,), (1,)), ((), ())), preferred_element_type=FULL)


def dot_tn(a, b):
    return lax.dot_general(a, b, (((0,), (0,)), ((), ())), preferred_element_type=FULL)


def normal(values):
    mean = jnp.mean(values, axis=-1, keepdims=True)
    centred = values - mean
    spread = jnp.mean(centred * centred, axis=-1, keepdims=True)
    scale = lax.rsqrt(spread + norm_eps)
    return centred * scale, scale


def normal_back(grad, unit, scale, gain):
    scaled = grad * gain
    one = jnp.mean(scaled, axis=-1, keepdims=True)
    two = jnp.mean(scaled * unit, axis=-1, keepdims=True)
    return scale * (scaled - one - unit * two)


def halves(block, low):
    zero = jnp.zeros_like(block)
    return jnp.concatenate([jnp.where(low, block, zero), jnp.where(low, zero, block)], axis=0)


def soft(query, keys, live, span):
    scores = jnp.where(live, dot_nt(query, keys), -1e30)
    parts = []
    for half in range(2):
        piece = scores[:, half * span : (half + 1) * span]
        weights = jnp.exp(piece - jnp.max(piece, axis=-1, keepdims=True))
        parts.append(weights * (1.0 / jnp.sum(weights, axis=-1, keepdims=True)))
    return parts


class Plan:
    def __init__(self, groups, pieces, rows, mp_at, dp_at, count=1):
        self.groups, self.pieces, self.rows = groups, pieces, rows
        self.mp_at, self.dp_at = mp_at, dp_at
        self.count = count

    def copies(self):
        return sum(len(places) for places, _ in self.pieces) * (self.groups // 2)


def fetch(plan, info, pieces, land, sems):
    size = plan.rows
    copies = []
    for (places, half), piece in zip(plan.pieces, pieces):
        for at, place in enumerate(places):
            start = pl.multiple_of(info[plan.dp_at + place] * size, 16)
            for inner in range(piece.shape[1]):
                copy = pltpu.make_async_copy(
                    piece.at[at, inner],
                    land(half * piece.shape[1] + inner, start, size),
                    sems.at[len(copies)],
                )
                copy.start()
                copies.append(copy)
    return copies


def padded(count):
    return -(-count // 16) * 16


def wait_all(copies):
    for copy in copies:
        copy.wait()


def turn(block):
    return jnp.concatenate([block[:, HEAD_DIM:], block[:, :HEAD_DIM]], axis=1)


def fetch_units(sections, up_all, down_all, w_up, w_down, sems):
    width = w_down.shape[1]
    copies = []
    for kind, (source, (base, size)) in enumerate(zip((up_all, down_all), sections)):
        for m in range(source.shape[0]):
            for at in range(source.shape[1]):
                if kind:
                    target = w_down.at[pl.ds(m * width + at * size, size), :]
                else:
                    target = w_up.at[pl.ds(at * size, size), m * width : (m + 1) * width]
                copy = pltpu.make_async_copy(
                    source.at[m, at, pl.ds(base, size), :],
                    target,
                    sems.at[kind, m * source.shape[1] + at],
                )
                copy.start()
                copies.append(copy)
    return copies


def fetch_out(section, plan, info, out_all, stage, sems):
    base, size = section
    copies = []
    for m in range(plan.groups):
        for at in range(out_all.shape[1]):
            copy = pltpu.make_async_copy(
                out_all.at[info[plan.mp_at + m], at, pl.ds(base, size), :],
                stage.at[m, pl.ds(at * size, size), :],
                sems.at[len(copies)],
            )
            copy.start()
            copies.append(copy)
    return copies


def pair_columns(stage, w_in):
    groups, width = stage.shape[:2]
    low = lax.broadcasted_iota(jnp.int32, (width, LANES), 1) < HEAD_DIM
    for part in range(3):
        base = part * width
        for m in range(groups):
            at = base + m * LANES
            w_in[:, at : at + LANES] = stage[m, :, part * LANES : (part + 1) * LANES]
        for m in range(0, groups, 2):
            at = base + (groups + m // 2) * LANES
            source = slice(3 * LANES, 4 * LANES) if part < 2 else slice(4 * LANES, 5 * LANES)
            left, right = stage[m, :, source], stage[m + 1, :, source]
            if part == 1:
                left = turn(left)
            else:
                right = turn(right)
            w_in[:, at : at + LANES] = jnp.where(low, left, right)


def pair_rows(stage, w_out, count):
    groups, rows = stage.shape[:2]
    share = w_out.shape[0] // groups // count
    step = rows // count
    for m in range(groups):
        parts = [stage[m, at * step : (at + 1) * step, :].astype(FULL)[:share] for at in range(count)]
        found = jnp.concatenate(parts, axis=0).astype(LOW)
        w_out[m * LANES : (m + 1) * LANES, :] = found[:LANES]
        goal = groups * LANES + m * HEAD_DIM
        w_out[goal : goal + HEAD_DIM, :] = found[LANES:]


def columns_of(block):
    at = [block[:, i * HEAD_DIM : (i + 1) * HEAD_DIM] for i in range(9)]
    order = ((0, 3), (1, 4), (2, 5), (6, 7))
    return [jnp.concatenate([at[i], at[j]], axis=1) for i, j in order] + [at[8]]


def heads_block_kernel(info, attend_in, bias, affine, position, out, small):
    rows = attend_in.shape[2]
    small[...] = jnp.zeros_like(small)
    small[0:6, :rows] = affine[0, 0]
    small[6:8, :rows] = bias[0]
    small[8:14, :rows] = affine[0, 1]
    small[16 : 16 + NSEG, :rows] = position[0]
    blocks = columns_of(attend_in[0, 0])
    blocks[4] = jnp.concatenate([blocks[4], small[...].T[:rows, :HEAD_DIM]], axis=1)
    for at, block in enumerate(blocks):
        out[:, at * LANES : (at + 1) * LANES] = block.astype(LOW)


def units_block_kernel(info, *refs):
    ins, out = refs[:-1], refs[-1]
    start = 0
    for source in ins:
        block = source[0, 0]
        rows = block.shape[0]
        if block.shape[1] != out.shape[1]:
            blocks = columns_of(block)
            blocks[4] = jnp.concatenate([blocks[4], jnp.zeros((rows, HEAD_DIM), FULL)], axis=1)
            blocks.append(jnp.zeros((rows, LANES), FULL))
            block = jnp.concatenate(blocks, axis=1)
        if padded(rows) > rows:
            block = jnp.concatenate([block, jnp.zeros((padded(rows) - rows, out.shape[1]), FULL)], axis=0)
        out[start : start + padded(rows), :] = block.astype(LOW)
        start += padded(rows)


def attend_kernel(plan, info, tok, *refs):
    pieces, refs = refs[:-9], refs[-9:]
    triple, context, w_in, affine_one, affine_two, position, b_up, stage, sems = refs
    step = pl.program_id(0)
    rows, width = tok.shape

    @pl.when(step == 0)
    def _():
        def land(m, start, size):
            return stage.at[m, pl.ds(start, size), :]

        wait_all(fetch(plan, info, pieces, land, sems))
        for m in range(plan.groups):
            small = stage[m, :, 4 * LANES : 5 * LANES].astype(FULL).T
            place = pl.multiple_of(info[plan.mp_at + m] * width, LANES)
            b_up[:, pl.ds(place, width)] = small[HEAD_DIM + 6 : HEAD_DIM + 7]
            if m == 0:
                affine_one[...] = small[HEAD_DIM : HEAD_DIM + 8]
                affine_two[...] = small[HEAD_DIM + 8 : HEAD_DIM + 16]
                position[...] = small[HEAD_DIM + 16 : HEAD_DIM + 16 + NSEG]
        pair_columns(stage, w_in)

    triple[...] = dot_nn(tok[...], w_in[...]).astype(LOW)
    low = lax.broadcasted_iota(jnp.int32, (SEG, LANES), 1) < HEAD_DIM
    spot = lax.broadcasted_iota(jnp.int32, (SEG, 2 * SEG), 1) % SEG
    for seg in range(rows // SEG):
        live = spot < info[step * (rows // SEG) + seg]
        here = slice(seg * SEG, (seg + 1) * SEG)
        for pair in range(width // LANES):
            at = pair * LANES
            query = triple[here, at : at + LANES] * LOW(HEAD_DIM ** (-0.5))
            keys = halves(triple[here, width + at : width + at + LANES], low)
            values = halves(triple[here, 2 * width + at : 2 * width + at + LANES], low)
            probs = jnp.concatenate([part.astype(LOW) for part in soft(query, keys, live, SEG)], axis=1)
            context[here, at : at + LANES] = dot_nn(probs, values).astype(LOW)


def feed_kernel(plan, sections, info, tok, context, affine, b_up, up_all, down_all, out_all, *refs):
    resid, hid_low, expanded, resid_two, first, tops, w_out, w_up, w_down, stage, sems, out_sems = refs
    step = pl.program_id(0)
    rows, width = tok.shape
    segs = rows // SEG

    @pl.when(step == 0)
    def _():
        outs = fetch_out(sections[2], plan, info, out_all, stage, out_sems)
        copies = fetch_units(sections[:2], up_all, down_all, w_up, w_down, sems)
        wait_all(outs)
        pair_rows(stage, w_out, plan.count)
        wait_all(copies)

    mixed = dot_nn(context[...], w_out[...])
    value = tok[...].astype(FULL) + mixed + affine[4:5, :]
    resid[...] = value
    hidden = normal(value)[0] * affine[0:1, :] + affine[1:2, :]
    low = hidden.astype(LOW)
    hid_low[...] = low
    total = hidden + affine[5:6, :]
    units = w_up.shape[1]
    block = width
    for at in range(0, units, block):
        up = dot_nn(low, w_up[:, at : at + block]) + b_up[:, at : at + block]
        expanded[:, at : at + block] = up.astype(LOW)
        curve = jnp.tanh(TANH_A * (up + TANH_B * up * up * up))
        active = (0.5 * up * (1.0 + curve)).astype(LOW)
        total = total + dot_nn(active, w_down[at : at + block, :])
    resid_two[...] = total
    result = normal(total)[0] * affine[2:3, :] + affine[3:4, :]
    row = lax.broadcasted_iota(jnp.int32, (SEG, 1), 0)
    for seg in range(segs):
        piece = result[seg * SEG : (seg + 1) * SEG, :]
        kept = jnp.where(row < info[step * segs + seg], piece, 0.0)
        first[seg * SEG : (seg + 1) * SEG, :] = kept.astype(LOW)
        tops[pl.ds(step * segs + seg, 1), :] = piece[0:1, :]


def feed_back_kernel(plan, sections, info, cot, back_heads, resid_two, expanded, resid, affine, *refs):
    ring, refs = refs[: plan.groups], refs[plan.groups :]
    up_all, down_all, grad_resid, active, grad_exp, grad_ret, grad_mixed, sums, bias = refs[:9]
    heads, w_up, w_down, sems = refs[9:]
    step = pl.program_id(0)
    rows, width = cot.shape
    segs = rows // SEG

    @pl.when(step == 0)
    def _():
        copies = fetch_units(sections[:2], up_all, down_all, w_up, w_down, sems)
        total = back_heads[...]
        for member in ring:
            total = total + member[...].astype(FULL)
        heads[...] = total
        wait_all(copies)

    row = lax.broadcasted_iota(jnp.int32, (SEG, 1), 0)
    first = info[plan.mp_at] * (pl.num_programs(0) * segs) + step * segs
    pieces = []
    for seg in range(segs):
        piece = cot[seg * SEG : (seg + 1) * SEG, :].astype(FULL)
        piece = jnp.where(row < info[step * segs + seg], piece, 0.0)
        pieces.append(jnp.where(row == 0, heads[pl.ds(first + seg, 1), :], piece))
    grad = jnp.concatenate(pieces, axis=0)
    unit, scale = normal(resid_two[...])

    @pl.when(step == 0)
    def _():
        sums[...] = jnp.zeros_like(sums)
        bias[...] = jnp.zeros_like(bias)

    back = normal_back(grad, unit, scale, affine[2:3, :])
    sums[2:3, :] += jnp.sum(grad * unit, axis=0, keepdims=True)
    sums[3:4, :] += jnp.sum(grad, axis=0, keepdims=True)
    sums[5:6, :] += jnp.sum(back, axis=0, keepdims=True)
    low = back.astype(LOW)
    grad_ret[...] = low
    units = w_up.shape[1]
    total = back
    block = width
    for at in range(0, units, block):
        grad_act = dot_nt(low, w_down[at : at + block, :])
        up = expanded[:, at : at + block].astype(FULL)
        square = up * up
        curve = jnp.tanh(TANH_A * (up + TANH_B * up * square))
        half = 0.5 * (1.0 + curve)
        active[:, at : at + block] = (up * half).astype(LOW)
        slope = half + 0.5 * up * (1.0 - curve * curve) * (TANH_A + 3.0 * TANH_A * TANH_B * square)
        wide = slope * grad_act
        bias[:, at : at + block] += jnp.sum(wide, axis=0, keepdims=True)
        short = wide.astype(LOW)
        grad_exp[:, at : at + block] = short
        total = total + dot_nt(short, w_up[:, at : at + block])
    unit, scale = normal(resid[...])
    back = normal_back(total, unit, scale, affine[0:1, :])
    sums[0:1, :] += jnp.sum(total * unit, axis=0, keepdims=True)
    sums[1:2, :] += jnp.sum(total, axis=0, keepdims=True)
    sums[4:5, :] += jnp.sum(back, axis=0, keepdims=True)
    grad_resid[...] = back
    grad_mixed[...] = back.astype(LOW)


def pair_back(query, keys, values, probs, down, low, span):
    grad_probs = dot_nt(down, values)
    scores = []
    for half in range(2):
        mine = probs[half]
        given = grad_probs[:, half * span : (half + 1) * span]
        product = mine * given
        inner = jnp.sum(product, axis=-1, keepdims=True)
        scores.append((product - mine * inner).astype(LOW))
    grad_scores = jnp.concatenate(scores, axis=1)
    probs = jnp.concatenate([part.astype(LOW) for part in probs], axis=1)
    grad_query = dot_nn(grad_scores, keys) * HEAD_DIM ** (-0.5)
    both = dot_tn(grad_scores, query)
    grad_key = jnp.where(low, both[:span], both[span:])
    both = dot_tn(probs, down)
    return grad_query, grad_key, jnp.where(low, both[:span], both[span:])


def attend_back_kernel(info, grad_resid, grad_mixed, triple, w_out, w_in, early, grad_in, grad_triple, grad_ctx):
    del early
    step = pl.program_id(0)
    rows, width = grad_resid.shape
    segs = rows // SEG
    grad_ctx[...] = dot_nt(grad_mixed[...], w_out[...]).astype(LOW)
    low = lax.broadcasted_iota(jnp.int32, (SEG, LANES), 1) < HEAD_DIM
    spot = lax.broadcasted_iota(jnp.int32, (SEG, 2 * SEG), 1) % SEG
    shrink = HEAD_DIM ** (-0.5)
    for seg in range(segs):
        live = spot < info[step * segs + seg]
        here = slice(seg * SEG, (seg + 1) * SEG)
        for pair in range(width // LANES):
            at = pair * LANES
            query = triple[here, at : at + LANES] * LOW(shrink)
            keys = halves(triple[here, width + at : width + at + LANES], low)
            values = halves(triple[here, 2 * width + at : 2 * width + at + LANES], low)
            probs = soft(query, keys, live, SEG)
            down = grad_ctx[here, at : at + LANES]
            found = pair_back(query, keys, values, probs, down, low, SEG)
            for part in range(3):
                goal = part * width + at
                grad_triple[here, goal : goal + LANES] = found[part].astype(LOW)
    grad_in[...] = (grad_resid[...] + dot_nt(grad_triple[...], w_in[...])).astype(LOW)


def unit_grad_kernel(
    plan, info, active, grad_ret, hid_low, grad_exp, context, grad_mixed, sums_one, sums_two, grad_heads, bias, bias_two, early, out, whole, mixing, small
):
    del early
    m = pl.program_id(0)
    size = plan.rows
    width = whole.shape[0]
    third = width // plan.groups
    share = third // out.shape[0]

    @pl.when(m == 0)
    def _():
        found = dot_tn(context[...], grad_mixed[...])
        for at in range(plan.groups):
            mixing[at * third : at * third + LANES, :] = found[at * LANES : (at + 1) * LANES]
            goal = plan.groups * LANES + at * HEAD_DIM
            mixing[at * third + LANES : (at + 1) * third, :] = found[goal : goal + HEAD_DIM]

    step = padded(size)
    for kind, (left, right) in enumerate(((active, grad_ret), (hid_low, grad_exp))):
        whole[...] = dot_tn(left[...], right[...])
        for at in range(out.shape[0]):
            out[at, 0, kind * step : kind * step + size, :] = whole[
                at * size : (at + 1) * size, :
            ].astype(LOW)
    leader = jnp.where(info[plan.mp_at] == 0, 1.0, 0.0)
    row = lax.broadcasted_iota(jnp.int32, (8, 1), 0)
    place = pl.multiple_of(info[plan.mp_at + m] * width, LANES)
    own = jnp.where(m == 0, 1.0, 0.0)
    biases = jnp.where(row == 6, bias[:, pl.ds(place, width)], bias_two[...] * own)
    small[0:8, :] = jnp.where(row < 6, sums_one[...], biases)
    small[8:16, :] = sums_two[...] * leader
    position = grad_heads[0:NSEG, :]
    for doc in range(1, grad_heads.shape[0] // NSEG):
        position = position + grad_heads[doc * NSEG : (doc + 1) * NSEG, :]
    small[16:, :] = position * leader
    gap = jnp.zeros((8, LANES - size), FULL)
    mine = mixing[pl.ds(pl.multiple_of(m * third, HEAD_DIM), third), :]
    for at in range(out.shape[0]):
        lines = small[:, at * size : (at + 1) * size]
        blocks = []
        for block in range(width // LANES):
            blocks += [lines[block * 8 : (block + 1) * 8], gap]
        rows = [jnp.concatenate(blocks, axis=1), mine[at * share : (at + 1) * share]]
        rest = out.shape[2] - 2 * step - share - 8
        if rest:
            rows.append(jnp.zeros((rest, width), FULL))
        out[at, 0, 2 * step :, :] = jnp.concatenate(rows, axis=0).astype(LOW)


def head_grad_kernel(plan, lists, info, tok, grad_triple, early, keep_a, send_a, keep_b, send_b, whole):
    del early
    size = plan.rows
    width = tok.shape[1]
    whole[...] = dot_tn(tok[...], grad_triple[...])
    low = lax.broadcasted_iota(jnp.int32, (size, LANES), 1) < HEAD_DIM
    for half, (keep, send) in enumerate(((keep_a, send_a), (keep_b, send_b))):
        for at, place in enumerate(lists[half]):
            for out, which in ((keep, place), (send, place ^ 1)):
                start = pl.multiple_of(info[plan.dp_at + which] * size, 8)
                for inner in range(plan.groups // 2):
                    m = half * (plan.groups // 2) + inner
                    for part in range(3):
                        goal = part * width + m * LANES
                        out[at, inner, :, part * LANES : (part + 1) * LANES] = whole[
                            pl.ds(start, size), goal : goal + LANES
                        ].astype(LOW)
                    blocks = []
                    for part in range(3):
                        goal = part * width + (plan.groups + m // 2) * LANES
                        blocks.append(whole[pl.ds(start, size), goal : goal + LANES])
                    if m % 2 == 0:
                        blocks = [blocks[0], turn(blocks[1]), blocks[2]]
                    else:
                        blocks = [turn(blocks[0]), blocks[1], turn(blocks[2])]
                    out[at, inner, :, 3 * LANES : 4 * LANES] = jnp.where(low, blocks[0], blocks[1]).astype(LOW)
                    out[at, inner, :, 4 * LANES : 5 * LANES] = jnp.where(low, blocks[2], 0.0).astype(LOW)


def spread_kernel(groups, mp_at, info, *refs):
    line, (tops, _, out, held, ready, in_sems, out_sems) = refs[:-7], refs[-7:]
    rows = held.shape[1]
    mine = info[mp_at]
    row = lax.broadcasted_iota(jnp.int32, (16, 1), 0)

    def take(at, step, part):
        place = mine + step
        slot = step % groups
        into = pltpu.make_async_copy(line[at], held.at[slot], in_sems.at[at])
        if ready is held:
            source = held.at[slot]
        else:
            source = ready.at[slot]
        goal = pl.ds(pl.multiple_of(place * rows, rows), rows)
        back = pltpu.make_async_copy(source, out.at[goal, :], out_sems.at[at])

        @pl.when(jnp.logical_and(place >= 0, place < groups))
        def _():
            if part == 0:
                into.start()
            elif part == 2:
                back.wait()
            else:
                into.wait()
                if ready is held:
                    segs = rows // SEG
                    for seg in range(segs):
                        near = held[slot, seg * SEG : seg * SEG + 16, :]
                        top = tops[pl.ds(place * segs + seg, 1), :].astype(held.dtype)
                        held[slot, seg * SEG : seg * SEG + 16, :] = jnp.where(row == 0, top, near)
                else:
                    ready[slot] = held[slot].astype(ready.dtype)
                back.start()

    for part in range(3):
        for at, step in enumerate(steps_of(groups)):
            take(at, step, part)


def steps_of(groups):
    return [0] + [-step for step in range(1, groups)] + [step for step in range(1, groups)]


def same_kernel(groups, mp_at, info, *refs):
    refs = list(refs)
    refs.insert(len(refs) - 2, refs[-3])
    spread_kernel(groups, mp_at, info, *refs)


def rows_of(block, width):
    return pl.BlockSpec((block, width), lambda i, c: (i, 0))


def load_own(section, source, target, sems):
    base, size = section
    copies = []
    for at in range(source.shape[0]):
        copy = pltpu.make_async_copy(
            source.at[at, pl.ds(base, size), :], target.at[pl.ds(at * size, size), :], sems.at[at]
        )
        copy.start()
        copies.append(copy)
    return copies


def own_out(stage, w_out, count):
    share = (w_out.shape[0] - HEAD_DIM) // count
    step = stage.shape[0] // count
    parts = [stage[at * step : (at + 1) * step, :].astype(FULL)[:share] for at in range(count)]
    parts.append(jnp.zeros((HEAD_DIM, stage.shape[1]), FULL))
    w_out[...] = jnp.concatenate(parts, axis=0).astype(LOW)


def ring_sum(plan, info, ring, total):
    for at, member in enumerate(ring):
        total[info[plan.mp_at + at]] = member[...].astype(FULL)
    found = total[0]
    for at in range(1, plan.groups):
        found = found + total[at]
    return found


def own_pairs(triple, here, live, low):
    zero = jnp.zeros((NSEG, LANES), LOW)
    block = [triple[here, at * LANES : (at + 1) * LANES] for at in range(5)]
    last = turn(block[3].astype(FULL)).astype(LOW)
    found = []
    for query, key, value in (
        (block[0], block[1], block[2]),
        (jnp.where(low, block[3], zero), jnp.where(low, last, zero), jnp.where(low, block[4], zero)),
    ):
        query = query * LOW(HEAD_DIM ** (-0.5))
        keys, values = halves(key, low), halves(value, low)
        found.append((query, keys, values, soft(query, keys, live, NSEG)))
    return found


def second_one_kernel(plan, sections, info, *refs):
    ring, refs = refs[: plan.groups], refs[plan.groups :]
    position, live, in_all, out_all, term, entry, tok, triple, context = refs[:9]
    heads, w_in, w_out, stage, sems = refs[9:]
    rows = entry.shape[0]
    copies = load_own(sections[0], in_all, w_in, sems.at[0])
    outs = load_own(sections[1], out_all, stage, sems.at[1])
    slots = ring[0].shape[0]
    for at in range(plan.groups):
        goal = pl.multiple_of(info[plan.mp_at + at] * slots, slots)
        heads[pl.ds(goal, slots), :] = ring[at][...]
    docs = rows // NSEG
    entry[...] = heads[...] + jnp.concatenate([position[...]] * docs, axis=0)
    tok[...] = entry[...].astype(LOW)
    wait_all(copies)
    triple[...] = dot_nn(tok[...], w_in[:, : 5 * LANES]).astype(LOW)
    low = lax.broadcasted_iota(jnp.int32, (NSEG, LANES), 1) < HEAD_DIM
    for doc in range(docs):
        here = slice(doc * NSEG, (doc + 1) * NSEG)
        mask = live[doc : doc + 1, :] > 0.5
        for pair, (_, _, values, probs) in enumerate(own_pairs(triple, here, mask, low)):
            probs = jnp.concatenate([part.astype(LOW) for part in probs], axis=1)
            context[here, pair * LANES : (pair + 1) * LANES] = dot_nn(probs, values).astype(LOW)
    wait_all(outs)
    own_out(stage, w_out, plan.count)
    term[...] = dot_nn(context[...], w_out[...]).astype(LOW)


def second_two_kernel(plan, sections, info, *refs):
    ring, refs = refs[: plan.groups], refs[plan.groups :]
    entry, affine, b_up, up_all, down_all, term, resid, hid_low, expanded, active = refs[:10]
    total, w_up, w_down, sems = refs[10:]
    copies = load_own(sections[2], up_all, w_up, sems.at[0])
    downs = load_own(sections[3], down_all, w_down, sems.at[1])
    value = entry[...] + ring_sum(plan, info, ring, total) + affine[4:5, :]
    resid[...] = value
    hid_low[...] = (normal(value)[0] * affine[0:1, :] + affine[1:2, :]).astype(LOW)
    wait_all(copies)
    up = dot_nn(hid_low[...], w_up[...]) + b_up[...]
    expanded[...] = up
    active[...] = (0.5 * up * (1.0 + jnp.tanh(TANH_A * (up + TANH_B * up * up * up)))).astype(LOW)
    wait_all(downs)
    term[...] = dot_nn(active[...], w_down[...]).astype(LOW)


def second_three_kernel(plan, sections, info, *refs):
    ring, refs = refs[: plan.groups], refs[plan.groups :]
    resid, expanded, top_grad, affine, up_all, down_all = refs[:6]
    term, second, back_two, grad_ret, grad_exp, sums, bias = refs[6:13]
    total, w_up, w_down, sems = refs[13:]
    copies = load_own(sections[3], down_all, w_down, sems.at[0])
    ups = load_own(sections[2], up_all, w_up, sems.at[1])
    hidden = normal(resid[...])[0] * affine[0:1, :] + affine[1:2, :]
    unit, scale = normal(hidden + ring_sum(plan, info, ring, total) + affine[5:6, :])
    second[...] = unit * affine[2:3, :] + affine[3:4, :]
    grad = top_grad[...]
    back = normal_back(grad, unit, scale, affine[2:3, :])
    back_two[...] = back
    sums[...] = jnp.zeros_like(sums)
    sums[2:3, :] = jnp.sum(grad * unit, axis=0, keepdims=True)
    sums[3:4, :] = jnp.sum(grad, axis=0, keepdims=True)
    sums[5:6, :] = jnp.sum(back, axis=0, keepdims=True)
    grad_ret[...] = back.astype(LOW)
    wait_all(copies)
    given = dot_nt(grad_ret[...], w_down[...])
    up = expanded[...]
    square = up * up
    curve = jnp.tanh(TANH_A * (up + TANH_B * up * square))
    half = 0.5 * (1.0 + curve)
    slope = half + 0.5 * up * (1.0 - curve * curve) * (TANH_A + 3.0 * TANH_A * TANH_B * square)
    wide = slope * given
    bias[...] = jnp.sum(wide, axis=0, keepdims=True)
    grad_exp[...] = wide.astype(LOW)
    wait_all(ups)
    term[...] = dot_nt(grad_exp[...], w_up[...]).astype(LOW)


def second_four_kernel(plan, sections, info, *refs):
    ring, refs = refs[: plan.groups], refs[plan.groups :]
    resid, back_two, triple, live, sums_in, affine, in_all, out_all = refs[:8]
    term, back_one, grad_mixed, grad_triple, sums = refs[8:13]
    total, w_in, w_out, stage, sems = refs[13:]
    outs = load_own(sections[1], out_all, stage, sems.at[0])
    copies = load_own(sections[0], in_all, w_in, sems.at[1])
    rows = resid.shape[0]
    grad = back_two[...] + ring_sum(plan, info, ring, total)
    unit, scale = normal(resid[...])
    back = normal_back(grad, unit, scale, affine[0:1, :])
    back_one[...] = back
    sums[...] = sums_in[...]
    sums[0:1, :] = jnp.sum(grad * unit, axis=0, keepdims=True)
    sums[1:2, :] = jnp.sum(grad, axis=0, keepdims=True)
    sums[4:5, :] = jnp.sum(back, axis=0, keepdims=True)
    grad_mixed[...] = back.astype(LOW)
    wait_all(outs)
    own_out(stage, w_out, plan.count)
    grad_ctx = dot_nt(grad_mixed[...], w_out[...]).astype(LOW)
    low = lax.broadcasted_iota(jnp.int32, (NSEG, LANES), 1) < HEAD_DIM
    for doc in range(rows // NSEG):
        here = slice(doc * NSEG, (doc + 1) * NSEG)
        mask = live[doc : doc + 1, :] > 0.5
        found = []
        for pair, (query, keys, values, probs) in enumerate(own_pairs(triple, here, mask, low)):
            down = grad_ctx[here, pair * LANES : (pair + 1) * LANES]
            found.append(pair_back(query, keys, values, probs, down, low, NSEG))
        blocks = list(found[0])
        blocks.append(jnp.where(low, found[1][0], turn(found[1][1])))
        blocks.append(jnp.where(low, found[1][2], 0.0))
        for at, block in enumerate(blocks):
            grad_triple[here, at * LANES : (at + 1) * LANES] = block.astype(LOW)
    wait_all(copies)
    term[...] = dot_nt(grad_triple[...], w_in[:, : 5 * LANES]).astype(LOW)


def second_grad_kernel(plan, info, tok, grad_triple, context, grad_mixed, hid_low, grad_exp, active, grad_ret, out):
    width = tok.shape[1]
    count, size = out.shape[0], plan.rows
    step = padded(size)
    share = width // plan.groups // count
    for kind, (left, right) in enumerate(
        ((tok, grad_triple), (hid_low, grad_exp), (active, grad_ret))
    ):
        value = dot_tn(left[...], right[...])
        if kind == 0:
            value = jnp.concatenate([value, jnp.zeros((width, LANES), FULL)], axis=1)
        for at in range(count):
            out[at, kind * step : kind * step + size, :] = value[at * size : (at + 1) * size].astype(LOW)
    value = dot_tn(context[...], grad_mixed[...])
    rest = out.shape[1] - 3 * step - share
    for at in range(count):
        rows = [value[at * share : (at + 1) * share]]
        if rest:
            rows.append(jnp.zeros((rest, width), FULL))
        out[at, 3 * step :, :] = jnp.concatenate(rows, axis=0).astype(LOW)


def collect_kernel(plan, info, *refs):
    count = plan.groups - 1
    unit_own, unit_ring, refs = refs[0], refs[1 : plan.groups], refs[plan.groups :]
    left, right, head_ring, refs = refs[0], refs[1], refs[2 : 2 + count], refs[2 + count :]
    second, unit_sum, head_sum, squares = refs
    total = unit_own[0].astype(FULL)
    for member in unit_ring:
        total = total + member[...].astype(FULL)
    unit_sum[...] = total
    heads = left[0].astype(FULL) + right[0].astype(FULL)
    for member in head_ring:
        heads = heads + member[...].astype(FULL)
    head_sum[...] = heads
    leader = jnp.where(info[plan.mp_at] == 0, 1.0, 0.0)
    step = padded(plan.rows)
    row = lax.broadcasted_iota(jnp.int32, (8, total.shape[1]), 0)
    lane = lax.broadcasted_iota(jnp.int32, (8, total.shape[1]), 1)
    once = jnp.logical_and(row >= 6, lane < LANES)

    def square(value):
        return jnp.sum(jnp.sum(value * value, axis=0, keepdims=True), axis=1, keepdims=True)

    small = total[2 * step : 2 * step + 8]
    found = square(total[: 2 * step]) + square(total[2 * step + 8 :])
    found = found + square(jnp.where(once, small, small * leader))
    found = found + square(heads) + square(second[...].astype(FULL))
    squares[...] = jnp.broadcast_to(found, squares.shape)


def update_kernel(plan, info, squares, unit_sum, head_sum, second, *refs):
    states, news, norm = refs[:7], refs[7:28], refs[28]
    total = squares[...]
    norm[...] = jnp.sqrt(total)
    factor = jnp.minimum(1.0, clip_level / jnp.sqrt(total[0:1, 0:1]))
    size, step = plan.rows, padded(plan.rows)
    share = states[1].shape[2]

    def put(kind, where, grad):
        state = states[kind]
        old = [state[(at, *where)] for at in range(3)]
        for at, value in enumerate(adam(old, grad, factor)):
            news[7 * at + kind][where] = value

    def columns(block):
        at = [block[:, i * HEAD_DIM : (i + 1) * HEAD_DIM] for i in range(9)]
        return jnp.concatenate([at[i] for i in (0, 2, 4, 1, 3, 5, 6, 7, 8)], axis=1)

    every = slice(None)
    put(0, (0, every, every), columns(head_sum[...]))
    put(0, (1, every, every), columns(second[:size, :].astype(FULL)))
    put(1, (0, every, every), unit_sum[2 * step + 8 : 2 * step + 8 + share, :])
    put(1, (1, every, every), second[3 * step : 3 * step + share, :].astype(FULL))
    put(2, (0, every, every), unit_sum[step : step + size, :])
    put(2, (1, every, every), second[step : step + size, :].astype(FULL))
    put(4, (0, every, every), unit_sum[:size, :])
    put(4, (1, every, every), second[2 * step : 2 * step + size, :].astype(FULL))
    small = unit_sum[2 * step : 2 * step + 8, :]
    put(3, (every, every), small[6:8, :size])
    put(5, (0, every, every), small[0:6, :size])
    put(5, (1, every, every), small[0:6, LANES : LANES + size])
    for block in range(NSEG // 8):
        goal = (block + 2) * LANES
        put(6, (slice(block * 8, (block + 1) * 8), every), small[:, goal : goal + size])


def own_rows(plan, rows, block, width):
    return pl.BlockSpec((block, width), lambda i, c: (c[plan.mp_at] * (rows // block) + i, 0))


WHOLE = pl.BlockSpec(memory_space=pltpu.VMEM)
OUTSIDE = pl.BlockSpec(memory_space=pl.ANY)


def shape(*dims, kind=LOW):
    return jax.ShapeDtypeStruct(dims, kind)


def run(kernel, steps, ins, outs, scratch, micros, info, args):
    return pl.pallas_call(
        kernel,
        grid_spec=pltpu.PrefetchScalarGridSpec(
            num_scalar_prefetch=1,
            grid=(steps,),
            in_specs=ins,
            out_specs=[spec for spec, _ in outs],
            scratch_shapes=scratch,
        ),
        out_shape=[kind for _, kind in outs],
        compiler_params=pltpu.CompilerParams(vmem_limit_bytes=VMEM_BYTES),
        cost_estimate=pl.CostEstimate(
            flops=int(micros * FLOPS), bytes_accessed=1024, transcendentals=0
        ),
    )(info, *args)


def layer_of(state, layer):
    return pl.BlockSpec((1, 1, *state.shape[2:]), lambda i, c: (0, layer, 0, 0))


def heads_block_of(info, attend_in, bias, affine, position):
    return run(
        heads_block_kernel,
        1,
        [layer_of(attend_in, 0), WHOLE, WHOLE, WHOLE],
        [(WHOLE, shape(attend_in.shape[2], 5 * LANES))],
        [pltpu.VMEM((LANES, LANES), FULL)],
        2,
        info,
        (attend_in, bias, affine, position),
    )[0]


def units_block_of(info, layer, states):
    rows = sum(padded(state.shape[2]) for state in states)
    return run(
        units_block_kernel,
        1,
        [layer_of(state, layer) for state in states],
        [(WHOLE, shape(rows, states[-1].shape[3]))],
        [],
        2,
        info,
        states,
    )[0]


def attend_forward(plan, info, tok, pieces, block=512):
    rows, width = tok.shape[0] // plan.groups, tok.shape[1]
    lanes = pieces[0].shape[-1]
    wide = rows_of(block, 3 * width)
    return run(
        functools.partial(attend_kernel, plan),
        rows // block,
        [own_rows(plan, rows, block, width)] + [OUTSIDE] * len(pieces),
        [
            (wide, shape(rows, 3 * width)),
            (rows_of(block, width), shape(rows, width)),
            (WHOLE, shape(width, 3 * width)),
            (WHOLE, shape(8, width, kind=FULL)),
            (WHOLE, shape(8, width, kind=FULL)),
            (WHOLE, shape(NSEG, width, kind=FULL)),
            (WHOLE, shape(1, plan.groups * width, kind=FULL)),
        ],
        [
            pltpu.VMEM((plan.groups, width, lanes), LOW),
            pltpu.SemaphoreType.DMA((plan.copies(),)),
        ],
        18,
        info,
        (tok, *pieces),
    )


def feed_forward(plan, sections, info, tok, context, affine, b_up, weights, block=256):
    rows, width = context.shape
    units = b_up.shape[1]
    line = rows_of(block, width)
    pieces = plan.groups * weights[0].shape[1]
    return run(
        functools.partial(feed_kernel, plan, sections),
        rows // block,
        [own_rows(plan, rows, block, width), line, WHOLE, WHOLE] + [OUTSIDE] * 3,
        [
            (line, shape(rows, width, kind=FULL)),
            (line, shape(rows, width)),
            (rows_of(block, units), shape(rows, units)),
            (line, shape(rows, width, kind=FULL)),
            (line, shape(rows, width)),
            (WHOLE, shape(rows // SEG, width, kind=FULL)),
            (WHOLE, shape(width, width)),
        ],
        [
            pltpu.VMEM((width, units), LOW),
            pltpu.VMEM((units, width), LOW),
            pltpu.VMEM((plan.groups, weights[2].shape[1] * sections[2][1], width), LOW),
            pltpu.SemaphoreType.DMA((2, pieces)),
            pltpu.SemaphoreType.DMA((pieces,)),
        ],
        24,
        info,
        (tok, context, affine, b_up, *weights),
    )


def feed_backward(plan, sections, info, cot, back_heads, ring, resid_two, expanded, resid, affine, weights, block=256):
    rows, width = resid.shape
    units = expanded.shape[1]
    line, wide = rows_of(block, width), rows_of(block, units)
    return run(
        functools.partial(feed_back_kernel, plan, sections),
        rows // block,
        [own_rows(plan, rows, block, width), WHOLE, line, wide, line, WHOLE]
        + [WHOLE] * plan.groups
        + [OUTSIDE] * 2,
        [
            (line, shape(rows, width, kind=FULL)),
            (wide, shape(rows, units)),
            (wide, shape(rows, units)),
            (line, shape(rows, width)),
            (line, shape(rows, width)),
            (WHOLE, shape(8, width, kind=FULL)),
            (WHOLE, shape(1, units, kind=FULL)),
            (WHOLE, shape(*back_heads.shape, kind=FULL)),
        ],
        [
            pltpu.VMEM((width, units), LOW),
            pltpu.VMEM((units, width), LOW),
            pltpu.SemaphoreType.DMA((2, plan.groups * weights[0].shape[1])),
        ],
        28,
        info,
        (cot, back_heads, resid_two, expanded, resid, affine, *ring, *weights[:2]),
    )


def attend_backward(info, grad_resid, grad_mixed, triple, w_out, w_in, early, block=256):
    rows, width = grad_resid.shape
    line, wide = rows_of(block, width), rows_of(block, 3 * width)
    return run(
        attend_back_kernel,
        rows // block,
        [line, line, wide, WHOLE, WHOLE, OUTSIDE],
        [(line, shape(rows, width)), (wide, shape(rows, 3 * width))],
        [pltpu.VMEM((block, width), LOW)],
        36,
        info,
        (grad_resid, grad_mixed, triple, w_out, w_in, early),
    )


def second_run(kernel, plan, sections, info, ring, args, weights, outs, scratch):
    count = weights[0].shape[0]
    return run(
        functools.partial(kernel, plan, sections),
        1,
        [WHOLE] * (len(ring) + len(args)) + [OUTSIDE] * len(weights),
        [(WHOLE, kind) for kind in outs],
        scratch + [pltpu.SemaphoreType.DMA((2, count))],
        5,
        info,
        (*ring, *args, *weights),
    )


def second_layer(sections, plan, info, ring, position, live, top_grad, affine, b_up, weights):
    rows, width = top_grad.shape
    groups = plan.groups
    in_all, out_all, up_all, down_all = weights
    own = width // groups
    tall = out_all.shape[0] * sections[1][1]
    full, low = shape(rows, width, kind=FULL), shape(rows, width)
    mixed = shape(rows, 5 * LANES)
    total = pltpu.VMEM((groups, rows, width), FULL)
    square = pltpu.VMEM((width, width), LOW)
    outer = [pltpu.VMEM((own + HEAD_DIM, width), LOW), pltpu.VMEM((tall, width), LOW)]

    term, entry, tok, triple, context = second_run(
        second_one_kernel, plan, sections, info, ring, (position, live), (in_all, out_all),
        [low, full, low, mixed, shape(rows, own + HEAD_DIM)],
        [pltpu.VMEM((rows, width), FULL), square] + outer,
    )
    term, resid, hid_low, expanded, active = second_run(
        second_two_kernel, plan, sections, info, around(term), (entry, affine, b_up), (up_all, down_all),
        [low, full, low, full, low],
        [total, square, square],
    )
    term, second, back_two, grad_ret, grad_exp, sums, bias = second_run(
        second_three_kernel, plan, sections, info, around(term), (resid, expanded, top_grad, affine), (up_all, down_all),
        [low, full, full, low, low, shape(8, width, kind=FULL), shape(1, width, kind=FULL)],
        [total, square, square],
    )
    term, back_one, grad_mixed, grad_triple, sums = second_run(
        second_four_kernel, plan, sections, info, around(term),
        (resid, back_two, triple, live, sums, affine), (in_all, out_all),
        [low, full, low, mixed, shape(8, width, kind=FULL)],
        [total, square] + outer,
    )
    saved = (tok, grad_triple, context, grad_mixed, hid_low, grad_exp, active, grad_ret)
    return second, back_one, around(term), sums, bias, saved


def second_grads_of(plan, count, info, saved):
    width = saved[0].shape[1]
    size = 3 * padded(plan.rows) + padded(width // plan.groups // count)
    return run(
        functools.partial(second_grad_kernel, plan),
        1,
        [WHOLE] * len(saved),
        [(WHOLE, shape(count, size, width))],
        [],
        5,
        info,
        saved,
    )[0]


def spread_out(groups, mp_at, info, line, tops, early, kind):
    count = len(line)
    rows, width = line[0].shape
    held = [pltpu.VMEM((groups, rows, width), line[0].dtype)]
    if tops is None:
        tops = jnp.zeros((8, width), FULL)
        held.append(pltpu.VMEM((groups, rows, width), kind))
        kernel = spread_kernel
    else:
        kernel = same_kernel
    return run(
        functools.partial(kernel, groups, mp_at),
        1,
        [OUTSIDE] * count + [WHOLE, OUTSIDE],
        [(OUTSIDE, shape(groups * rows, width, kind=kind))],
        held + [pltpu.SemaphoreType.DMA((count,)), pltpu.SemaphoreType.DMA((count,))],
        7,
        info,
        (*line, tops, early),
    )[0]


def unit_grads(plan, info, active, grad_ret, hid_low, grad_exp, context, grad_mixed, small, early):
    rows, width = grad_ret.shape
    fixed = pl.BlockSpec((rows, width), lambda m, c: (0, 0))
    moving = pl.BlockSpec((rows, width), lambda m, c: (0, c[plan.mp_at + m]))
    size = 2 * padded(plan.rows) + padded(width // plan.groups // plan.count + 8)
    out = pl.BlockSpec((plan.count, 1, size, width), lambda m, c: (0, m, 0, 0))
    square = pltpu.VMEM((width, width), FULL)
    return run(
        functools.partial(unit_grad_kernel, plan),
        plan.groups,
        [moving, fixed, fixed, moving, fixed, fixed] + [WHOLE] * len(small) + [OUTSIDE],
        [(out, shape(plan.count, plan.groups, size, width))],
        [square, square, pltpu.VMEM((width // LANES * 8, width), FULL)],
        19,
        info,
        (active, grad_ret, hid_low, grad_exp, context, grad_mixed, *small, early),
    )[0]


def collect(plan, info, unit_own, unit_ring, head_own, head_ring, second):
    return run(
        functools.partial(collect_kernel, plan),
        1,
        [WHOLE] * (4 + len(unit_ring) + len(head_ring)),
        [
            (WHOLE, shape(*unit_ring[0].shape, kind=FULL)),
            (WHOLE, shape(*head_ring[0].shape, kind=FULL)),
            (WHOLE, shape(8, LANES, kind=FULL)),
        ],
        [],
        4,
        info,
        (unit_own, *unit_ring, *head_own, *head_ring, second),
    )


def update(plan, info, squares, unit_sum, head_sum, second, states):
    outs = [(WHOLE, shape(*state.shape[1:], kind=FULL)) for _ in range(3) for state in states]
    return run(
        functools.partial(update_kernel, plan),
        1,
        [WHOLE] * (4 + len(states)),
        outs + [(WHOLE, shape(8, LANES, kind=FULL))],
        [],
        7,
        info,
        (squares, unit_sum, head_sum, second, *states),
    )


def head_grads(plan, lists, info, tok, grad_triple, early):
    rows, width = grad_triple.shape[0], tok.shape[1]
    out = shape(len(lists[0]), plan.groups // 2, plan.rows, 5 * LANES)
    return run(
        functools.partial(head_grad_kernel, plan, lists),
        1,
        [own_rows(plan, rows, rows, width), WHOLE, OUTSIDE],
        [(WHOLE, out)] * 4,
        [pltpu.VMEM((width, 3 * width), FULL)],
        10,
        info,
        (tok, grad_triple, early),
    )


def swap(value, bit, axis="dp"):
    return lax.ppermute(value, axis, [(i, i ^ bit) for i in range(lax.axis_size(axis))])


def ahead(value, step):
    size = lax.axis_size("mp")
    return lax.ppermute(value, "mp", [(i, (i + step) % size) for i in range(size)])


def onward(value, step):
    size = lax.axis_size("mp")
    return lax.ppermute(
        value, "mp", [(i, i + step) for i in range(size) if 0 <= i + step < size]
    )


def all_sum(value, axes):
    for axis in axes:
        bit = 1
        while bit < lax.axis_size(axis):
            value = value + swap(value, bit, axis)
            bit *= 2
    return value


def around(value):
    return [value] + [ahead(value, step) for step in range(1, lax.axis_size("mp"))]


def bits_of(count):
    bits, bit = [], 2
    while bit < count:
        bits.append(bit)
        bit *= 2
    return bits


def tie(value, *first):
    return lax.optimization_barrier((value, first))[0]


def gather(ring, gates):
    half = len(ring) // 2
    bits = bits_of(lax.axis_size("dp"))
    held = [[([0], jnp.stack(ring[:half])[None])], [([0], jnp.stack(ring[half:])[None])]]
    arrived = []
    for stage in range(len(bits)):
        arrived.append([])
        for which, order in enumerate((bits, bits[::-1])):
            bit = order[stage]
            places = sum((member[0] for member in held[which]), [])
            block = [member[1] for member in held[which]]
            block = block[0] if len(block) == 1 else jnp.concatenate(block)
            if stage < len(gates):
                block = tie(block, *gates[stage])
            got = swap(block, bit)
            arrived[-1].append(got)
            held[which] = [(places, block), ([j ^ bit for j in places], got)]
    pieces = []
    for which in range(2):
        for places, block in held[which]:
            pieces.append((places, which, block))
            pieces.append(([j ^ 1 for j in places], which, swap(block, 1)))
    return pieces, arrived


def pick(stack, order, count):
    return jnp.concatenate(
        [lax.dynamic_slice_in_dim(stack, order[at], 1) for at in range(count)]
    )


def straighten(pieces, device):
    merged = []
    for which in range(2):
        mine = [member for member in pieces if member[1] == which]
        places = sum((member[0] for member in mine), [])
        block = jnp.concatenate([member[2] for member in mine])
        order = sorted(range(len(places)), key=lambda at: places[at])
        block = pick(jnp.stack([block[at] for at in order]), device ^ jnp.arange(len(places)), len(places))
        count, groups, rows, lanes = block.shape
        block = block.transpose(1, 0, 2, 3).reshape(1, groups, count * rows, lanes)
        merged.append(([0], which, block))
    return merged


def places_of(order):
    places = [0]
    for bit in reversed(order):
        places = places + [place | bit for place in places]
    return places


def add(left, right):
    return (left.astype(FULL) + right.astype(FULL)).astype(LOW)


def reduce_dp(keep, send, order, early):
    got = tie(swap(send, 1), *early)
    for bit in order:
        half = keep.shape[0] // 2
        out = swap(add(keep[half:], got[half:]), bit)
        keep, got = add(keep[:half], got[:half]), out
    return keep[0], got[0]


def adam(state, grad, factor):
    clipped = grad * factor
    first = beta_one * state[1] + (1.0 - beta_one) * clipped
    second = beta_two * state[2] + (1.0 - beta_two) * clipped * clipped
    fixed_first = first / (1.0 - beta_one**adam_step)
    fixed_second = second / (1.0 - beta_two**adam_step)
    master = state[0] - rate * (
        fixed_first / (jnp.sqrt(fixed_second) + adam_eps) + decay * state[0]
    )
    return (master, first, second)


def shards(
    tokens,
    cotangent,
    counts,
    attend_in,
    attend_out,
    expand_in,
    expand_bias,
    expand_out,
    affine_state,
    position_state,
):
    shards_dp, groups = lax.axis_size("dp"), lax.axis_size("mp")
    device, mine = lax.axis_index("dp"), lax.axis_index("mp")
    width = tokens.shape[1]
    slots = counts.size // groups
    piece = width // shards_dp
    share = attend_out.shape[2]
    before = (mine - jnp.arange(groups)) % groups
    info = jnp.concatenate(
        [
            lax.dynamic_slice_in_dim(counts.reshape(-1), mine * slots, slots),
            before,
            device ^ jnp.arange(shards_dp),
        ]
    ).astype(jnp.int32)
    bits = bits_of(shards_dp)
    lists = (places_of(bits), places_of(bits[::-1]))
    mp_at, dp_at = slots, slots + groups

    heads_block = heads_block_of(info, attend_in, expand_bias, affine_state, position_state)
    units_block = units_block_of(info, 0, (expand_in, expand_out, attend_out))
    second_block = units_block_of(info, 1, (attend_in, expand_in, expand_out, attend_out))
    units_all = lax.all_gather(units_block, ("mp", "dp"), axis=0)
    units_all = units_all.reshape(groups, shards_dp, -1, width)
    heads_pieces, _ = gather(around(heads_block), [])
    second_all = lax.all_gather(second_block, "dp", axis=0)

    step, low_share = padded(piece), padded(share)
    units_sections = [(0, piece), (step, piece), (2 * step, low_share)]
    units = [units_all] * 3
    sections = [(0, piece), (3 * step, low_share), (step, piece), (2 * step, piece)]
    weights = [second_all] * 4
    load_info = info
    if piece % 16:
        heads_pieces = straighten(heads_pieces, device)
        load_info = info.at[dp_at].set(0)
        units = [
            units_all[:, :, base : base + rows].reshape(groups, 1, shards_dp * rows, width)
            for base, rows in units_sections
        ]
        weights = [
            second_all[:, base : base + rows].reshape(1, shards_dp * rows, width)
            for base, rows in sections
        ]
        units_sections = [(0, shards_dp * rows) for _, rows in units_sections]
        sections = [(0, shards_dp * rows) for _, rows in sections]

    def plan_of(pieces, rows):
        places = [(member[0], member[1]) for member in pieces]
        return Plan(groups, places, rows, mp_at, dp_at, shards_dp)

    heads_plan = plan_of(heads_pieces, heads_pieces[0][2].shape[2])
    own_plan = plan_of([], piece)
    heads_pieces = [member[2] for member in heads_pieces]

    triple, context, w_in, affine_one, affine_two, position, b_up = attend_forward(
        heads_plan, load_info, tokens, heads_pieces
    )
    resid, hid_low, expanded, resid_two, first, tops, w_out = feed_forward(
        own_plan, units_sections, info, tokens, context, affine_one, b_up, units
    )

    keep_heads = (counts > 0).astype(FULL)
    live = jnp.concatenate([keep_heads, keep_heads], axis=1)
    keep_heads = keep_heads.reshape(-1, 1)
    top_grad = cotangent.reshape(-1, SEG, width)[:, 0].astype(FULL) * keep_heads
    tops_ring = around(tops)
    second, back_heads, heads_ring, sums_two, bias_two, saved = second_layer(
        sections, own_plan, info, tops_ring, position, live, top_grad, affine_two, affine_one[7:8], weights
    )
    first_later = tie(first, *heads_ring[1:])
    out_line = [(onward(first_later, 1), onward(first_later, -1))]
    grad_resid, active, grad_exp, grad_ret, grad_mixed, sums_one, bias, grad_heads = feed_backward(
        own_plan, units_sections, info, cotangent, back_heads, heads_ring, resid_two, expanded, resid, affine_one, units
    )
    second_grads = second_grads_of(own_plan, shards_dp, tie(info, sums_one), saved)
    second_share = lax.psum_scatter(second_grads, "dp", scatter_dimension=0)
    out_line.append((onward(out_line[0][0], 1), onward(out_line[0][1], -1)))
    grad_in, grad_triple = attend_backward(
        tie(info, *out_line[0]), grad_resid, grad_mixed, triple, w_out, w_in, active
    )
    out_line.append((onward(out_line[1][0], 1), onward(out_line[1][1], -1)))
    small = (sums_one, sums_two, grad_heads, bias, bias_two)
    unit_out = unit_grads(
        own_plan,
        tie(info, *out_line[1]),
        active,
        grad_ret,
        hid_low,
        grad_exp,
        context,
        grad_mixed,
        small,
        grad_in,
    )
    unit_terms = lax.psum_scatter(unit_out, "dp", scatter_dimension=0)
    keep_a, send_a, keep_b, send_b = head_grads(own_plan, lists, info, tokens, grad_triple, unit_out)

    def in_line(own, line):
        return [own] + [pair[0] for pair in line] + [pair[1] for pair in line]

    grad_later = tie(grad_in, keep_a, *out_line[2])
    grad_line = [(onward(grad_later, 1), onward(grad_later, -1))]
    left_a, right_a = reduce_dp(keep_a, send_a, bits, out_line[2])
    left_b, right_b = reduce_dp(keep_b, send_b, bits[::-1], out_line[2])
    terms = [(left_a[s], right_a[s]) for s in range(1, groups // 2)]
    terms += [(left_b[s], right_b[s]) for s in range(groups - groups // 2)]
    head_ring = [
        ahead(tie(add(*term), *grad_line[0]), -at - 1) for at, term in enumerate(terms)
    ]
    merged = spread_out(
        groups,
        mp_at,
        info,
        in_line(first, out_line),
        second * keep_heads,
        grad_line[0][0],
        LOW,
    )
    grad_line.append((onward(grad_line[0][0], 1), onward(grad_line[0][1], -1)))
    unit_ring = [
        ahead(tie(unit_terms[at], *grad_line[1]), -at) for at in range(1, groups)
    ]
    unit_sum, head_sum, squares = collect(
        own_plan, info, unit_terms, unit_ring, (left_a, right_a), head_ring, second_share
    )
    last = tie(grad_line[1], *unit_ring)
    grad_line.append((onward(last[0], 1), onward(last[1], -1)))
    squares = all_sum(squares, ("dp", "mp"))
    input_grad = spread_out(
        groups, mp_at, info, in_line(grad_in, grad_line), None, grad_triple, FULL
    )
    states = (
        attend_in,
        attend_out,
        expand_in,
        expand_bias,
        expand_out,
        affine_state,
        position_state,
    )
    *updated, norm = update(own_plan, info, squares, unit_sum, head_sum, second_share, states)
    return (merged, input_grad, norm[0, 0], *updated)


def solution(mesh):
    in_specs = (
        P("dp", None),
        P("dp", None),
        P("dp", None),
        P(None, None, "dp", "mp"),
        P(None, None, ("mp", "dp"), None),
        P(None, None, "dp", "mp"),
        P(None, None, ("mp", "dp")),
        P(None, None, ("mp", "dp"), None),
        P(None, None, None, "dp"),
        P(None, None, "dp"),
    )
    out_specs = (
        P("dp", None),
        P("dp", None),
        P(),
        P(None, "dp", "mp"),
        P(None, ("mp", "dp"), None),
        P(None, "dp", "mp"),
        P(None, ("mp", "dp")),
        P(None, ("mp", "dp"), None),
        P(None, None, "dp"),
        P(None, "dp"),
        P(None, "dp", "mp"),
        P(None, ("mp", "dp"), None),
        P(None, "dp", "mp"),
        P(None, ("mp", "dp")),
        P(None, ("mp", "dp"), None),
        P(None, None, "dp"),
        P(None, "dp"),
        P(None, "dp", "mp"),
        P(None, ("mp", "dp"), None),
        P(None, "dp", "mp"),
        P(None, ("mp", "dp")),
        P(None, ("mp", "dp"), None),
        P(None, None, "dp"),
        P(None, "dp"),
    )
    return jax.shard_map(shards, mesh=mesh, in_specs=in_specs, out_specs=out_specs, check_vma=False)
```

```python
import functools

import jax
import jax.numpy as jnp
from jax import lax
from jax.experimental import pallas as pl
from jax.experimental.pallas import tpu as pltpu
from jax.sharding import PartitionSpec as P

LOW = jnp.bfloat16
FULL = jnp.float32
HEAD_DIM = 64
SEG = 128
NSEG = 32
norm_eps = 1e-05
clip_level = 1.0
rate = 0.02
decay = 0.01
beta_one = 0.9
beta_two = 0.999
adam_eps = 1e-08
adam_step = 10
LANES = 2 * HEAD_DIM
TANH_A = 0.7978845608028654
TANH_B = 0.044715
VMEM_BYTES = 60 * 1024 * 1024
FLOPS = 1.15e9


def dot_nn(a, b):
    return lax.dot_general(a, b, (((1,), (0,)), ((), ())), preferred_element_type=FULL)


def dot_nt(a, b):
    return lax.dot_general(a, b, (((1,), (1,)), ((), ())), preferred_element_type=FULL)


def dot_tn(a, b):
    return lax.dot_general(a, b, (((0,), (0,)), ((), ())), preferred_element_type=FULL)


def normal(values):
    mean = jnp.mean(values, axis=-1, keepdims=True)
    centred = values - mean
    spread = jnp.mean(centred * centred, axis=-1, keepdims=True)
    scale = lax.rsqrt(spread + norm_eps)
    return centred * scale, scale


def normal_back(grad, unit, scale, gain):
    scaled = grad * gain
    one = jnp.mean(scaled, axis=-1, keepdims=True)
    two = jnp.mean(scaled * unit, axis=-1, keepdims=True)
    return scale * (scaled - one - unit * two)


def halves(block, low):
    zero = jnp.zeros_like(block)
    return jnp.concatenate([jnp.where(low, block, zero), jnp.where(low, zero, block)], axis=0)


def soft(query, keys, live, span):
    scores = jnp.where(live, dot_nt(query, keys), -1e30)
    parts = []
    for half in range(2):
        piece = scores[:, half * span : (half + 1) * span]
        weights = jnp.exp(piece - jnp.max(piece, axis=-1, keepdims=True))
        parts.append(weights * (1.0 / jnp.sum(weights, axis=-1, keepdims=True)))
    return parts


class Plan:
    def __init__(self, groups, pieces, rows, mp_at, dp_at, count=1):
        self.groups, self.pieces, self.rows = groups, pieces, rows
        self.mp_at, self.dp_at = mp_at, dp_at
        self.count = count

    def copies(self):
        return sum(len(places) for places, _ in self.pieces) * (self.groups // 2)


def fetch(plan, info, pieces, land, sems, begin=True):
    size = plan.rows
    copies = []
    for (places, half), piece in zip(plan.pieces, pieces):
        for at, place in enumerate(places):
            start = pl.multiple_of(info[plan.dp_at + place] * size, 16)
            for inner in range(piece.shape[1]):
                copy = pltpu.make_async_copy(
                    piece.at[at, inner],
                    land(half * piece.shape[1] + inner, start, size),
                    sems.at[len(copies)],
                )
                if begin:
                    copy.start()
                copies.append(copy)
    return copies


def padded(count):
    return -(-count // 16) * 16


def wait_all(copies):
    for copy in copies:
        copy.wait()


def turn(block):
    return jnp.concatenate([block[:, HEAD_DIM:], block[:, :HEAD_DIM]], axis=1)


def fetch_units(plan, section, info, pieces, down_all, w_up, w_down, sems, begin=True):
    width = w_down.shape[1]
    base, size = section

    def up(m, start, rows):
        place = pl.multiple_of(info[plan.mp_at + m] * width, LANES)
        return w_up.at[pl.ds(start, rows), pl.ds(place, width)]

    ups = fetch(plan, info, pieces, up, sems.at[0], begin)
    copies = []
    for m in range(down_all.shape[0]):
        for at in range(down_all.shape[1]):
            copy = pltpu.make_async_copy(
                down_all.at[m, at, pl.ds(base, size), :],
                w_down.at[pl.ds(m * width + at * size, size), :],
                sems.at[1, m * down_all.shape[1] + at],
            )
            if begin:
                copy.start()
            copies.append(copy)
    return ups, copies


def fetch_out(section, plan, info, out_all, stage, sems):
    base, size = section
    copies = []
    for m in range(plan.groups):
        for at in range(out_all.shape[1]):
            copy = pltpu.make_async_copy(
                out_all.at[info[plan.mp_at + m], at, pl.ds(base, size), :],
                stage.at[m, pl.ds(at * size, size), :],
                sems.at[len(copies)],
            )
            copy.start()
            copies.append(copy)
    return copies


def pair_columns(stage, w_in):
    groups, width = stage.shape[:2]
    low = lax.broadcasted_iota(jnp.int32, (width, LANES), 1) < HEAD_DIM
    for part in range(3):
        base = part * width
        for m in range(groups):
            at = base + m * LANES
            w_in[:, at : at + LANES] = stage[m, :, part * LANES : (part + 1) * LANES]
        for m in range(0, groups, 2):
            at = base + (groups + m // 2) * LANES
            source = slice(3 * LANES, 4 * LANES) if part < 2 else slice(4 * LANES, 5 * LANES)
            left, right = stage[m, :, source], stage[m + 1, :, source]
            if part == 1:
                left = turn(left)
            else:
                right = turn(right)
            w_in[:, at : at + LANES] = jnp.where(low, left, right)


def pair_rows(stage, w_out, count):
    groups, rows = stage.shape[:2]
    share = w_out.shape[0] // groups // count
    step = rows // count
    for m in range(groups):
        parts = [stage[m, at * step : (at + 1) * step, :].astype(FULL)[:share] for at in range(count)]
        found = jnp.concatenate(parts, axis=0).astype(LOW)
        w_out[m * LANES : (m + 1) * LANES, :] = found[:LANES]
        goal = groups * LANES + m * HEAD_DIM
        w_out[goal : goal + HEAD_DIM, :] = found[LANES:]


def columns_of(block):
    at = [block[:, i * HEAD_DIM : (i + 1) * HEAD_DIM] for i in range(9)]
    order = ((0, 3), (1, 4), (2, 5), (6, 7))
    return [jnp.concatenate([at[i], at[j]], axis=1) for i, j in order] + [at[8]]


def heads_block_kernel(info, attend_in, bias, affine, position, out, small):
    rows = attend_in.shape[2]
    small[...] = jnp.zeros_like(small)
    small[0:6, :rows] = affine[0, 0]
    small[6:8, :rows] = bias[0]
    small[8:14, :rows] = affine[0, 1]
    small[16 : 16 + NSEG, :rows] = position[0]
    blocks = columns_of(attend_in[0, 0])
    blocks[4] = jnp.concatenate([blocks[4], small[...].T[:rows, :HEAD_DIM]], axis=1)
    for at, block in enumerate(blocks):
        out[:, at * LANES : (at + 1) * LANES] = block.astype(LOW)


def units_block_kernel(info, *refs):
    ins, out = refs[:-1], refs[-1]
    start = 0
    for source in ins:
        block = source[0, 0]
        rows = block.shape[0]
        if block.shape[1] != out.shape[1]:
            blocks = columns_of(block)
            blocks[4] = jnp.concatenate([blocks[4], jnp.zeros((rows, HEAD_DIM), FULL)], axis=1)
            blocks.append(jnp.zeros((rows, LANES), FULL))
            block = jnp.concatenate(blocks, axis=1)
        if padded(rows) > rows:
            block = jnp.concatenate([block, jnp.zeros((padded(rows) - rows, out.shape[1]), FULL)], axis=0)
        out[start : start + padded(rows), :] = block.astype(LOW)
        start += padded(rows)


def attend_kernel(plan, info, tok, *refs):
    pieces, refs = refs[:-10], refs[-10:]
    triple, context, chances, w_in, affine_one, affine_two, position, b_up, stage, sems = refs
    step = pl.program_id(0)
    rows, width = tok.shape

    @pl.when(step == 0)
    def _():
        def land(m, start, size):
            return stage.at[m, pl.ds(start, size), :]

        wait_all(fetch(plan, info, pieces, land, sems))
        for m in range(plan.groups):
            small = stage[m, :, 4 * LANES : 5 * LANES].astype(FULL).T
            place = pl.multiple_of(info[plan.mp_at + m] * width, LANES)
            b_up[:, pl.ds(place, width)] = small[HEAD_DIM + 6 : HEAD_DIM + 7]
            if m == 0:
                affine_one[...] = small[HEAD_DIM : HEAD_DIM + 8]
                affine_two[...] = small[HEAD_DIM + 8 : HEAD_DIM + 16]
                position[...] = small[HEAD_DIM + 16 : HEAD_DIM + 16 + NSEG]
        pair_columns(stage, w_in)

    triple[...] = dot_nn(tok[...], w_in[...]).astype(LOW)
    low = lax.broadcasted_iota(jnp.int32, (SEG, LANES), 1) < HEAD_DIM
    spot = lax.broadcasted_iota(jnp.int32, (SEG, 2 * SEG), 1) % SEG
    for seg in range(rows // SEG):
        live = spot < info[step * (rows // SEG) + seg]
        here = slice(seg * SEG, (seg + 1) * SEG)
        for pair in range(width // LANES):
            at = pair * LANES
            query = triple[here, at : at + LANES] * LOW(HEAD_DIM ** (-0.5))
            keys = halves(triple[here, width + at : width + at + LANES], low)
            values = halves(triple[here, 2 * width + at : 2 * width + at + LANES], low)
            probs = jnp.concatenate([part.astype(LOW) for part in soft(query, keys, live, SEG)], axis=1)
            chances[here, 2 * at : 2 * at + 2 * SEG] = probs
            context[here, at : at + LANES] = dot_nn(probs, values).astype(LOW)


def feed_kernel(plan, sections, info, tok, context, affine, b_up, down_all, out_all, *refs):
    pieces, refs = refs[: len(plan.pieces)], refs[len(plan.pieces) :]
    resid, hid_low, expanded, resid_two, first, tops, w_out, w_up, w_down, stage, sems, out_sems = refs
    step = pl.program_id(0)
    rows, width = tok.shape
    segs = rows // SEG

    @pl.when(step == 0)
    def _():
        outs = fetch_out(sections[1], plan, info, out_all, stage, out_sems)
        fetch_units(plan, sections[0], info, pieces, down_all, w_up, w_down, sems)
        wait_all(outs)
        pair_rows(stage, w_out, plan.count)

    mixed = dot_nn(context[...], w_out[...])
    value = tok[...].astype(FULL) + mixed + affine[4:5, :]
    resid[...] = value
    hidden = normal(value)[0] * affine[0:1, :] + affine[1:2, :]
    low = hidden.astype(LOW)
    hid_low[...] = low
    total = hidden + affine[5:6, :]
    units = w_up.shape[1]
    block = width

    @pl.when(step == 0)
    def _():
        ups, downs = fetch_units(plan, sections[0], info, pieces, down_all, w_up, w_down, sems, False)
        wait_all(ups)
        wait_all(downs)

    for at in range(0, units, block):
        up = dot_nn(low, w_up[:, at : at + block]) + b_up[:, at : at + block]
        expanded[:, at : at + block] = up.astype(LOW)
        curve = jnp.tanh(TANH_A * (up + TANH_B * up * up * up))
        active = (0.5 * up * (1.0 + curve)).astype(LOW)
        total = total + dot_nn(active, w_down[at : at + block, :])
    resid_two[...] = total
    result = normal(total)[0] * affine[2:3, :] + affine[3:4, :]
    row = lax.broadcasted_iota(jnp.int32, (SEG, 1), 0)
    for seg in range(segs):
        piece = result[seg * SEG : (seg + 1) * SEG, :]
        kept = jnp.where(row < info[step * segs + seg], piece, 0.0)
        first[seg * SEG : (seg + 1) * SEG, :] = kept.astype(LOW)
        tops[pl.ds(step * segs + seg, 1), :] = piece[0:1, :]


def feed_back_kernel(plan, sections, info, cot, back_heads, resid_two, expanded, resid, affine, *refs):
    ring, refs = refs[: plan.groups], refs[plan.groups :]
    pieces, refs = refs[: len(plan.pieces)], refs[len(plan.pieces) :]
    down_all, grad_resid, active, grad_exp, grad_ret, grad_mixed, sums, bias = refs[:8]
    heads, w_up, w_down, sems = refs[8:]
    step = pl.program_id(0)
    rows, width = cot.shape
    segs = rows // SEG

    @pl.when(step == 0)
    def _():
        fetch_units(plan, sections[0], info, pieces, down_all, w_up, w_down, sems)
        total = back_heads[...]
        for member in ring:
            total = total + member[...].astype(FULL)
        heads[...] = total

    row = lax.broadcasted_iota(jnp.int32, (SEG, 1), 0)
    first = info[plan.mp_at] * (pl.num_programs(0) * segs) + step * segs
    blocks = []
    for seg in range(segs):
        piece = cot[seg * SEG : (seg + 1) * SEG, :].astype(FULL)
        piece = jnp.where(row < info[step * segs + seg], piece, 0.0)
        blocks.append(jnp.where(row == 0, heads[pl.ds(first + seg, 1), :], piece))
    grad = jnp.concatenate(blocks, axis=0)
    unit, scale = normal(resid_two[...])

    @pl.when(step == 0)
    def _():
        sums[...] = jnp.zeros_like(sums)
        bias[...] = jnp.zeros_like(bias)

    back = normal_back(grad, unit, scale, affine[2:3, :])
    sums[2:3, :] += jnp.sum(grad * unit, axis=0, keepdims=True)
    sums[3:4, :] += jnp.sum(grad, axis=0, keepdims=True)
    sums[5:6, :] += jnp.sum(back, axis=0, keepdims=True)
    low = back.astype(LOW)
    grad_ret[...] = low
    units = w_up.shape[1]
    total = back
    block = width

    @pl.when(step == 0)
    def _():
        ups, downs = fetch_units(plan, sections[0], info, pieces, down_all, w_up, w_down, sems, False)
        wait_all(downs)
        wait_all(ups)

    for at in range(0, units, block):
        grad_act = dot_nt(low, w_down[at : at + block, :])
        up = expanded[:, at : at + block].astype(FULL)
        square = up * up
        curve = jnp.tanh(TANH_A * (up + TANH_B * up * square))
        half = 0.5 * (1.0 + curve)
        active[:, at : at + block] = (up * half).astype(LOW)
        slope = half + 0.5 * up * (1.0 - curve * curve) * (TANH_A + 3.0 * TANH_A * TANH_B * square)
        wide = slope * grad_act
        bias[:, at : at + block] += jnp.sum(wide, axis=0, keepdims=True)
        short = wide.astype(LOW)
        grad_exp[:, at : at + block] = short
        total = total + dot_nt(short, w_up[:, at : at + block])
    unit, scale = normal(resid[...])
    back = normal_back(total, unit, scale, affine[0:1, :])
    sums[0:1, :] += jnp.sum(total * unit, axis=0, keepdims=True)
    sums[1:2, :] += jnp.sum(total, axis=0, keepdims=True)
    sums[4:5, :] += jnp.sum(back, axis=0, keepdims=True)
    grad_resid[...] = back
    grad_mixed[...] = back.astype(LOW)


def pair_back(query, keys, values, probs, down, low, span):
    grad_probs = dot_nt(down, values)
    scores = []
    for half in range(2):
        mine = probs[half]
        given = grad_probs[:, half * span : (half + 1) * span]
        product = mine * given
        inner = jnp.sum(product, axis=-1, keepdims=True)
        scores.append((product - mine * inner).astype(LOW))
    grad_scores = jnp.concatenate(scores, axis=1)
    probs = jnp.concatenate([part.astype(LOW) for part in probs], axis=1)
    grad_query = dot_nn(grad_scores, keys) * HEAD_DIM ** (-0.5)
    both = dot_tn(grad_scores, query)
    grad_key = jnp.where(low, both[:span], both[span:])
    both = dot_tn(probs, down)
    return grad_query, grad_key, jnp.where(low, both[:span], both[span:])


def attend_back_kernel(info, grad_resid, grad_mixed, triple, chances, context, w_out, w_in, early, grad_in, grad_triple, grad_ctx):
    del early
    rows, width = grad_resid.shape
    grad_ctx[...] = dot_nt(grad_mixed[...], w_out[...]).astype(LOW)
    low = lax.broadcasted_iota(jnp.int32, (SEG, LANES), 1) < HEAD_DIM
    for seg in range(rows // SEG):
        here = slice(seg * SEG, (seg + 1) * SEG)
        for pair in range(width // LANES):
            at = pair * LANES
            query = triple[here, at : at + LANES] * LOW(HEAD_DIM ** (-0.5))
            keys = halves(triple[here, width + at : width + at + LANES], low)
            values = halves(triple[here, 2 * width + at : 2 * width + at + LANES], low)
            probs = chances[here, 2 * at : 2 * at + 2 * SEG]
            down = grad_ctx[here, at : at + LANES]
            product = down.astype(FULL) * context[here, at : at + LANES].astype(FULL)
            left = jnp.sum(jnp.where(low, product, 0.0), axis=-1, keepdims=True)
            right = jnp.sum(jnp.where(low, 0.0, product), axis=-1, keepdims=True)
            grad_probs = dot_nt(down, values)
            scores = [grad_probs[:, :SEG] - left, grad_probs[:, SEG:] - right]
            grad_scores = (probs.astype(FULL) * jnp.concatenate(scores, axis=1)).astype(LOW)
            grad_query = dot_nn(grad_scores, keys) * HEAD_DIM ** (-0.5)
            both = dot_tn(grad_scores, query)
            grad_key = jnp.where(low, both[:SEG], both[SEG:])
            both = dot_tn(probs, down)
            grad_value = jnp.where(low, both[:SEG], both[SEG:])
            for part, found in enumerate((grad_query, grad_key, grad_value)):
                goal = part * width + at
                grad_triple[here, goal : goal + LANES] = found.astype(LOW)
    grad_in[...] = (grad_resid[...] + dot_nt(grad_triple[...], w_in[...])).astype(LOW)


def unit_grad_kernel(
    plan, info, active, grad_ret, hid_low, grad_exp, context, grad_mixed, sums_one, sums_two, grad_heads, bias, bias_two, *refs
):
    saved, (out, whole, mixing, small, second) = refs[:-5], refs[-5:]
    m = pl.program_id(0)
    extra = second.shape[1] // plan.groups
    rest_at = out.shape[2] - extra
    size = plan.rows
    width = whole.shape[0]
    third = width // plan.groups
    share = third // out.shape[0]

    @pl.when(m == 0)
    def _():
        second_grads_into(plan, *saved, second)
        found = dot_tn(context[...], grad_mixed[...])
        for at in range(plan.groups):
            mixing[at * third : at * third + LANES, :] = found[at * LANES : (at + 1) * LANES]
            goal = plan.groups * LANES + at * HEAD_DIM
            mixing[at * third + LANES : (at + 1) * third, :] = found[goal : goal + HEAD_DIM]

    part = pl.ds(pl.multiple_of(m * extra, 16), extra)
    for at in range(out.shape[0]):
        out[at, 0, rest_at:, :] = second[at, part, :]
    step = padded(size)
    for kind, (left, right) in enumerate(((active, grad_ret), (hid_low, grad_exp))):
        whole[...] = dot_tn(left[...], right[...])
        for at in range(out.shape[0]):
            out[at, 0, kind * step : kind * step + size, :] = whole[
                at * size : (at + 1) * size, :
            ].astype(LOW)
    leader = jnp.where(info[plan.mp_at] == 0, 1.0, 0.0)
    row = lax.broadcasted_iota(jnp.int32, (8, 1), 0)
    place = pl.multiple_of(info[plan.mp_at + m] * width, LANES)
    own = jnp.where(m == 0, 1.0, 0.0)
    biases = jnp.where(row == 6, bias[:, pl.ds(place, width)], bias_two[...] * own)
    small[0:8, :] = jnp.where(row < 6, sums_one[...], biases)
    small[8:16, :] = sums_two[...] * leader
    position = grad_heads[0:NSEG, :]
    for doc in range(1, grad_heads.shape[0] // NSEG):
        position = position + grad_heads[doc * NSEG : (doc + 1) * NSEG, :]
    small[16:, :] = position * leader
    gap = jnp.zeros((8, LANES - size), FULL)
    mine = mixing[pl.ds(pl.multiple_of(m * third, HEAD_DIM), third), :]
    for at in range(out.shape[0]):
        lines = small[:, at * size : (at + 1) * size]
        blocks = []
        for block in range(width // LANES):
            blocks += [lines[block * 8 : (block + 1) * 8], gap]
        rows = [jnp.concatenate(blocks, axis=1), mine[at * share : (at + 1) * share]]
        rest = rest_at - 2 * step - share - 8
        if rest:
            rows.append(jnp.zeros((rest, width), FULL))
        out[at, 0, 2 * step : rest_at, :] = jnp.concatenate(rows, axis=0).astype(LOW)


def head_grad_kernel(plan, lists, info, tok, grad_triple, early, keep_a, send_a, keep_b, send_b, whole):
    del early
    size = plan.rows
    width = tok.shape[1]
    whole[...] = dot_tn(tok[...], grad_triple[...])
    low = lax.broadcasted_iota(jnp.int32, (size, LANES), 1) < HEAD_DIM
    for half, (keep, send) in enumerate(((keep_a, send_a), (keep_b, send_b))):
        for at, place in enumerate(lists[half]):
            for out, which in ((keep, place), (send, place ^ 1)):
                start = pl.multiple_of(info[plan.dp_at + which] * size, 8)
                for inner in range(plan.groups // 2):
                    m = half * (plan.groups // 2) + inner
                    for part in range(3):
                        goal = part * width + m * LANES
                        out[at, inner, :, part * LANES : (part + 1) * LANES] = whole[
                            pl.ds(start, size), goal : goal + LANES
                        ].astype(LOW)
                    blocks = []
                    for part in range(3):
                        goal = part * width + (plan.groups + m // 2) * LANES
                        blocks.append(whole[pl.ds(start, size), goal : goal + LANES])
                    if m % 2 == 0:
                        blocks = [blocks[0], turn(blocks[1]), blocks[2]]
                    else:
                        blocks = [turn(blocks[0]), blocks[1], turn(blocks[2])]
                    out[at, inner, :, 3 * LANES : 4 * LANES] = jnp.where(low, blocks[0], blocks[1]).astype(LOW)
                    out[at, inner, :, 4 * LANES : 5 * LANES] = jnp.where(low, blocks[2], 0.0).astype(LOW)


def tops_kernel(info, tops, rows, out, held, in_sems, out_sems):
    row = lax.broadcasted_iota(jnp.int32, (16, 1), 0)
    parts = in_sems.shape[0]
    segs = tops.shape[0] // parts
    ins, outs = [], []
    for part in range(parts):
        where = pl.ds(part * segs * SEG, segs * SEG)
        ins.append(pltpu.make_async_copy(rows.at[where, :], held.at[where, :], in_sems.at[part]))
        outs.append(pltpu.make_async_copy(held.at[where, :], out.at[where, :], out_sems.at[part]))
        ins[-1].start()
    for part in range(parts):
        ins[part].wait()
        for seg in range(part * segs, (part + 1) * segs):
            near = slice(seg * SEG, seg * SEG + 16)
            held[near, :] = jnp.where(row == 0, tops[seg : seg + 1, :].astype(LOW), held[near, :])
        outs[part].start()
    wait_all(outs)


def spread_kernel(groups, mp_at, steps, info, *refs):
    count = len(steps)
    line, (out, held, ready, in_sems, out_sems) = refs[:count], refs[-5:]
    rows = held.shape[1]
    mine = info[mp_at]

    def take(at, step, part):
        place = mine + step
        into = pltpu.make_async_copy(line[at], held.at[at], in_sems.at[at])
        goal = pl.ds(pl.multiple_of(place * rows, rows), rows)
        back = pltpu.make_async_copy(ready.at[at], out.at[goal, :], out_sems.at[at])

        @pl.when(jnp.logical_and(place >= 0, place < groups))
        def _():
            if part == 0:
                into.start()
            elif part == 2:
                back.wait()
            else:
                into.wait()
                ready[at] = held[at].astype(ready.dtype)
                back.start()

    for part in range(3):
        for at, step in enumerate(steps):
            take(at, step, part)


def rows_of(block, width):
    return pl.BlockSpec((block, width), lambda i, c: (i, 0))


def load_own(section, source, target, sems):
    base, size = section
    copies = []
    for at in range(source.shape[0]):
        copy = pltpu.make_async_copy(
            source.at[at, pl.ds(base, size), :], target.at[pl.ds(at * size, size), :], sems.at[at]
        )
        copy.start()
        copies.append(copy)
    return copies


def own_out(stage, w_out, count):
    share = (w_out.shape[0] - HEAD_DIM) // count
    step = stage.shape[0] // count
    parts = [stage[at * step : (at + 1) * step, :].astype(FULL)[:share] for at in range(count)]
    parts.append(jnp.zeros((HEAD_DIM, stage.shape[1]), FULL))
    w_out[...] = jnp.concatenate(parts, axis=0).astype(LOW)


def ring_sum(plan, info, ring, total):
    for at, member in enumerate(ring):
        total[info[plan.mp_at + at]] = member[...].astype(FULL)
    found = total[0]
    for at in range(1, plan.groups):
        found = found + total[at]
    return found


def own_pairs(triple, here, live, low):
    zero = jnp.zeros((NSEG, LANES), LOW)
    block = [triple[here, at * LANES : (at + 1) * LANES] for at in range(5)]
    last = turn(block[3].astype(FULL)).astype(LOW)
    found = []
    for query, key, value in (
        (block[0], block[1], block[2]),
        (jnp.where(low, block[3], zero), jnp.where(low, last, zero), jnp.where(low, block[4], zero)),
    ):
        query = query * LOW(HEAD_DIM ** (-0.5))
        keys, values = halves(key, low), halves(value, low)
        found.append((query, keys, values, soft(query, keys, live, NSEG)))
    return found


def second_one_kernel(plan, sections, info, *refs):
    ring, refs = refs[: plan.groups], refs[plan.groups :]
    position, live, in_all, out_all, term, entry, tok, triple, context = refs[:9]
    heads, w_in, w_out, stage, sems = refs[9:]
    rows = entry.shape[0]
    copies = load_own(sections[0], in_all, w_in, sems.at[0])
    outs = load_own(sections[1], out_all, stage, sems.at[1])
    slots = ring[0].shape[0]
    for at in range(plan.groups):
        goal = pl.multiple_of(info[plan.mp_at + at] * slots, slots)
        heads[pl.ds(goal, slots), :] = ring[at][...]
    docs = rows // NSEG
    entry[...] = heads[...] + jnp.concatenate([position[...]] * docs, axis=0)
    tok[...] = entry[...].astype(LOW)
    wait_all(copies)
    triple[...] = dot_nn(tok[...], w_in[:, : 5 * LANES]).astype(LOW)
    low = lax.broadcasted_iota(jnp.int32, (NSEG, LANES), 1) < HEAD_DIM
    for doc in range(docs):
        here = slice(doc * NSEG, (doc + 1) * NSEG)
        mask = live[doc : doc + 1, :] > 0.5
        for pair, (_, _, values, probs) in enumerate(own_pairs(triple, here, mask, low)):
            probs = jnp.concatenate([part.astype(LOW) for part in probs], axis=1)
            context[here, pair * LANES : (pair + 1) * LANES] = dot_nn(probs, values).astype(LOW)
    wait_all(outs)
    own_out(stage, w_out, plan.count)
    term[...] = dot_nn(context[...], w_out[...]).astype(LOW)


def second_two_kernel(plan, sections, info, *refs):
    ring, refs = refs[: plan.groups], refs[plan.groups :]
    entry, affine, b_up, up_all, down_all, term, resid, hid_low, expanded, active = refs[:10]
    total, w_up, w_down, sems = refs[10:]
    copies = load_own(sections[2], up_all, w_up, sems.at[0])
    downs = load_own(sections[3], down_all, w_down, sems.at[1])
    value = entry[...] + ring_sum(plan, info, ring, total) + affine[4:5, :]
    resid[...] = value
    hid_low[...] = (normal(value)[0] * affine[0:1, :] + affine[1:2, :]).astype(LOW)
    wait_all(copies)
    up = dot_nn(hid_low[...], w_up[...]) + b_up[7:8, :]
    expanded[...] = up
    active[...] = (0.5 * up * (1.0 + jnp.tanh(TANH_A * (up + TANH_B * up * up * up)))).astype(LOW)
    wait_all(downs)
    term[...] = dot_nn(active[...], w_down[...]).astype(LOW)


def second_three_kernel(plan, sections, info, *refs):
    ring, refs = refs[: plan.groups], refs[plan.groups :]
    resid, expanded, top_grad, affine, up_all, down_all = refs[:6]
    term, second, back_two, grad_ret, grad_exp, sums, bias = refs[6:13]
    total, w_up, w_down, sems = refs[13:]
    copies = load_own(sections[3], down_all, w_down, sems.at[0])
    ups = load_own(sections[2], up_all, w_up, sems.at[1])
    hidden = normal(resid[...])[0] * affine[0:1, :] + affine[1:2, :]
    unit, scale = normal(hidden + ring_sum(plan, info, ring, total) + affine[5:6, :])
    second[...] = unit * affine[2:3, :] + affine[3:4, :]
    grad = top_grad[...]
    back = normal_back(grad, unit, scale, affine[2:3, :])
    back_two[...] = back
    sums[...] = jnp.zeros_like(sums)
    sums[2:3, :] = jnp.sum(grad * unit, axis=0, keepdims=True)
    sums[3:4, :] = jnp.sum(grad, axis=0, keepdims=True)
    sums[5:6, :] = jnp.sum(back, axis=0, keepdims=True)
    grad_ret[...] = back.astype(LOW)
    wait_all(copies)
    given = dot_nt(grad_ret[...], w_down[...])
    up = expanded[...]
    square = up * up
    curve = jnp.tanh(TANH_A * (up + TANH_B * up * square))
    half = 0.5 * (1.0 + curve)
    slope = half + 0.5 * up * (1.0 - curve * curve) * (TANH_A + 3.0 * TANH_A * TANH_B * square)
    wide = slope * given
    bias[...] = jnp.sum(wide, axis=0, keepdims=True)
    grad_exp[...] = wide.astype(LOW)
    wait_all(ups)
    term[...] = dot_nt(grad_exp[...], w_up[...]).astype(LOW)


def second_four_kernel(plan, sections, info, *refs):
    ring, refs = refs[: plan.groups], refs[plan.groups :]
    resid, back_two, triple, live, sums_in, affine, in_all, out_all = refs[:8]
    term, back_one, grad_mixed, grad_triple, sums = refs[8:13]
    total, w_in, w_out, stage, sems = refs[13:]
    outs = load_own(sections[1], out_all, stage, sems.at[0])
    copies = load_own(sections[0], in_all, w_in, sems.at[1])
    rows = resid.shape[0]
    grad = back_two[...] + ring_sum(plan, info, ring, total)
    unit, scale = normal(resid[...])
    back = normal_back(grad, unit, scale, affine[0:1, :])
    back_one[...] = back
    sums[...] = sums_in[...]
    sums[0:1, :] = jnp.sum(grad * unit, axis=0, keepdims=True)
    sums[1:2, :] = jnp.sum(grad, axis=0, keepdims=True)
    sums[4:5, :] = jnp.sum(back, axis=0, keepdims=True)
    grad_mixed[...] = back.astype(LOW)
    wait_all(outs)
    own_out(stage, w_out, plan.count)
    grad_ctx = dot_nt(grad_mixed[...], w_out[...]).astype(LOW)
    low = lax.broadcasted_iota(jnp.int32, (NSEG, LANES), 1) < HEAD_DIM
    for doc in range(rows // NSEG):
        here = slice(doc * NSEG, (doc + 1) * NSEG)
        mask = live[doc : doc + 1, :] > 0.5
        found = []
        for pair, (query, keys, values, probs) in enumerate(own_pairs(triple, here, mask, low)):
            down = grad_ctx[here, pair * LANES : (pair + 1) * LANES]
            found.append(pair_back(query, keys, values, probs, down, low, NSEG))
        blocks = list(found[0])
        blocks.append(jnp.where(low, found[1][0], turn(found[1][1])))
        blocks.append(jnp.where(low, found[1][2], 0.0))
        for at, block in enumerate(blocks):
            grad_triple[here, at * LANES : (at + 1) * LANES] = block.astype(LOW)
    wait_all(copies)
    term[...] = dot_nt(grad_triple[...], w_in[:, : 5 * LANES]).astype(LOW)


def second_grads_into(plan, tok, grad_triple, context, grad_mixed, hid_low, grad_exp, active, grad_ret, out):
    width = tok.shape[1]
    count, size = plan.count, plan.rows
    step = padded(size)
    share = width // plan.groups // count
    for kind, (left, right) in enumerate(
        ((tok, grad_triple), (hid_low, grad_exp), (active, grad_ret))
    ):
        value = dot_tn(left[...], right[...])
        if kind == 0:
            value = jnp.concatenate([value, jnp.zeros((width, LANES), FULL)], axis=1)
        for at in range(count):
            out[at, kind * step : kind * step + size, :] = value[at * size : (at + 1) * size].astype(LOW)
    value = dot_tn(context[...], grad_mixed[...])
    rest = out.shape[1] - 3 * step - share
    for at in range(count):
        rows = [value[at * share : (at + 1) * share]]
        if rest:
            rows.append(jnp.zeros((rest, width), FULL))
        out[at, 3 * step :, :] = jnp.concatenate(rows, axis=0).astype(LOW)


def collect_kernel(plan, info, *refs):
    count = plan.groups - 1
    unit_own, unit_ring, refs = refs[0], refs[1 : plan.groups], refs[plan.groups :]
    left, right, head_ring, refs = refs[0], refs[1], refs[2 : 2 + count], refs[2 + count :]
    unit_sum, head_sum, second, squares = refs
    tall = unit_sum.shape[0]
    extra = unit_own.shape[1] - tall
    for m in range(plan.groups):
        second[m * extra : (m + 1) * extra, :] = unit_own[m, tall:, :].astype(FULL)
    total = unit_own[0, :tall].astype(FULL)
    for member in unit_ring:
        total = total + member[...].astype(FULL)
    unit_sum[...] = total
    heads = left[0].astype(FULL) + right[0].astype(FULL)
    for member in head_ring:
        heads = heads + member[...].astype(FULL)
    head_sum[...] = heads
    leader = jnp.where(info[plan.mp_at] == 0, 1.0, 0.0)
    step = padded(plan.rows)
    row = lax.broadcasted_iota(jnp.int32, (8, total.shape[1]), 0)
    lane = lax.broadcasted_iota(jnp.int32, (8, total.shape[1]), 1)
    once = jnp.logical_and(row >= 6, lane < LANES)

    def square(value):
        return jnp.sum(jnp.sum(value * value, axis=0, keepdims=True), axis=1, keepdims=True)

    small = total[2 * step : 2 * step + 8]
    found = square(total[: 2 * step]) + square(total[2 * step + 8 :])
    found = found + square(jnp.where(once, small, small * leader))
    found = found + square(heads) + square(second[...])
    squares[...] = jnp.broadcast_to(found, squares.shape)


def update_kernel(plan, info, squares, unit_sum, head_sum, second, *refs):
    states, news, norm = refs[:7], refs[7:28], refs[28]
    total = squares[...]
    norm[...] = jnp.sqrt(total)
    factor = jnp.minimum(1.0, clip_level / jnp.sqrt(total[0:1, 0:1]))
    size, step = plan.rows, padded(plan.rows)
    share = states[1].shape[2]

    def put(kind, where, grad):
        state = states[kind]
        old = [state[(at, *where)] for at in range(3)]
        for at, value in enumerate(adam(old, grad, factor)):
            news[7 * at + kind][where] = value

    def columns(block):
        at = [block[:, i * HEAD_DIM : (i + 1) * HEAD_DIM] for i in range(9)]
        return jnp.concatenate([at[i] for i in (0, 2, 4, 1, 3, 5, 6, 7, 8)], axis=1)

    every = slice(None)
    put(0, (0, every, every), columns(head_sum[...]))
    put(0, (1, every, every), columns(second[:size, :]))
    put(1, (0, every, every), unit_sum[2 * step + 8 : 2 * step + 8 + share, :])
    put(1, (1, every, every), second[3 * step : 3 * step + share, :])
    put(2, (0, every, every), unit_sum[step : step + size, :])
    put(2, (1, every, every), second[step : step + size, :])
    put(4, (0, every, every), unit_sum[:size, :])
    put(4, (1, every, every), second[2 * step : 2 * step + size, :])
    small = unit_sum[2 * step : 2 * step + 8, :]
    put(3, (every, every), small[6:8, :size])
    put(5, (0, every, every), small[0:6, :size])
    put(5, (1, every, every), small[0:6, LANES : LANES + size])
    for block in range(NSEG // 8):
        goal = (block + 2) * LANES
        put(6, (slice(block * 8, (block + 1) * 8), every), small[:, goal : goal + size])


def own_rows(plan, rows, block, width):
    return pl.BlockSpec((block, width), lambda i, c: (c[plan.mp_at] * (rows // block) + i, 0))


WHOLE = pl.BlockSpec(memory_space=pltpu.VMEM)
OUTSIDE = pl.BlockSpec(memory_space=pl.ANY)


def shape(*dims, kind=LOW):
    return jax.ShapeDtypeStruct(dims, kind)


def run(kernel, steps, ins, outs, scratch, micros, info, args, aliases=None):
    return pl.pallas_call(
        kernel,
        grid_spec=pltpu.PrefetchScalarGridSpec(
            num_scalar_prefetch=1,
            grid=(steps,),
            in_specs=ins,
            out_specs=[spec for spec, _ in outs],
            scratch_shapes=scratch,
        ),
        out_shape=[kind for _, kind in outs],
        input_output_aliases=aliases or {},
        compiler_params=pltpu.CompilerParams(vmem_limit_bytes=VMEM_BYTES),
        cost_estimate=pl.CostEstimate(
            flops=int(micros * FLOPS), bytes_accessed=1024, transcendentals=0
        ),
    )(info, *args)


def layer_of(state, layer):
    return pl.BlockSpec((1, 1, *state.shape[2:]), lambda i, c: (0, layer, 0, 0))


def heads_block_of(info, attend_in, bias, affine, position):
    return run(
        heads_block_kernel,
        1,
        [layer_of(attend_in, 0), WHOLE, WHOLE, WHOLE],
        [(WHOLE, shape(attend_in.shape[2], 5 * LANES))],
        [pltpu.VMEM((LANES, LANES), FULL)],
        2,
        info,
        (attend_in, bias, affine, position),
    )[0]


def units_block_of(info, layer, states):
    rows = sum(padded(state.shape[2]) for state in states)
    return run(
        units_block_kernel,
        1,
        [layer_of(state, layer) for state in states],
        [(WHOLE, shape(rows, states[-1].shape[3]))],
        [],
        2,
        info,
        states,
    )[0]


def attend_forward(plan, info, tok, pieces, block=512):
    rows, width = tok.shape[0] // plan.groups, tok.shape[1]
    lanes = pieces[0].shape[-1]
    wide = rows_of(block, 3 * width)
    return run(
        functools.partial(attend_kernel, plan),
        rows // block,
        [own_rows(plan, rows, block, width)] + [OUTSIDE] * len(pieces),
        [
            (wide, shape(rows, 3 * width)),
            (rows_of(block, width), shape(rows, width)),
            (rows_of(block, 2 * width), shape(rows, 2 * width)),
            (WHOLE, shape(width, 3 * width)),
            (WHOLE, shape(8, width, kind=FULL)),
            (WHOLE, shape(8, width, kind=FULL)),
            (WHOLE, shape(NSEG, width, kind=FULL)),
            (WHOLE, shape(1, plan.groups * width, kind=FULL)),
        ],
        [
            pltpu.VMEM((plan.groups, width, lanes), LOW),
            pltpu.SemaphoreType.DMA((plan.copies(),)),
        ],
        18,
        info,
        (tok, *pieces),
    )


def feed_forward(plan, sections, info, tok, context, affine, b_up, pieces, weights, block=512):
    rows, width = context.shape
    units = b_up.shape[1]
    line = rows_of(block, width)
    downs = plan.groups * weights[0].shape[1]
    return run(
        functools.partial(feed_kernel, plan, sections),
        rows // block,
        [own_rows(plan, rows, block, width), line, WHOLE, WHOLE]
        + [OUTSIDE] * (2 + len(pieces)),
        [
            (line, shape(rows, width, kind=FULL)),
            (line, shape(rows, width)),
            (rows_of(block, units), shape(rows, units)),
            (line, shape(rows, width, kind=FULL)),
            (line, shape(rows, width)),
            (WHOLE, shape(rows // SEG, width, kind=FULL)),
            (WHOLE, shape(width, width)),
        ],
        [
            pltpu.VMEM((width, units), LOW),
            pltpu.VMEM((units, width), LOW),
            pltpu.VMEM((plan.groups, weights[1].shape[1] * sections[1][1], width), LOW),
            pltpu.SemaphoreType.DMA((2, max(downs, plan.copies()))),
            pltpu.SemaphoreType.DMA((downs,)),
        ],
        24,
        info,
        (tok, context, affine, b_up, *weights, *pieces),
    )


def feed_backward(plan, sections, info, cot, back_heads, ring, resid_two, expanded, resid, affine, pieces, weights, block=256):
    rows, width = resid.shape
    units = expanded.shape[1]
    line, wide = rows_of(block, width), rows_of(block, units)
    return run(
        functools.partial(feed_back_kernel, plan, sections),
        rows // block,
        [own_rows(plan, rows, block, width), WHOLE, line, wide, line, WHOLE]
        + [WHOLE] * plan.groups
        + [OUTSIDE] * (1 + len(pieces)),
        [
            (line, shape(rows, width, kind=FULL)),
            (wide, shape(rows, units)),
            (wide, shape(rows, units)),
            (line, shape(rows, width)),
            (line, shape(rows, width)),
            (WHOLE, shape(8, width, kind=FULL)),
            (WHOLE, shape(1, units, kind=FULL)),
            (WHOLE, shape(*back_heads.shape, kind=FULL)),
        ],
        [
            pltpu.VMEM((width, units), LOW),
            pltpu.VMEM((units, width), LOW),
            pltpu.SemaphoreType.DMA((2, max(plan.groups * weights[0].shape[1], plan.copies()))),
        ],
        28,
        info,
        (cot, back_heads, resid_two, expanded, resid, affine, *ring, *pieces, weights[0]),
    )


def attend_backward(info, grad_resid, grad_mixed, triple, chances, context, w_out, w_in, early, block=512):
    rows, width = grad_resid.shape
    line, wide = rows_of(block, width), rows_of(block, 3 * width)
    return run(
        attend_back_kernel,
        rows // block,
        [line, line, wide, rows_of(block, 2 * width), line, WHOLE, WHOLE, OUTSIDE],
        [(line, shape(rows, width)), (wide, shape(rows, 3 * width))],
        [pltpu.VMEM((block, width), LOW)],
        30,
        info,
        (grad_resid, grad_mixed, triple, chances, context, w_out, w_in, early),
    )


def second_run(kernel, plan, sections, info, ring, args, weights, outs, scratch):
    count = weights[0].shape[0]
    return run(
        functools.partial(kernel, plan, sections),
        1,
        [WHOLE] * (len(ring) + len(args)) + [OUTSIDE] * len(weights),
        [(WHOLE, kind) for kind in outs],
        scratch + [pltpu.SemaphoreType.DMA((2, count))],
        5,
        info,
        (*ring, *args, *weights),
    )


def second_layer(sections, plan, info, ring, position, live, top_grad, affine, b_up, weights):
    rows, width = top_grad.shape
    groups = plan.groups
    in_all, out_all, up_all, down_all = weights
    own = width // groups
    tall = out_all.shape[0] * sections[1][1]
    full, low = shape(rows, width, kind=FULL), shape(rows, width)
    mixed = shape(rows, 5 * LANES)
    total = pltpu.VMEM((groups, rows, width), FULL)
    square = pltpu.VMEM((width, width), LOW)
    outer = [pltpu.VMEM((own + HEAD_DIM, width), LOW), pltpu.VMEM((tall, width), LOW)]

    term, entry, tok, triple, context = second_run(
        second_one_kernel, plan, sections, info, ring, (position, live), (in_all, out_all),
        [low, full, low, mixed, shape(rows, own + HEAD_DIM)],
        [pltpu.VMEM((rows, width), FULL), square] + outer,
    )
    term, resid, hid_low, expanded, active = second_run(
        second_two_kernel, plan, sections, info, around(term), (entry, affine, b_up), (up_all, down_all),
        [low, full, low, full, low],
        [total, square, square],
    )
    term, second, back_two, grad_ret, grad_exp, sums, bias = second_run(
        second_three_kernel, plan, sections, info, around(term), (resid, expanded, top_grad, affine), (up_all, down_all),
        [low, full, full, low, low, shape(8, width, kind=FULL), shape(1, width, kind=FULL)],
        [total, square, square],
    )
    term, back_one, grad_mixed, grad_triple, sums = second_run(
        second_four_kernel, plan, sections, info, around(term),
        (resid, back_two, triple, live, sums, affine), (in_all, out_all),
        [low, full, low, mixed, shape(8, width, kind=FULL)],
        [total, square] + outer,
    )
    saved = (tok, grad_triple, context, grad_mixed, hid_low, grad_exp, active, grad_ret)
    return second, back_one, around(term), sums, bias, saved


def second_rows(plan, width):
    size = 3 * padded(plan.rows) + padded(width // plan.groups // plan.count)
    return -(-size // (16 * plan.groups)) * 16 * plan.groups


def place_tops(info, tops, rows):
    return run(
        tops_kernel,
        1,
        [WHOLE, OUTSIDE],
        [(OUTSIDE, shape(*rows.shape))],
        [
            pltpu.VMEM(rows.shape, LOW),
            pltpu.SemaphoreType.DMA((8,)),
            pltpu.SemaphoreType.DMA((8,)),
        ],
        4,
        info,
        (tops, rows),
    )[0]


def spread_out(groups, mp_at, info, line, steps, before):
    count = len(line)
    rows, width = line[0].shape
    again = before.shape[0] == groups * rows
    return run(
        functools.partial(spread_kernel, groups, mp_at, steps),
        1,
        [OUTSIDE] * (count + 1),
        [(OUTSIDE, shape(groups * rows, width, kind=FULL))],
        [
            pltpu.VMEM((count, rows, width), line[0].dtype),
            pltpu.VMEM((count, rows, width), FULL),
            pltpu.SemaphoreType.DMA((count,)),
            pltpu.SemaphoreType.DMA((count,)),
        ],
        3 if again else 6,
        info,
        (*line, before),
        {count + 1: 0} if again else None,
    )[0]


def unit_rows(plan, width):
    return 2 * padded(plan.rows) + padded(width // plan.groups // plan.count + 8)


def unit_grads(plan, info, active, grad_ret, hid_low, grad_exp, context, grad_mixed, small, saved):
    rows, width = grad_ret.shape
    fixed = pl.BlockSpec((rows, width), lambda m, c: (0, 0))
    moving = pl.BlockSpec((rows, width), lambda m, c: (0, c[plan.mp_at + m]))
    tall = second_rows(plan, width)
    size = unit_rows(plan, width) + tall // plan.groups
    out = pl.BlockSpec((plan.count, 1, size, width), lambda m, c: (0, m, 0, 0))
    square = pltpu.VMEM((width, width), FULL)
    return run(
        functools.partial(unit_grad_kernel, plan),
        plan.groups,
        [moving, fixed, fixed, moving, fixed, fixed] + [WHOLE] * (len(small) + len(saved)),
        [(out, shape(plan.count, plan.groups, size, width))],
        [
            square,
            square,
            pltpu.VMEM((width // LANES * 8, width), FULL),
            pltpu.VMEM((plan.count, tall, width), LOW),
        ],
        19,
        info,
        (active, grad_ret, hid_low, grad_exp, context, grad_mixed, *small, *saved),
    )[0]


def collect(plan, info, unit_own, unit_ring, head_own, head_ring):
    extra = (unit_own.shape[1] - unit_ring[0].shape[0]) * plan.groups
    return run(
        functools.partial(collect_kernel, plan),
        1,
        [WHOLE] * (3 + len(unit_ring) + len(head_ring)),
        [
            (WHOLE, shape(*unit_ring[0].shape, kind=FULL)),
            (WHOLE, shape(*head_ring[0].shape, kind=FULL)),
            (WHOLE, shape(extra, unit_own.shape[2], kind=FULL)),
            (WHOLE, shape(8, LANES, kind=FULL)),
        ],
        [],
        4,
        info,
        (unit_own, *unit_ring, *head_own, *head_ring),
    )


def update(plan, info, squares, unit_sum, head_sum, second, states):
    outs = [(WHOLE, shape(*state.shape[1:], kind=FULL)) for _ in range(3) for state in states]
    return run(
        functools.partial(update_kernel, plan),
        1,
        [WHOLE] * (4 + len(states)),
        outs + [(WHOLE, shape(8, LANES, kind=FULL))],
        [],
        7,
        info,
        (squares, unit_sum, head_sum, second, *states),
    )


def head_grads(plan, lists, info, tok, grad_triple, early):
    rows, width = grad_triple.shape[0], tok.shape[1]
    out = shape(len(lists[0]), plan.groups // 2, plan.rows, 5 * LANES)
    return run(
        functools.partial(head_grad_kernel, plan, lists),
        1,
        [own_rows(plan, rows, rows, width), WHOLE, OUTSIDE],
        [(WHOLE, out)] * 4,
        [pltpu.VMEM((width, 3 * width), FULL)],
        10,
        info,
        (tok, grad_triple, early),
    )


def swap(value, bit, axis="dp"):
    return lax.ppermute(value, axis, [(i, i ^ bit) for i in range(lax.axis_size(axis))])


def ahead(value, step):
    size = lax.axis_size("mp")
    return lax.ppermute(value, "mp", [(i, (i + step) % size) for i in range(size)])


def onward(value, step):
    size = lax.axis_size("mp")
    return lax.ppermute(
        value, "mp", [(i, i + step) for i in range(size) if 0 <= i + step < size]
    )


def all_sum(value, axes):
    for axis in axes:
        bit = 1
        while bit < lax.axis_size(axis):
            value = value + swap(value, bit, axis)
            bit *= 2
    return value


def around(value):
    return [value] + [ahead(value, step) for step in range(1, lax.axis_size("mp"))]


def bits_of(count):
    bits, bit = [], 2
    while bit < count:
        bits.append(bit)
        bit *= 2
    return bits


def tie(value, *first):
    return lax.optimization_barrier((value, first))[0]


def gather(ring, gates, hold=()):
    half = len(ring) // 2
    bits = bits_of(lax.axis_size("dp"))
    held = [[([0], jnp.stack(ring[:half])[None])], [([0], jnp.stack(ring[half:])[None])]]
    arrived = []
    for stage in range(len(bits)):
        arrived.append([])
        for which, order in enumerate((bits, bits[::-1])):
            bit = order[stage]
            places = sum((member[0] for member in held[which]), [])
            block = [member[1] for member in held[which]]
            block = block[0] if len(block) == 1 else jnp.concatenate(block)
            if stage < len(gates):
                block = tie(block, *gates[stage])
            got = swap(block, bit)
            arrived[-1].append(got)
            held[which] = [(places, block), ([j ^ bit for j in places], got)]
    pieces = []
    for which in range(2):
        for places, block in held[which]:
            pieces.append((places, which, block))
            pieces.append(([j ^ 1 for j in places], which, swap(tie(block, *hold), 1)))
    return pieces, arrived


def pick(stack, order, count):
    return jnp.concatenate(
        [lax.dynamic_slice_in_dim(stack, order[at], 1) for at in range(count)]
    )


def straighten(pieces, device):
    merged = []
    for which in range(2):
        mine = [member for member in pieces if member[1] == which]
        places = sum((member[0] for member in mine), [])
        block = jnp.concatenate([member[2] for member in mine])
        order = sorted(range(len(places)), key=lambda at: places[at])
        block = pick(jnp.stack([block[at] for at in order]), device ^ jnp.arange(len(places)), len(places))
        count, groups, rows, lanes = block.shape
        block = block.transpose(1, 0, 2, 3).reshape(1, groups, count * rows, lanes)
        merged.append(([0], which, block))
    return merged


def places_of(order):
    places = [0]
    for bit in reversed(order):
        places = places + [place | bit for place in places]
    return places


def add(left, right):
    return (left.astype(FULL) + right.astype(FULL)).astype(LOW)


def reduce_dp(keep, send, order, early):
    got = tie(swap(send, 1), *early)
    for bit in order:
        half = keep.shape[0] // 2
        out = swap(add(keep[half:], got[half:]), bit)
        keep, got = add(keep[:half], got[:half]), out
    return keep[0], got[0]


def adam(state, grad, factor):
    clipped = grad * factor
    first = beta_one * state[1] + (1.0 - beta_one) * clipped
    second = beta_two * state[2] + (1.0 - beta_two) * clipped * clipped
    fixed_first = first / (1.0 - beta_one**adam_step)
    fixed_second = second / (1.0 - beta_two**adam_step)
    master = state[0] - rate * (
        fixed_first / (jnp.sqrt(fixed_second) + adam_eps) + decay * state[0]
    )
    return (master, first, second)


def shards(
    tokens,
    cotangent,
    counts,
    attend_in,
    attend_out,
    expand_in,
    expand_bias,
    expand_out,
    affine_state,
    position_state,
):
    shards_dp, groups = lax.axis_size("dp"), lax.axis_size("mp")
    device, mine = lax.axis_index("dp"), lax.axis_index("mp")
    width = tokens.shape[1]
    slots = counts.size // groups
    piece = width // shards_dp
    share = attend_out.shape[2]
    before = (mine - jnp.arange(groups)) % groups
    info = jnp.concatenate(
        [
            lax.dynamic_slice_in_dim(counts.reshape(-1), mine * slots, slots),
            before,
            device ^ jnp.arange(shards_dp),
        ]
    ).astype(jnp.int32)
    bits = bits_of(shards_dp)
    lists = (places_of(bits), places_of(bits[::-1]))
    mp_at, dp_at = slots, slots + groups

    heads_block = heads_block_of(info, attend_in, expand_bias, affine_state, position_state)
    up_block = units_block_of(info, 0, (expand_in,))
    units_block = units_block_of(info, 0, (expand_out, attend_out))
    second_block = units_block_of(info, 1, (attend_in, expand_in, expand_out, attend_out))
    units_all = lax.all_gather(units_block, ("mp", "dp"), axis=0)
    units_all = units_all.reshape(groups, shards_dp, -1, width)
    heads_ring = around(heads_block)
    heads_pieces, heads_got = gather(heads_ring, [])
    second_all = lax.all_gather(second_block, "dp", axis=0)

    step, low_share = padded(piece), padded(share)
    up_ring = around(tie(up_block, *heads_ring[1:]))
    units_sections = [(0, piece), (step, low_share)]
    units = [units_all] * 2
    sections = [(0, piece), (3 * step, low_share), (step, piece), (2 * step, piece)]
    weights = [second_all] * 4
    load_info = info
    if piece % 16:
        heads_pieces = straighten(heads_pieces, device)
        load_info = info.at[dp_at].set(0)
        units = [
            units_all[:, :, base : base + rows].reshape(groups, 1, shards_dp * rows, width)
            for base, rows in units_sections
        ]
        weights = [
            second_all[:, base : base + rows].reshape(1, shards_dp * rows, width)
            for base, rows in sections
        ]
        units_sections = [(0, shards_dp * rows) for _, rows in units_sections]
        sections = [(0, shards_dp * rows) for _, rows in sections]

    def plan_of(pieces, rows):
        places = [(member[0], member[1]) for member in pieces]
        return Plan(groups, places, rows, mp_at, dp_at, shards_dp)

    heads_plan = plan_of(heads_pieces, heads_pieces[0][2].shape[2])
    own_plan = plan_of([], piece)
    heads_pieces = [member[2] for member in heads_pieces]

    triple, context, chances, w_in, affine_one, affine_two, position, b_up = attend_forward(
        heads_plan, load_info, tokens, heads_pieces
    )
    up_pieces, _ = gather(up_ring, heads_got[-1:], (b_up,))
    if piece % 16:
        up_pieces = straighten([(p, w, b[:, :, :piece]) for p, w, b in up_pieces], device)
    up_plan = plan_of(up_pieces, up_pieces[0][2].shape[2])
    up_pieces = [member[2] for member in up_pieces]
    resid, hid_low, expanded, resid_two, first, tops, w_out = feed_forward(
        up_plan, units_sections, load_info, tokens, context, affine_one, b_up, up_pieces, units
    )

    keep_heads = (counts > 0).astype(FULL)
    live = jnp.concatenate([keep_heads, keep_heads], axis=1)
    keep_heads = keep_heads.reshape(-1, 1)
    top_grad = cotangent.reshape(-1, SEG, width)[:, 0].astype(FULL) * keep_heads
    tops_ring = around(tops)
    second, back_heads, heads_ring, sums_two, bias_two, saved = second_layer(
        sections, own_plan, info, tops_ring, position, live, top_grad, affine_two, affine_one, weights
    )
    out_rows = lax.all_gather(first, "mp", axis=0, tiled=True)
    grad_resid, active, grad_exp, grad_ret, grad_mixed, sums_one, bias, grad_heads = feed_backward(
        up_plan,
        units_sections,
        load_info,
        cotangent,
        back_heads,
        heads_ring,
        resid_two,
        expanded,
        resid,
        affine_one,
        up_pieces,
        units,
    )
    small = (sums_one, sums_two, grad_heads, bias, bias_two)
    unit_out = unit_grads(
        own_plan,
        info,
        active,
        grad_ret,
        hid_low,
        grad_exp,
        context,
        grad_mixed,
        small,
        saved,
    )
    unit_terms = lax.psum_scatter(unit_out, "dp", scatter_dimension=0)
    grad_in, grad_triple = attend_backward(
        info, grad_resid, grad_mixed, triple, chances, context, w_out, w_in, unit_out
    )
    merged = place_tops(info, second * keep_heads, out_rows)
    keep_a, send_a, keep_b, send_b = head_grads(own_plan, lists, tie(info, merged), tokens, grad_triple, unit_out)

    grad_line = [(onward(grad_in, 1), onward(grad_in, -1))]
    left_a, right_a = reduce_dp(keep_a, send_a, bits, grad_line[0])
    left_b, right_b = reduce_dp(keep_b, send_b, bits[::-1], grad_line[0])
    terms = [(left_a[s], right_a[s]) for s in range(1, groups // 2)]
    terms += [(left_b[s], right_b[s]) for s in range(groups - groups // 2)]
    last = tie(grad_line[0], keep_a)
    grad_line.append((onward(last[0], 1), onward(last[1], -1)))
    head_ring = [
        ahead(tie(add(*term), *grad_line[1]), -at - 1) for at, term in enumerate(terms)
    ]
    unit_ring = [
        ahead(tie(unit_terms[at, : unit_rows(own_plan, width)], *grad_line[1]), -at)
        for at in range(1, groups)
    ]
    unit_sum, head_sum, second_sum, squares = collect(
        own_plan, info, unit_terms, unit_ring, (left_a, right_a), head_ring
    )
    squares = all_sum(squares, ("mp",))
    last = tie(grad_line[1], squares)
    grad_line.append((onward(last[0], 1), onward(last[1], -1)))
    squares = all_sum(squares, ("dp",))
    input_grad = spread_out(
        groups,
        mp_at,
        info,
        [grad_in, *grad_line[0], *grad_line[1]],
        (0, -1, 1, -2, 2),
        grad_line[1][0],
    )
    input_grad = spread_out(groups, mp_at, info, grad_line[2], (-3, 3), input_grad)
    states = (
        attend_in,
        attend_out,
        expand_in,
        expand_bias,
        expand_out,
        affine_state,
        position_state,
    )
    assert groups == 4
    *updated, norm = update(own_plan, info, squares, unit_sum, head_sum, second_sum, states)
    return (merged, input_grad, norm[0, 0], *updated)


def solution(mesh):
    in_specs = (
        P("dp", None),
        P("dp", None),
        P("dp", None),
        P(None, None, "dp", "mp"),
        P(None, None, ("mp", "dp"), None),
        P(None, None, "dp", "mp"),
        P(None, None, ("mp", "dp")),
        P(None, None, ("mp", "dp"), None),
        P(None, None, None, "dp"),
        P(None, None, "dp"),
    )
    out_specs = (
        P("dp", None),
        P("dp", None),
        P(),
        P(None, "dp", "mp"),
        P(None, ("mp", "dp"), None),
        P(None, "dp", "mp"),
        P(None, ("mp", "dp")),
        P(None, ("mp", "dp"), None),
        P(None, None, "dp"),
        P(None, "dp"),
        P(None, "dp", "mp"),
        P(None, ("mp", "dp"), None),
        P(None, "dp", "mp"),
        P(None, ("mp", "dp")),
        P(None, ("mp", "dp"), None),
        P(None, None, "dp"),
        P(None, "dp"),
        P(None, "dp", "mp"),
        P(None, ("mp", "dp"), None),
        P(None, "dp", "mp"),
        P(None, ("mp", "dp")),
        P(None, ("mp", "dp"), None),
        P(None, None, "dp"),
        P(None, "dp"),
    )
    return jax.shard_map(shards, mesh=mesh, in_specs=in_specs, out_specs=out_specs, check_vma=False)
```

```python
import functools

import jax
import jax.numpy as jnp
from jax import lax
from jax.experimental import pallas as pl
from jax.experimental.pallas import tpu as pltpu
from jax.sharding import PartitionSpec as P

LOW = jnp.bfloat16
FULL = jnp.float32
HEAD_DIM = 64
SEG = 128
NSEG = 32
norm_eps = 1e-05
clip_level = 1.0
rate = 0.02
decay = 0.01
beta_one = 0.9
beta_two = 0.999
adam_eps = 1e-08
adam_step = 10
LANES = 2 * HEAD_DIM
TANH_A = 0.7978845608028654
TANH_B = 0.044715
VMEM_BYTES = 60 * 1024 * 1024
FLOPS = 1.15e9


def dot_nn(a, b):
    return lax.dot_general(a, b, (((1,), (0,)), ((), ())), preferred_element_type=FULL)


def dot_nt(a, b):
    return lax.dot_general(a, b, (((1,), (1,)), ((), ())), preferred_element_type=FULL)


def dot_tn(a, b):
    return lax.dot_general(a, b, (((0,), (0,)), ((), ())), preferred_element_type=FULL)


def normal(values):
    mean = jnp.mean(values, axis=-1, keepdims=True)
    centred = values - mean
    spread = jnp.mean(centred * centred, axis=-1, keepdims=True)
    scale = lax.rsqrt(spread + norm_eps)
    return centred * scale, scale


def normal_back(grad, unit, scale, gain):
    scaled = grad * gain
    one = jnp.mean(scaled, axis=-1, keepdims=True)
    two = jnp.mean(scaled * unit, axis=-1, keepdims=True)
    return scale * (scaled - one - unit * two)


def halves(block, low):
    zero = jnp.zeros_like(block)
    return jnp.concatenate([jnp.where(low, block, zero), jnp.where(low, zero, block)], axis=0)


def soft(query, keys, live, span):
    scores = jnp.where(live, dot_nt(query, keys), -1e30)
    parts = []
    for half in range(2):
        piece = scores[:, half * span : (half + 1) * span]
        weights = jnp.exp(piece - jnp.max(piece, axis=-1, keepdims=True))
        parts.append(weights * (1.0 / jnp.sum(weights, axis=-1, keepdims=True)))
    return parts


class Plan:
    def __init__(self, groups, pieces, rows, mp_at, dp_at, count=1):
        self.groups, self.pieces, self.rows = groups, pieces, rows
        self.mp_at, self.dp_at = mp_at, dp_at
        self.count = count

    def copies(self):
        return sum(len(places) for places, _ in self.pieces) * (self.groups // 2)


def fetch(plan, info, pieces, land, sems, begin=True):
    size = plan.rows
    copies = []
    for (places, half), piece in zip(plan.pieces, pieces):
        for at, place in enumerate(places):
            start = pl.multiple_of(info[plan.dp_at + place] * size, 16)
            for inner in range(piece.shape[1]):
                copy = pltpu.make_async_copy(
                    piece.at[at, inner],
                    land(half * piece.shape[1] + inner, start, size),
                    sems.at[len(copies)],
                )
                if begin:
                    copy.start()
                copies.append(copy)
    return copies


def padded(count):
    return -(-count // 16) * 16


def wait_all(copies):
    for copy in copies:
        copy.wait()


def turn(block):
    return jnp.concatenate([block[:, HEAD_DIM:], block[:, :HEAD_DIM]], axis=1)


def fetch_units(plan, section, info, pieces, down_all, w_up, w_down, sems, begin=True):
    width = w_down.shape[1]
    base, size = section

    def up(m, start, rows):
        place = pl.multiple_of(info[plan.mp_at + m] * width, LANES)
        return w_up.at[pl.ds(start, rows), pl.ds(place, width)]

    ups = fetch(plan, info, pieces, up, sems.at[0], begin)
    copies = []
    for m in range(down_all.shape[0]):
        for at in range(down_all.shape[1]):
            copy = pltpu.make_async_copy(
                down_all.at[m, at, pl.ds(base, size), :],
                w_down.at[pl.ds(m * width + at * size, size), :],
                sems.at[1, m * down_all.shape[1] + at],
            )
            if begin:
                copy.start()
            copies.append(copy)
    return ups, copies


def fetch_out(section, plan, info, out_all, stage, sems):
    base, size = section
    copies = []
    for m in range(plan.groups):
        for at in range(out_all.shape[1]):
            copy = pltpu.make_async_copy(
                out_all.at[info[plan.mp_at + m], at, pl.ds(base, size), :],
                stage.at[m, pl.ds(at * size, size), :],
                sems.at[len(copies)],
            )
            copy.start()
            copies.append(copy)
    return copies


def pair_columns(stage, w_in):
    groups, width = stage.shape[:2]
    low = lax.broadcasted_iota(jnp.int32, (width, LANES), 1) < HEAD_DIM
    for part in range(3):
        base = part * width
        for m in range(groups):
            at = base + m * LANES
            w_in[:, at : at + LANES] = stage[m, :, part * LANES : (part + 1) * LANES]
        for m in range(0, groups, 2):
            at = base + (groups + m // 2) * LANES
            source = slice(3 * LANES, 4 * LANES) if part < 2 else slice(4 * LANES, 5 * LANES)
            left, right = stage[m, :, source], stage[m + 1, :, source]
            if part == 1:
                left = turn(left)
            else:
                right = turn(right)
            w_in[:, at : at + LANES] = jnp.where(low, left, right)


def pair_rows(stage, w_out, count):
    groups, rows = stage.shape[:2]
    share = w_out.shape[0] // groups // count
    step = rows // count
    for m in range(groups):
        parts = [stage[m, at * step : (at + 1) * step, :].astype(FULL)[:share] for at in range(count)]
        found = jnp.concatenate(parts, axis=0).astype(LOW)
        w_out[m * LANES : (m + 1) * LANES, :] = found[:LANES]
        goal = groups * LANES + m * HEAD_DIM
        w_out[goal : goal + HEAD_DIM, :] = found[LANES:]


def columns_of(block):
    at = [block[:, i * HEAD_DIM : (i + 1) * HEAD_DIM] for i in range(9)]
    order = ((0, 3), (1, 4), (2, 5), (6, 7))
    return [jnp.concatenate([at[i], at[j]], axis=1) for i, j in order] + [at[8]]


def heads_block_kernel(info, attend_in, bias, affine, position, out, small):
    rows = attend_in.shape[2]
    small[...] = jnp.zeros_like(small)
    small[0:6, :rows] = affine[0, 0]
    small[6:8, :rows] = bias[0]
    small[8:14, :rows] = affine[0, 1]
    small[16 : 16 + NSEG, :rows] = position[0]
    blocks = columns_of(attend_in[0, 0])
    blocks[4] = jnp.concatenate([blocks[4], small[...].T[:rows, :HEAD_DIM]], axis=1)
    for at, block in enumerate(blocks):
        out[:, at * LANES : (at + 1) * LANES] = block.astype(LOW)


def units_block_kernel(info, *refs):
    ins, out = refs[:-1], refs[-1]
    start = 0
    for source in ins:
        block = source[0, 0]
        rows = block.shape[0]
        if block.shape[1] != out.shape[1]:
            blocks = columns_of(block)
            blocks[4] = jnp.concatenate([blocks[4], jnp.zeros((rows, HEAD_DIM), FULL)], axis=1)
            blocks.append(jnp.zeros((rows, LANES), FULL))
            block = jnp.concatenate(blocks, axis=1)
        if padded(rows) > rows:
            block = jnp.concatenate([block, jnp.zeros((padded(rows) - rows, out.shape[1]), FULL)], axis=0)
        out[start : start + padded(rows), :] = block.astype(LOW)
        start += padded(rows)


def attend_kernel(plan, info, tok, *refs):
    pieces, refs = refs[:-10], refs[-10:]
    triple, context, chances, w_in, affine_one, affine_two, position, b_up, stage, sems = refs
    step = pl.program_id(0)
    rows, width = tok.shape

    @pl.when(step == 0)
    def _():
        def land(m, start, size):
            return stage.at[m, pl.ds(start, size), :]

        wait_all(fetch(plan, info, pieces, land, sems))
        for m in range(plan.groups):
            small = stage[m, :, 4 * LANES : 5 * LANES].astype(FULL).T
            place = pl.multiple_of(info[plan.mp_at + m] * width, LANES)
            b_up[:, pl.ds(place, width)] = small[HEAD_DIM + 6 : HEAD_DIM + 7]
            if m == 0:
                affine_one[...] = small[HEAD_DIM : HEAD_DIM + 8]
                affine_two[...] = small[HEAD_DIM + 8 : HEAD_DIM + 16]
                position[...] = small[HEAD_DIM + 16 : HEAD_DIM + 16 + NSEG]
        pair_columns(stage, w_in)

    triple[...] = dot_nn(tok[...], w_in[...]).astype(LOW)
    low = lax.broadcasted_iota(jnp.int32, (SEG, LANES), 1) < HEAD_DIM
    spot = lax.broadcasted_iota(jnp.int32, (SEG, 2 * SEG), 1) % SEG
    for seg in range(rows // SEG):
        live = spot < info[step * (rows // SEG) + seg]
        here = slice(seg * SEG, (seg + 1) * SEG)
        for pair in range(width // LANES):
            at = pair * LANES
            query = triple[here, at : at + LANES] * LOW(HEAD_DIM ** (-0.5))
            keys = halves(triple[here, width + at : width + at + LANES], low)
            values = halves(triple[here, 2 * width + at : 2 * width + at + LANES], low)
            probs = jnp.concatenate([part.astype(LOW) for part in soft(query, keys, live, SEG)], axis=1)
            chances[here, 2 * at : 2 * at + 2 * SEG] = probs
            context[here, at : at + LANES] = dot_nn(probs, values).astype(LOW)


def feed_kernel(plan, sections, info, tok, context, affine, b_up, down_all, out_all, *refs):
    pieces, refs = refs[: len(plan.pieces)], refs[len(plan.pieces) :]
    resid, hid_low, expanded, resid_two, first, tops, w_out, w_up, w_down, stage, sems, out_sems = refs
    step = pl.program_id(0)
    rows, width = tok.shape
    segs = rows // SEG

    @pl.when(step == 0)
    def _():
        outs = fetch_out(sections[1], plan, info, out_all, stage, out_sems)
        fetch_units(plan, sections[0], info, pieces, down_all, w_up, w_down, sems)
        wait_all(outs)
        pair_rows(stage, w_out, plan.count)

    mixed = dot_nn(context[...], w_out[...])
    value = tok[...].astype(FULL) + mixed + affine[4:5, :]
    resid[...] = value
    hidden = normal(value)[0] * affine[0:1, :] + affine[1:2, :]
    low = hidden.astype(LOW)
    hid_low[...] = low
    total = hidden + affine[5:6, :]
    units = w_up.shape[1]
    block = width

    @pl.when(step == 0)
    def _():
        ups, downs = fetch_units(plan, sections[0], info, pieces, down_all, w_up, w_down, sems, False)
        wait_all(ups)
        wait_all(downs)

    for at in range(0, units, block):
        up = dot_nn(low, w_up[:, at : at + block]) + b_up[:, at : at + block]
        expanded[:, at : at + block] = up.astype(LOW)
        curve = jnp.tanh(TANH_A * (up + TANH_B * up * up * up))
        active = (0.5 * up * (1.0 + curve)).astype(LOW)
        total = total + dot_nn(active, w_down[at : at + block, :])
    resid_two[...] = total
    result = normal(total)[0] * affine[2:3, :] + affine[3:4, :]
    row = lax.broadcasted_iota(jnp.int32, (SEG, 1), 0)
    for seg in range(segs):
        piece = result[seg * SEG : (seg + 1) * SEG, :]
        kept = jnp.where(row < info[step * segs + seg], piece, 0.0)
        first[seg * SEG : (seg + 1) * SEG, :] = kept.astype(LOW)
        tops[pl.ds(step * segs + seg, 1), :] = piece[0:1, :]


def feed_back_kernel(plan, sections, info, cot, back_heads, resid_two, expanded, resid, affine, *refs):
    ring, refs = refs[: plan.groups], refs[plan.groups :]
    pieces, refs = refs[: len(plan.pieces)], refs[len(plan.pieces) :]
    down_all, grad_resid, active, grad_exp, grad_ret, grad_mixed, sums, bias = refs[:8]
    heads, w_up, w_down, sems = refs[8:]
    step = pl.program_id(0)
    rows, width = cot.shape
    segs = rows // SEG

    @pl.when(step == 0)
    def _():
        fetch_units(plan, sections[0], info, pieces, down_all, w_up, w_down, sems)
        total = back_heads[...]
        for member in ring:
            total = total + member[...].astype(FULL)
        heads[...] = total

    row = lax.broadcasted_iota(jnp.int32, (SEG, 1), 0)
    first = info[plan.mp_at] * (pl.num_programs(0) * segs) + step * segs
    blocks = []
    for seg in range(segs):
        piece = cot[seg * SEG : (seg + 1) * SEG, :].astype(FULL)
        piece = jnp.where(row < info[step * segs + seg], piece, 0.0)
        blocks.append(jnp.where(row == 0, heads[pl.ds(first + seg, 1), :], piece))
    grad = jnp.concatenate(blocks, axis=0)
    unit, scale = normal(resid_two[...])

    @pl.when(step == 0)
    def _():
        sums[...] = jnp.zeros_like(sums)
        bias[...] = jnp.zeros_like(bias)

    back = normal_back(grad, unit, scale, affine[2:3, :])
    sums[2:3, :] += jnp.sum(grad * unit, axis=0, keepdims=True)
    sums[3:4, :] += jnp.sum(grad, axis=0, keepdims=True)
    sums[5:6, :] += jnp.sum(back, axis=0, keepdims=True)
    low = back.astype(LOW)
    grad_ret[...] = low
    units = w_up.shape[1]
    total = back
    block = width

    @pl.when(step == 0)
    def _():
        ups, downs = fetch_units(plan, sections[0], info, pieces, down_all, w_up, w_down, sems, False)
        wait_all(downs)
        wait_all(ups)

    for at in range(0, units, block):
        grad_act = dot_nt(low, w_down[at : at + block, :])
        up = expanded[:, at : at + block].astype(FULL)
        square = up * up
        curve = jnp.tanh(TANH_A * (up + TANH_B * up * square))
        half = 0.5 * (1.0 + curve)
        active[:, at : at + block] = (up * half).astype(LOW)
        slope = half + 0.5 * up * (1.0 - curve * curve) * (TANH_A + 3.0 * TANH_A * TANH_B * square)
        wide = slope * grad_act
        bias[:, at : at + block] += jnp.sum(wide, axis=0, keepdims=True)
        short = wide.astype(LOW)
        grad_exp[:, at : at + block] = short
        total = total + dot_nt(short, w_up[:, at : at + block])
    unit, scale = normal(resid[...])
    back = normal_back(total, unit, scale, affine[0:1, :])
    sums[0:1, :] += jnp.sum(total * unit, axis=0, keepdims=True)
    sums[1:2, :] += jnp.sum(total, axis=0, keepdims=True)
    sums[4:5, :] += jnp.sum(back, axis=0, keepdims=True)
    grad_resid[...] = back
    grad_mixed[...] = back.astype(LOW)


def pair_back(query, keys, values, probs, down, low, span):
    grad_probs = dot_nt(down, values)
    scores = []
    for half in range(2):
        mine = probs[half]
        given = grad_probs[:, half * span : (half + 1) * span]
        product = mine * given
        inner = jnp.sum(product, axis=-1, keepdims=True)
        scores.append((product - mine * inner).astype(LOW))
    grad_scores = jnp.concatenate(scores, axis=1)
    probs = jnp.concatenate([part.astype(LOW) for part in probs], axis=1)
    grad_query = dot_nn(grad_scores, keys) * HEAD_DIM ** (-0.5)
    both = dot_tn(grad_scores, query)
    grad_key = jnp.where(low, both[:span], both[span:])
    both = dot_tn(probs, down)
    return grad_query, grad_key, jnp.where(low, both[:span], both[span:])


def attend_back_kernel(info, grad_resid, grad_mixed, triple, chances, context, w_out, w_in, early, grad_in, grad_triple, grad_ctx):
    del early
    rows, width = grad_resid.shape
    grad_ctx[...] = dot_nt(grad_mixed[...], w_out[...]).astype(LOW)
    low = lax.broadcasted_iota(jnp.int32, (SEG, LANES), 1) < HEAD_DIM
    for seg in range(rows // SEG):
        here = slice(seg * SEG, (seg + 1) * SEG)
        for pair in range(width // LANES):
            at = pair * LANES
            query = triple[here, at : at + LANES] * LOW(HEAD_DIM ** (-0.5))
            keys = halves(triple[here, width + at : width + at + LANES], low)
            values = halves(triple[here, 2 * width + at : 2 * width + at + LANES], low)
            probs = chances[here, 2 * at : 2 * at + 2 * SEG]
            down = grad_ctx[here, at : at + LANES]
            product = down.astype(FULL) * context[here, at : at + LANES].astype(FULL)
            left = jnp.sum(jnp.where(low, product, 0.0), axis=-1, keepdims=True)
            right = jnp.sum(jnp.where(low, 0.0, product), axis=-1, keepdims=True)
            grad_probs = dot_nt(down, values)
            scores = [grad_probs[:, :SEG] - left, grad_probs[:, SEG:] - right]
            grad_scores = (probs.astype(FULL) * jnp.concatenate(scores, axis=1)).astype(LOW)
            grad_query = dot_nn(grad_scores, keys) * HEAD_DIM ** (-0.5)
            both = dot_tn(grad_scores, query)
            grad_key = jnp.where(low, both[:SEG], both[SEG:])
            both = dot_tn(probs, down)
            grad_value = jnp.where(low, both[:SEG], both[SEG:])
            for part, found in enumerate((grad_query, grad_key, grad_value)):
                goal = part * width + at
                grad_triple[here, goal : goal + LANES] = found.astype(LOW)
    grad_in[...] = (grad_resid[...] + dot_nt(grad_triple[...], w_in[...])).astype(LOW)


def unit_grad_kernel(
    plan, info, active, grad_ret, hid_low, grad_exp, context, grad_mixed, sums_one, sums_two, grad_heads, bias, bias_two, *refs
):
    saved, (out, whole, mixing, small, second) = refs[:-5], refs[-5:]
    m = pl.program_id(0)
    extra = second.shape[1] // plan.groups
    rest_at = out.shape[2] - extra
    size = plan.rows
    width = whole.shape[0]
    third = width // plan.groups
    share = third // out.shape[0]

    @pl.when(m == 0)
    def _():
        second_grads_into(plan, *saved, second)
        found = dot_tn(context[...], grad_mixed[...])
        for at in range(plan.groups):
            mixing[at * third : at * third + LANES, :] = found[at * LANES : (at + 1) * LANES]
            goal = plan.groups * LANES + at * HEAD_DIM
            mixing[at * third + LANES : (at + 1) * third, :] = found[goal : goal + HEAD_DIM]

    part = pl.ds(pl.multiple_of(m * extra, 16), extra)
    for at in range(out.shape[0]):
        out[at, 0, rest_at:, :] = second[at, part, :]
    step = padded(size)
    for kind, (left, right) in enumerate(((active, grad_ret), (hid_low, grad_exp))):
        whole[...] = dot_tn(left[...], right[...])
        for at in range(out.shape[0]):
            out[at, 0, kind * step : kind * step + size, :] = whole[
                at * size : (at + 1) * size, :
            ].astype(LOW)
    leader = jnp.where(info[plan.mp_at] == 0, 1.0, 0.0)
    row = lax.broadcasted_iota(jnp.int32, (8, 1), 0)
    place = pl.multiple_of(info[plan.mp_at + m] * width, LANES)
    own = jnp.where(m == 0, 1.0, 0.0)
    biases = jnp.where(row == 6, bias[:, pl.ds(place, width)], bias_two[...] * own)
    small[0:8, :] = jnp.where(row < 6, sums_one[...], biases)
    small[8:16, :] = sums_two[...] * leader
    position = grad_heads[0:NSEG, :]
    for doc in range(1, grad_heads.shape[0] // NSEG):
        position = position + grad_heads[doc * NSEG : (doc + 1) * NSEG, :]
    small[16:, :] = position * leader
    gap = jnp.zeros((8, LANES - size), FULL)
    mine = mixing[pl.ds(pl.multiple_of(m * third, HEAD_DIM), third), :]
    for at in range(out.shape[0]):
        lines = small[:, at * size : (at + 1) * size]
        blocks = []
        for block in range(width // LANES):
            blocks += [lines[block * 8 : (block + 1) * 8], gap]
        rows = [jnp.concatenate(blocks, axis=1), mine[at * share : (at + 1) * share]]
        rest = rest_at - 2 * step - share - 8
        if rest:
            rows.append(jnp.zeros((rest, width), FULL))
        out[at, 0, 2 * step : rest_at, :] = jnp.concatenate(rows, axis=0).astype(LOW)


def head_grad_kernel(plan, lists, info, tok, grad_triple, early, keep_a, send_a, keep_b, send_b, whole):
    del early
    size = plan.rows
    width = tok.shape[1]
    whole[...] = dot_tn(tok[...], grad_triple[...])
    low = lax.broadcasted_iota(jnp.int32, (size, LANES), 1) < HEAD_DIM
    for half, (keep, send) in enumerate(((keep_a, send_a), (keep_b, send_b))):
        for at, place in enumerate(lists[half]):
            for out, which in ((keep, place), (send, place ^ 1)):
                start = pl.multiple_of(info[plan.dp_at + which] * size, 8)
                for inner in range(plan.groups // 2):
                    m = half * (plan.groups // 2) + inner
                    for part in range(3):
                        goal = part * width + m * LANES
                        out[at, inner, :, part * LANES : (part + 1) * LANES] = whole[
                            pl.ds(start, size), goal : goal + LANES
                        ].astype(LOW)
                    blocks = []
                    for part in range(3):
                        goal = part * width + (plan.groups + m // 2) * LANES
                        blocks.append(whole[pl.ds(start, size), goal : goal + LANES])
                    if m % 2 == 0:
                        blocks = [blocks[0], turn(blocks[1]), blocks[2]]
                    else:
                        blocks = [turn(blocks[0]), blocks[1], turn(blocks[2])]
                    out[at, inner, :, 3 * LANES : 4 * LANES] = jnp.where(low, blocks[0], blocks[1]).astype(LOW)
                    out[at, inner, :, 4 * LANES : 5 * LANES] = jnp.where(low, blocks[2], 0.0).astype(LOW)


def tops_kernel(info, tops, rows, out, held, in_sems, out_sems):
    row = lax.broadcasted_iota(jnp.int32, (16, 1), 0)
    parts = in_sems.shape[0]
    segs = tops.shape[0] // parts
    ins, outs = [], []
    for part in range(parts):
        where = pl.ds(part * segs * SEG, segs * SEG)
        ins.append(pltpu.make_async_copy(rows.at[where, :], held.at[where, :], in_sems.at[part]))
        outs.append(pltpu.make_async_copy(held.at[where, :], out.at[where, :], out_sems.at[part]))
        ins[-1].start()
    for part in range(parts):
        ins[part].wait()
        for seg in range(part * segs, (part + 1) * segs):
            near = slice(seg * SEG, seg * SEG + 16)
            held[near, :] = jnp.where(row == 0, tops[seg : seg + 1, :].astype(LOW), held[near, :])
        outs[part].start()
    wait_all(outs)


def spread_kernel(groups, mp_at, steps, info, *refs):
    count = len(steps)
    line, (out, held, ready, in_sems, out_sems) = refs[:count], refs[-5:]
    rows = held.shape[1]
    mine = info[mp_at]

    def take(at, step, part):
        place = mine + step
        into = pltpu.make_async_copy(line[at], held.at[at], in_sems.at[at])
        goal = pl.ds(pl.multiple_of(place * rows, rows), rows)
        back = pltpu.make_async_copy(ready.at[at], out.at[goal, :], out_sems.at[at])

        @pl.when(jnp.logical_and(place >= 0, place < groups))
        def _():
            if part == 0:
                into.start()
            elif part == 2:
                back.wait()
            else:
                into.wait()
                ready[at] = held[at].astype(ready.dtype)
                back.start()

    for part in range(3):
        for at, step in enumerate(steps):
            take(at, step, part)


def rows_of(block, width):
    return pl.BlockSpec((block, width), lambda i, c: (i, 0))


def load_own(section, source, target, sems):
    base, size = section
    copies = []
    for at in range(source.shape[0]):
        copy = pltpu.make_async_copy(
            source.at[at, pl.ds(base, size), :], target.at[pl.ds(at * size, size), :], sems.at[at]
        )
        copy.start()
        copies.append(copy)
    return copies


def own_out(stage, w_out, count):
    share = (w_out.shape[0] - HEAD_DIM) // count
    step = stage.shape[0] // count
    parts = [stage[at * step : (at + 1) * step, :].astype(FULL)[:share] for at in range(count)]
    parts.append(jnp.zeros((HEAD_DIM, stage.shape[1]), FULL))
    w_out[...] = jnp.concatenate(parts, axis=0).astype(LOW)


def ring_sum(plan, info, ring, total):
    for at, member in enumerate(ring):
        total[info[plan.mp_at + at]] = member[...].astype(FULL)
    found = total[0]
    for at in range(1, plan.groups):
        found = found + total[at]
    return found


def own_pairs(triple, here, live, low):
    zero = jnp.zeros((NSEG, LANES), LOW)
    block = [triple[here, at * LANES : (at + 1) * LANES] for at in range(5)]
    last = turn(block[3].astype(FULL)).astype(LOW)
    found = []
    for query, key, value in (
        (block[0], block[1], block[2]),
        (jnp.where(low, block[3], zero), jnp.where(low, last, zero), jnp.where(low, block[4], zero)),
    ):
        query = query * LOW(HEAD_DIM ** (-0.5))
        keys, values = halves(key, low), halves(value, low)
        found.append((query, keys, values, soft(query, keys, live, NSEG)))
    return found


def second_one_kernel(plan, sections, info, *refs):
    ring, refs = refs[: plan.groups], refs[plan.groups :]
    position, live, in_all, out_all, term, entry, tok, triple, context = refs[:9]
    heads, w_in, w_out, stage, sems = refs[9:]
    rows = entry.shape[0]
    copies = load_own(sections[0], in_all, w_in, sems.at[0])
    outs = load_own(sections[1], out_all, stage, sems.at[1])
    slots = ring[0].shape[0]
    for at in range(plan.groups):
        goal = pl.multiple_of(info[plan.mp_at + at] * slots, slots)
        heads[pl.ds(goal, slots), :] = ring[at][...]
    docs = rows // NSEG
    entry[...] = heads[...] + jnp.concatenate([position[...]] * docs, axis=0)
    tok[...] = entry[...].astype(LOW)
    wait_all(copies)
    triple[...] = dot_nn(tok[...], w_in[:, : 5 * LANES]).astype(LOW)
    low = lax.broadcasted_iota(jnp.int32, (NSEG, LANES), 1) < HEAD_DIM
    for doc in range(docs):
        here = slice(doc * NSEG, (doc + 1) * NSEG)
        mask = live[doc : doc + 1, :] > 0.5
        for pair, (_, _, values, probs) in enumerate(own_pairs(triple, here, mask, low)):
            probs = jnp.concatenate([part.astype(LOW) for part in probs], axis=1)
            context[here, pair * LANES : (pair + 1) * LANES] = dot_nn(probs, values).astype(LOW)
    wait_all(outs)
    own_out(stage, w_out, plan.count)
    term[...] = dot_nn(context[...], w_out[...]).astype(LOW)


def second_two_kernel(plan, sections, info, *refs):
    ring, refs = refs[: plan.groups], refs[plan.groups :]
    entry, affine, b_up, up_all, down_all, term, resid, hid_low, expanded, active = refs[:10]
    total, w_up, w_down, sems = refs[10:]
    copies = load_own(sections[2], up_all, w_up, sems.at[0])
    downs = load_own(sections[3], down_all, w_down, sems.at[1])
    value = entry[...] + ring_sum(plan, info, ring, total) + affine[4:5, :]
    resid[...] = value
    hid_low[...] = (normal(value)[0] * affine[0:1, :] + affine[1:2, :]).astype(LOW)
    wait_all(copies)
    up = dot_nn(hid_low[...], w_up[...]) + b_up[7:8, :]
    expanded[...] = up
    active[...] = (0.5 * up * (1.0 + jnp.tanh(TANH_A * (up + TANH_B * up * up * up)))).astype(LOW)
    wait_all(downs)
    term[...] = dot_nn(active[...], w_down[...]).astype(LOW)


def second_three_kernel(plan, sections, info, *refs):
    ring, refs = refs[: plan.groups], refs[plan.groups :]
    resid, expanded, top_grad, affine, up_all, down_all = refs[:6]
    term, second, back_two, grad_ret, grad_exp, sums, bias = refs[6:13]
    total, w_up, w_down, sems = refs[13:]
    copies = load_own(sections[3], down_all, w_down, sems.at[0])
    ups = load_own(sections[2], up_all, w_up, sems.at[1])
    hidden = normal(resid[...])[0] * affine[0:1, :] + affine[1:2, :]
    unit, scale = normal(hidden + ring_sum(plan, info, ring, total) + affine[5:6, :])
    second[...] = unit * affine[2:3, :] + affine[3:4, :]
    grad = top_grad[...]
    back = normal_back(grad, unit, scale, affine[2:3, :])
    back_two[...] = back
    sums[...] = jnp.zeros_like(sums)
    sums[2:3, :] = jnp.sum(grad * unit, axis=0, keepdims=True)
    sums[3:4, :] = jnp.sum(grad, axis=0, keepdims=True)
    sums[5:6, :] = jnp.sum(back, axis=0, keepdims=True)
    grad_ret[...] = back.astype(LOW)
    wait_all(copies)
    given = dot_nt(grad_ret[...], w_down[...])
    up = expanded[...]
    square = up * up
    curve = jnp.tanh(TANH_A * (up + TANH_B * up * square))
    half = 0.5 * (1.0 + curve)
    slope = half + 0.5 * up * (1.0 - curve * curve) * (TANH_A + 3.0 * TANH_A * TANH_B * square)
    wide = slope * given
    bias[...] = jnp.sum(wide, axis=0, keepdims=True)
    grad_exp[...] = wide.astype(LOW)
    wait_all(ups)
    term[...] = dot_nt(grad_exp[...], w_up[...]).astype(LOW)


def second_four_kernel(plan, sections, info, *refs):
    ring, refs = refs[: plan.groups], refs[plan.groups :]
    resid, back_two, triple, live, sums_in, affine, in_all, out_all = refs[:8]
    term, back_one, grad_mixed, grad_triple, sums = refs[8:13]
    total, w_in, w_out, stage, sems = refs[13:]
    outs = load_own(sections[1], out_all, stage, sems.at[0])
    copies = load_own(sections[0], in_all, w_in, sems.at[1])
    rows = resid.shape[0]
    grad = back_two[...] + ring_sum(plan, info, ring, total)
    unit, scale = normal(resid[...])
    back = normal_back(grad, unit, scale, affine[0:1, :])
    back_one[...] = back
    sums[...] = sums_in[...]
    sums[0:1, :] = jnp.sum(grad * unit, axis=0, keepdims=True)
    sums[1:2, :] = jnp.sum(grad, axis=0, keepdims=True)
    sums[4:5, :] = jnp.sum(back, axis=0, keepdims=True)
    grad_mixed[...] = back.astype(LOW)
    wait_all(outs)
    own_out(stage, w_out, plan.count)
    grad_ctx = dot_nt(grad_mixed[...], w_out[...]).astype(LOW)
    low = lax.broadcasted_iota(jnp.int32, (NSEG, LANES), 1) < HEAD_DIM
    for doc in range(rows // NSEG):
        here = slice(doc * NSEG, (doc + 1) * NSEG)
        mask = live[doc : doc + 1, :] > 0.5
        found = []
        for pair, (query, keys, values, probs) in enumerate(own_pairs(triple, here, mask, low)):
            down = grad_ctx[here, pair * LANES : (pair + 1) * LANES]
            found.append(pair_back(query, keys, values, probs, down, low, NSEG))
        blocks = list(found[0])
        blocks.append(jnp.where(low, found[1][0], turn(found[1][1])))
        blocks.append(jnp.where(low, found[1][2], 0.0))
        for at, block in enumerate(blocks):
            grad_triple[here, at * LANES : (at + 1) * LANES] = block.astype(LOW)
    wait_all(copies)
    term[...] = dot_nt(grad_triple[...], w_in[:, : 5 * LANES]).astype(LOW)


def second_grads_into(plan, tok, grad_triple, context, grad_mixed, hid_low, grad_exp, active, grad_ret, out):
    width = tok.shape[1]
    count, size = plan.count, plan.rows
    step = padded(size)
    share = width // plan.groups // count
    for kind, (left, right) in enumerate(
        ((tok, grad_triple), (hid_low, grad_exp), (active, grad_ret))
    ):
        value = dot_tn(left[...], right[...])
        if kind == 0:
            value = jnp.concatenate([value, jnp.zeros((width, LANES), FULL)], axis=1)
        for at in range(count):
            out[at, kind * step : kind * step + size, :] = value[at * size : (at + 1) * size].astype(LOW)
    value = dot_tn(context[...], grad_mixed[...])
    rest = out.shape[1] - 3 * step - share
    for at in range(count):
        rows = [value[at * share : (at + 1) * share]]
        if rest:
            rows.append(jnp.zeros((rest, width), FULL))
        out[at, 3 * step :, :] = jnp.concatenate(rows, axis=0).astype(LOW)


def collect_kernel(plan, info, *refs):
    count = plan.groups - 1
    unit_own, unit_ring, refs = refs[0], refs[1 : plan.groups], refs[plan.groups :]
    left, right, head_ring, refs = refs[0], refs[1], refs[2 : 2 + count], refs[2 + count :]
    unit_sum, head_sum, second, squares, ends = refs
    tall = unit_sum.shape[0]
    extra = unit_own.shape[1] - tall
    for m in range(plan.groups):
        second[m * extra : (m + 1) * extra, :] = unit_own[m, tall:, :].astype(FULL)
    total = unit_own[0, :tall].astype(FULL)
    for member in unit_ring:
        total = total + member[...].astype(FULL)
    tail = slice(2 * padded(plan.rows), tall)
    ends[info[plan.mp_at]] = unit_own[0, tail].astype(FULL)
    for at, member in enumerate(unit_ring):
        ends[info[plan.mp_at + plan.groups - 1 - at]] = member[tail, :].astype(FULL)
    found = ends[0]
    for at in range(1, plan.groups):
        found = found + ends[at]
    total = jnp.concatenate([total[: 2 * padded(plan.rows)], found], axis=0)
    unit_sum[...] = total
    heads = left[0].astype(FULL) + right[0].astype(FULL)
    for member in head_ring:
        heads = heads + member[...].astype(FULL)
    head_sum[...] = heads
    leader = jnp.where(info[plan.mp_at] == 0, 1.0, 0.0)
    step = padded(plan.rows)
    row = lax.broadcasted_iota(jnp.int32, (8, total.shape[1]), 0)
    lane = lax.broadcasted_iota(jnp.int32, (8, total.shape[1]), 1)
    once = jnp.logical_and(row >= 6, lane < LANES)

    def square(value):
        return jnp.sum(jnp.sum(value * value, axis=0, keepdims=True), axis=1, keepdims=True)

    small = total[2 * step : 2 * step + 8]
    found = square(total[: 2 * step]) + square(total[2 * step + 8 :])
    found = found + square(jnp.where(once, small, small * leader))
    found = found + square(heads) + square(second[...])
    squares[...] = jnp.broadcast_to(found, squares.shape)


def update_kernel(plan, info, squares, unit_sum, head_sum, second, *refs):
    states, news, norm = refs[:7], refs[7:28], refs[28]
    total = squares[...]
    norm[...] = jnp.sqrt(total)
    factor = jnp.minimum(1.0, clip_level / jnp.sqrt(total[0:1, 0:1]))
    size, step = plan.rows, padded(plan.rows)
    share = states[1].shape[2]

    def put(kind, where, grad):
        state = states[kind]
        old = [state[(at, *where)] for at in range(3)]
        for at, value in enumerate(adam(old, grad, factor)):
            news[7 * at + kind][where] = value

    def columns(block):
        at = [block[:, i * HEAD_DIM : (i + 1) * HEAD_DIM] for i in range(9)]
        return jnp.concatenate([at[i] for i in (0, 2, 4, 1, 3, 5, 6, 7, 8)], axis=1)

    every = slice(None)
    put(0, (0, every, every), columns(head_sum[...]))
    put(0, (1, every, every), columns(second[:size, :]))
    put(1, (0, every, every), unit_sum[2 * step + 8 : 2 * step + 8 + share, :])
    put(1, (1, every, every), second[3 * step : 3 * step + share, :])
    put(2, (0, every, every), unit_sum[step : step + size, :])
    put(2, (1, every, every), second[step : step + size, :])
    put(4, (0, every, every), unit_sum[:size, :])
    put(4, (1, every, every), second[2 * step : 2 * step + size, :])
    small = unit_sum[2 * step : 2 * step + 8, :]
    put(3, (every, every), small[6:8, :size])
    put(5, (0, every, every), small[0:6, :size])
    put(5, (1, every, every), small[0:6, LANES : LANES + size])
    for block in range(NSEG // 8):
        goal = (block + 2) * LANES
        put(6, (slice(block * 8, (block + 1) * 8), every), small[:, goal : goal + size])


def own_rows(plan, rows, block, width):
    return pl.BlockSpec((block, width), lambda i, c: (c[plan.mp_at] * (rows // block) + i, 0))


WHOLE = pl.BlockSpec(memory_space=pltpu.VMEM)
OUTSIDE = pl.BlockSpec(memory_space=pl.ANY)


def shape(*dims, kind=LOW):
    return jax.ShapeDtypeStruct(dims, kind)


def run(kernel, steps, ins, outs, scratch, micros, info, args, aliases=None):
    return pl.pallas_call(
        kernel,
        grid_spec=pltpu.PrefetchScalarGridSpec(
            num_scalar_prefetch=1,
            grid=(steps,),
            in_specs=ins,
            out_specs=[spec for spec, _ in outs],
            scratch_shapes=scratch,
        ),
        out_shape=[kind for _, kind in outs],
        input_output_aliases=aliases or {},
        compiler_params=pltpu.CompilerParams(vmem_limit_bytes=VMEM_BYTES),
        cost_estimate=pl.CostEstimate(
            flops=int(micros * FLOPS), bytes_accessed=1024, transcendentals=0
        ),
    )(info, *args)


def layer_of(state, layer):
    return pl.BlockSpec((1, 1, *state.shape[2:]), lambda i, c: (0, layer, 0, 0))


def heads_block_of(info, attend_in, bias, affine, position):
    return run(
        heads_block_kernel,
        1,
        [layer_of(attend_in, 0), WHOLE, WHOLE, WHOLE],
        [(WHOLE, shape(attend_in.shape[2], 5 * LANES))],
        [pltpu.VMEM((LANES, LANES), FULL)],
        2,
        info,
        (attend_in, bias, affine, position),
    )[0]


def units_block_of(info, layer, states):
    rows = sum(padded(state.shape[2]) for state in states)
    return run(
        units_block_kernel,
        1,
        [layer_of(state, layer) for state in states],
        [(WHOLE, shape(rows, states[-1].shape[3]))],
        [],
        2,
        info,
        states,
    )[0]


def attend_forward(plan, info, tok, pieces, block=512):
    rows, width = tok.shape[0] // plan.groups, tok.shape[1]
    lanes = pieces[0].shape[-1]
    wide = rows_of(block, 3 * width)
    return run(
        functools.partial(attend_kernel, plan),
        rows // block,
        [own_rows(plan, rows, block, width)] + [OUTSIDE] * len(pieces),
        [
            (wide, shape(rows, 3 * width)),
            (rows_of(block, width), shape(rows, width)),
            (rows_of(block, 2 * width), shape(rows, 2 * width)),
            (WHOLE, shape(width, 3 * width)),
            (WHOLE, shape(8, width, kind=FULL)),
            (WHOLE, shape(8, width, kind=FULL)),
            (WHOLE, shape(NSEG, width, kind=FULL)),
            (WHOLE, shape(1, plan.groups * width, kind=FULL)),
        ],
        [
            pltpu.VMEM((plan.groups, width, lanes), LOW),
            pltpu.SemaphoreType.DMA((plan.copies(),)),
        ],
        18,
        info,
        (tok, *pieces),
    )


def feed_forward(plan, sections, info, tok, context, affine, b_up, pieces, weights, block=512):
    rows, width = context.shape
    units = b_up.shape[1]
    line = rows_of(block, width)
    downs = plan.groups * weights[0].shape[1]
    return run(
        functools.partial(feed_kernel, plan, sections),
        rows // block,
        [own_rows(plan, rows, block, width), line, WHOLE, WHOLE]
        + [OUTSIDE] * (2 + len(pieces)),
        [
            (line, shape(rows, width, kind=FULL)),
            (line, shape(rows, width)),
            (rows_of(block, units), shape(rows, units)),
            (line, shape(rows, width, kind=FULL)),
            (line, shape(rows, width)),
            (WHOLE, shape(rows // SEG, width, kind=FULL)),
            (WHOLE, shape(width, width)),
        ],
        [
            pltpu.VMEM((width, units), LOW),
            pltpu.VMEM((units, width), LOW),
            pltpu.VMEM((plan.groups, weights[1].shape[1] * sections[1][1], width), LOW),
            pltpu.SemaphoreType.DMA((2, max(downs, plan.copies()))),
            pltpu.SemaphoreType.DMA((downs,)),
        ],
        24,
        info,
        (tok, context, affine, b_up, *weights, *pieces),
    )


def feed_backward(plan, sections, info, cot, back_heads, ring, resid_two, expanded, resid, affine, pieces, weights, block=256):
    rows, width = resid.shape
    units = expanded.shape[1]
    line, wide = rows_of(block, width), rows_of(block, units)
    return run(
        functools.partial(feed_back_kernel, plan, sections),
        rows // block,
        [own_rows(plan, rows, block, width), WHOLE, line, wide, line, WHOLE]
        + [WHOLE] * plan.groups
        + [OUTSIDE] * (1 + len(pieces)),
        [
            (line, shape(rows, width, kind=FULL)),
            (wide, shape(rows, units)),
            (wide, shape(rows, units)),
            (line, shape(rows, width)),
            (line, shape(rows, width)),
            (WHOLE, shape(8, width, kind=FULL)),
            (WHOLE, shape(1, units, kind=FULL)),
            (WHOLE, shape(*back_heads.shape, kind=FULL)),
        ],
        [
            pltpu.VMEM((width, units), LOW),
            pltpu.VMEM((units, width), LOW),
            pltpu.SemaphoreType.DMA((2, max(plan.groups * weights[0].shape[1], plan.copies()))),
        ],
        28,
        info,
        (cot, back_heads, resid_two, expanded, resid, affine, *ring, *pieces, weights[0]),
    )


def attend_backward(info, grad_resid, grad_mixed, triple, chances, context, w_out, w_in, early, block=512):
    rows, width = grad_resid.shape
    line, wide = rows_of(block, width), rows_of(block, 3 * width)
    return run(
        attend_back_kernel,
        rows // block,
        [line, line, wide, rows_of(block, 2 * width), line, WHOLE, WHOLE, OUTSIDE],
        [(line, shape(rows, width)), (wide, shape(rows, 3 * width))],
        [pltpu.VMEM((block, width), LOW)],
        30,
        info,
        (grad_resid, grad_mixed, triple, chances, context, w_out, w_in, early),
    )


def second_run(kernel, plan, sections, info, ring, args, weights, outs, scratch):
    count = weights[0].shape[0]
    return run(
        functools.partial(kernel, plan, sections),
        1,
        [WHOLE] * (len(ring) + len(args)) + [OUTSIDE] * len(weights),
        [(WHOLE, kind) for kind in outs],
        scratch + [pltpu.SemaphoreType.DMA((2, count))],
        5,
        info,
        (*ring, *args, *weights),
    )


def second_layer(sections, plan, info, ring, position, live, top_grad, affine, b_up, weights):
    rows, width = top_grad.shape
    groups = plan.groups
    in_all, out_all, up_all, down_all = weights
    own = width // groups
    tall = out_all.shape[0] * sections[1][1]
    full, low = shape(rows, width, kind=FULL), shape(rows, width)
    mixed = shape(rows, 5 * LANES)
    total = pltpu.VMEM((groups, rows, width), FULL)
    square = pltpu.VMEM((width, width), LOW)
    outer = [pltpu.VMEM((own + HEAD_DIM, width), LOW), pltpu.VMEM((tall, width), LOW)]

    term, entry, tok, triple, context = second_run(
        second_one_kernel, plan, sections, info, ring, (position, live), (in_all, out_all),
        [low, full, low, mixed, shape(rows, own + HEAD_DIM)],
        [pltpu.VMEM((rows, width), FULL), square] + outer,
    )
    term, resid, hid_low, expanded, active = second_run(
        second_two_kernel, plan, sections, info, around(term), (entry, affine, b_up), (up_all, down_all),
        [low, full, low, full, low],
        [total, square, square],
    )
    term, second, back_two, grad_ret, grad_exp, sums, bias = second_run(
        second_three_kernel, plan, sections, info, around(term), (resid, expanded, top_grad, affine), (up_all, down_all),
        [low, full, full, low, low, shape(8, width, kind=FULL), shape(1, width, kind=FULL)],
        [total, square, square],
    )
    term, back_one, grad_mixed, grad_triple, sums = second_run(
        second_four_kernel, plan, sections, info, around(term),
        (resid, back_two, triple, live, sums, affine), (in_all, out_all),
        [low, full, low, mixed, shape(8, width, kind=FULL)],
        [total, square] + outer,
    )
    saved = (tok, grad_triple, context, grad_mixed, hid_low, grad_exp, active, grad_ret)
    return second, back_one, around(term), sums, bias, saved


def second_rows(plan, width):
    size = 3 * padded(plan.rows) + padded(width // plan.groups // plan.count)
    return -(-size // (16 * plan.groups)) * 16 * plan.groups


def place_tops(info, tops, rows):
    return run(
        tops_kernel,
        1,
        [WHOLE, OUTSIDE],
        [(OUTSIDE, shape(*rows.shape))],
        [
            pltpu.VMEM(rows.shape, LOW),
            pltpu.SemaphoreType.DMA((8,)),
            pltpu.SemaphoreType.DMA((8,)),
        ],
        4,
        info,
        (tops, rows),
    )[0]


def spread_out(groups, mp_at, info, line, steps, before):
    count = len(line)
    rows, width = line[0].shape
    again = before.shape[0] == groups * rows
    return run(
        functools.partial(spread_kernel, groups, mp_at, steps),
        1,
        [OUTSIDE] * (count + 1),
        [(OUTSIDE, shape(groups * rows, width, kind=FULL))],
        [
            pltpu.VMEM((count, rows, width), line[0].dtype),
            pltpu.VMEM((count, rows, width), FULL),
            pltpu.SemaphoreType.DMA((count,)),
            pltpu.SemaphoreType.DMA((count,)),
        ],
        3 if again else 6,
        info,
        (*line, before),
        {count + 1: 0} if again else None,
    )[0]


def unit_rows(plan, width):
    return 2 * padded(plan.rows) + padded(width // plan.groups // plan.count + 8)


def unit_grads(plan, info, active, grad_ret, hid_low, grad_exp, context, grad_mixed, small, saved):
    rows, width = grad_ret.shape
    fixed = pl.BlockSpec((rows, width), lambda m, c: (0, 0))
    moving = pl.BlockSpec((rows, width), lambda m, c: (0, c[plan.mp_at + m]))
    tall = second_rows(plan, width)
    size = unit_rows(plan, width) + tall // plan.groups
    out = pl.BlockSpec((plan.count, 1, size, width), lambda m, c: (0, m, 0, 0))
    square = pltpu.VMEM((width, width), FULL)
    return run(
        functools.partial(unit_grad_kernel, plan),
        plan.groups,
        [moving, fixed, fixed, moving, fixed, fixed] + [WHOLE] * (len(small) + len(saved)),
        [(out, shape(plan.count, plan.groups, size, width))],
        [
            square,
            square,
            pltpu.VMEM((width // LANES * 8, width), FULL),
            pltpu.VMEM((plan.count, tall, width), LOW),
        ],
        19,
        info,
        (active, grad_ret, hid_low, grad_exp, context, grad_mixed, *small, *saved),
    )[0]


def collect(plan, info, unit_own, unit_ring, head_own, head_ring):
    extra = (unit_own.shape[1] - unit_ring[0].shape[0]) * plan.groups
    return run(
        functools.partial(collect_kernel, plan),
        1,
        [WHOLE] * (3 + len(unit_ring) + len(head_ring)),
        [
            (WHOLE, shape(*unit_ring[0].shape, kind=FULL)),
            (WHOLE, shape(*head_ring[0].shape, kind=FULL)),
            (WHOLE, shape(extra, unit_own.shape[2], kind=FULL)),
            (WHOLE, shape(8, LANES, kind=FULL)),
        ],
        [pltpu.VMEM((plan.groups, unit_ring[0].shape[0] - 2 * padded(plan.rows), unit_own.shape[2]), FULL)],
        4,
        info,
        (unit_own, *unit_ring, *head_own, *head_ring),
    )


def update(plan, info, squares, unit_sum, head_sum, second, states):
    outs = [(WHOLE, shape(*state.shape[1:], kind=FULL)) for _ in range(3) for state in states]
    return run(
        functools.partial(update_kernel, plan),
        1,
        [WHOLE] * (4 + len(states)),
        outs + [(WHOLE, shape(8, LANES, kind=FULL))],
        [],
        7,
        info,
        (squares, unit_sum, head_sum, second, *states),
    )


def head_grads(plan, lists, info, tok, grad_triple, early):
    rows, width = grad_triple.shape[0], tok.shape[1]
    out = shape(len(lists[0]), plan.groups // 2, plan.rows, 5 * LANES)
    return run(
        functools.partial(head_grad_kernel, plan, lists),
        1,
        [own_rows(plan, rows, rows, width), WHOLE, OUTSIDE],
        [(WHOLE, out)] * 4,
        [pltpu.VMEM((width, 3 * width), FULL)],
        10,
        info,
        (tok, grad_triple, early),
    )


def swap(value, bit, axis="dp"):
    return lax.ppermute(value, axis, [(i, i ^ bit) for i in range(lax.axis_size(axis))])


def ahead(value, step):
    size = lax.axis_size("mp")
    return lax.ppermute(value, "mp", [(i, (i + step) % size) for i in range(size)])


def onward(value, step):
    size = lax.axis_size("mp")
    return lax.ppermute(
        value, "mp", [(i, i + step) for i in range(size) if 0 <= i + step < size]
    )


def all_sum(value, axes):
    for axis in axes:
        bit = 1
        while bit < lax.axis_size(axis):
            value = value + swap(value, bit, axis)
            bit *= 2
    return value


def around(value):
    return [value] + [ahead(value, step) for step in range(1, lax.axis_size("mp"))]


def bits_of(count):
    bits, bit = [], 2
    while bit < count:
        bits.append(bit)
        bit *= 2
    return bits


def tie(value, *first):
    return lax.optimization_barrier((value, first))[0]


def gather(ring, gates, hold=()):
    half = len(ring) // 2
    bits = bits_of(lax.axis_size("dp"))
    held = [[([0], jnp.stack(ring[:half])[None])], [([0], jnp.stack(ring[half:])[None])]]
    arrived = []
    for stage in range(len(bits)):
        arrived.append([])
        for which, order in enumerate((bits, bits[::-1])):
            bit = order[stage]
            places = sum((member[0] for member in held[which]), [])
            block = [member[1] for member in held[which]]
            block = block[0] if len(block) == 1 else jnp.concatenate(block)
            if stage < len(gates):
                block = tie(block, *gates[stage])
            got = swap(block, bit)
            arrived[-1].append(got)
            held[which] = [(places, block), ([j ^ bit for j in places], got)]
    pieces = []
    for which in range(2):
        for places, block in held[which]:
            pieces.append((places, which, block))
            pieces.append(([j ^ 1 for j in places], which, swap(tie(block, *hold), 1)))
    return pieces, arrived


def pick(stack, order, count):
    return jnp.concatenate(
        [lax.dynamic_slice_in_dim(stack, order[at], 1) for at in range(count)]
    )


def straighten(pieces, device):
    merged = []
    for which in range(2):
        mine = [member for member in pieces if member[1] == which]
        places = sum((member[0] for member in mine), [])
        block = jnp.concatenate([member[2] for member in mine])
        order = sorted(range(len(places)), key=lambda at: places[at])
        block = pick(jnp.stack([block[at] for at in order]), device ^ jnp.arange(len(places)), len(places))
        count, groups, rows, lanes = block.shape
        block = block.transpose(1, 0, 2, 3).reshape(1, groups, count * rows, lanes)
        merged.append(([0], which, block))
    return merged


def places_of(order):
    places = [0]
    for bit in reversed(order):
        places = places + [place | bit for place in places]
    return places


def add(left, right):
    return (left.astype(FULL) + right.astype(FULL)).astype(LOW)


def reduce_dp(keep, send, order, early):
    got = tie(swap(send, 1), *early)
    for bit in order:
        half = keep.shape[0] // 2
        out = swap(add(keep[half:], got[half:]), bit)
        keep, got = add(keep[:half], got[:half]), out
    return keep[0], got[0]


def adam(state, grad, factor):
    clipped = grad * factor
    first = beta_one * state[1] + (1.0 - beta_one) * clipped
    second = beta_two * state[2] + (1.0 - beta_two) * clipped * clipped
    fixed_first = first / (1.0 - beta_one**adam_step)
    fixed_second = second / (1.0 - beta_two**adam_step)
    master = state[0] - rate * (
        fixed_first / (jnp.sqrt(fixed_second) + adam_eps) + decay * state[0]
    )
    return (master, first, second)


def shards(
    tokens,
    cotangent,
    counts,
    attend_in,
    attend_out,
    expand_in,
    expand_bias,
    expand_out,
    affine_state,
    position_state,
):
    shards_dp, groups = lax.axis_size("dp"), lax.axis_size("mp")
    device, mine = lax.axis_index("dp"), lax.axis_index("mp")
    width = tokens.shape[1]
    slots = counts.size // groups
    piece = width // shards_dp
    share = attend_out.shape[2]
    before = (mine - jnp.arange(groups)) % groups
    info = jnp.concatenate(
        [
            lax.dynamic_slice_in_dim(counts.reshape(-1), mine * slots, slots),
            before,
            device ^ jnp.arange(shards_dp),
        ]
    ).astype(jnp.int32)
    bits = bits_of(shards_dp)
    lists = (places_of(bits), places_of(bits[::-1]))
    mp_at, dp_at = slots, slots + groups

    heads_block = heads_block_of(info, attend_in, expand_bias, affine_state, position_state)
    up_block = units_block_of(info, 0, (expand_in,))
    units_block = units_block_of(info, 0, (expand_out, attend_out))
    second_block = units_block_of(info, 1, (attend_in, expand_in, expand_out, attend_out))
    units_all = lax.all_gather(units_block, ("mp", "dp"), axis=0)
    units_all = units_all.reshape(groups, shards_dp, -1, width)
    heads_ring = around(heads_block)
    heads_pieces, heads_got = gather(heads_ring, [])
    second_all = lax.all_gather(second_block, "dp", axis=0)

    step, low_share = padded(piece), padded(share)
    up_ring = around(tie(up_block, *heads_ring[1:]))
    units_sections = [(0, piece), (step, low_share)]
    units = [units_all] * 2
    sections = [(0, piece), (3 * step, low_share), (step, piece), (2 * step, piece)]
    weights = [second_all] * 4
    load_info = info
    if piece % 16:
        heads_pieces = straighten(heads_pieces, device)
        load_info = info.at[dp_at].set(0)
        units = [
            units_all[:, :, base : base + rows].reshape(groups, 1, shards_dp * rows, width)
            for base, rows in units_sections
        ]
        weights = [
            second_all[:, base : base + rows].reshape(1, shards_dp * rows, width)
            for base, rows in sections
        ]
        units_sections = [(0, shards_dp * rows) for _, rows in units_sections]
        sections = [(0, shards_dp * rows) for _, rows in sections]

    def plan_of(pieces, rows):
        places = [(member[0], member[1]) for member in pieces]
        return Plan(groups, places, rows, mp_at, dp_at, shards_dp)

    heads_plan = plan_of(heads_pieces, heads_pieces[0][2].shape[2])
    own_plan = plan_of([], piece)
    heads_pieces = [member[2] for member in heads_pieces]

    triple, context, chances, w_in, affine_one, affine_two, position, b_up = attend_forward(
        heads_plan, load_info, tokens, heads_pieces
    )
    up_pieces, _ = gather(up_ring, heads_got[-1:], (b_up,))
    if piece % 16:
        up_pieces = straighten([(p, w, b[:, :, :piece]) for p, w, b in up_pieces], device)
    up_plan = plan_of(up_pieces, up_pieces[0][2].shape[2])
    up_pieces = [member[2] for member in up_pieces]
    resid, hid_low, expanded, resid_two, first, tops, w_out = feed_forward(
        up_plan, units_sections, load_info, tokens, context, affine_one, b_up, up_pieces, units
    )

    keep_heads = (counts > 0).astype(FULL)
    live = jnp.concatenate([keep_heads, keep_heads], axis=1)
    keep_heads = keep_heads.reshape(-1, 1)
    top_grad = cotangent.reshape(-1, SEG, width)[:, 0].astype(FULL) * keep_heads
    tops_ring = around(tops)
    second, back_heads, heads_ring, sums_two, bias_two, saved = second_layer(
        sections, own_plan, info, tops_ring, position, live, top_grad, affine_two, affine_one, weights
    )
    out_rows = lax.all_gather(first, "mp", axis=0, tiled=True)
    grad_resid, active, grad_exp, grad_ret, grad_mixed, sums_one, bias, grad_heads = feed_backward(
        up_plan,
        units_sections,
        load_info,
        cotangent,
        back_heads,
        heads_ring,
        resid_two,
        expanded,
        resid,
        affine_one,
        up_pieces,
        units,
    )
    small = (sums_one, sums_two, grad_heads, bias, bias_two)
    unit_out = unit_grads(
        own_plan,
        info,
        active,
        grad_ret,
        hid_low,
        grad_exp,
        context,
        grad_mixed,
        small,
        saved,
    )
    unit_terms = lax.psum_scatter(unit_out, "dp", scatter_dimension=0)
    grad_in, grad_triple = attend_backward(
        info, grad_resid, grad_mixed, triple, chances, context, w_out, w_in, unit_out
    )
    merged = place_tops(info, second * keep_heads, out_rows)
    keep_a, send_a, keep_b, send_b = head_grads(own_plan, lists, tie(info, merged), tokens, grad_triple, unit_out)

    grad_line = [(onward(grad_in, 1), onward(grad_in, -1))]
    left_a, right_a = reduce_dp(keep_a, send_a, bits, grad_line[0])
    left_b, right_b = reduce_dp(keep_b, send_b, bits[::-1], grad_line[0])
    terms = [(left_a[s], right_a[s]) for s in range(1, groups // 2)]
    terms += [(left_b[s], right_b[s]) for s in range(groups - groups // 2)]
    last = tie(grad_line[0], keep_a)
    grad_line.append((onward(last[0], 1), onward(last[1], -1)))
    head_ring = [
        ahead(tie(add(*term), *grad_line[1]), -at - 1) for at, term in enumerate(terms)
    ]
    tall = unit_rows(own_plan, width)
    line = lax.broadcasted_iota(jnp.int32, (tall, width), 0) - 2 * step
    lane = lax.broadcasted_iota(jnp.int32, (tall, width), 1)
    shared = (line >= 0) & (line < 8) & ~((line >= 6) & (lane < LANES))
    unit_ring = [
        ahead(
            tie(jnp.where(shared, unit_terms[0, :tall], unit_terms[at, :tall]), *grad_line[1]), -at
        )
        for at in range(1, groups)
    ]
    unit_sum, head_sum, second_sum, squares = collect(
        own_plan, info, unit_terms, unit_ring, (left_a, right_a), head_ring
    )
    squares = all_sum(squares, ("mp",))
    last = tie(grad_line[1], squares)
    grad_line.append((onward(last[0], 1), onward(last[1], -1)))
    squares = all_sum(squares, ("dp",))
    input_grad = spread_out(
        groups,
        mp_at,
        info,
        [grad_in, *grad_line[0], *grad_line[1]],
        (0, -1, 1, -2, 2),
        grad_line[1][0],
    )
    input_grad = spread_out(groups, mp_at, info, grad_line[2], (-3, 3), input_grad)
    states = (
        attend_in,
        attend_out,
        expand_in,
        expand_bias,
        expand_out,
        affine_state,
        position_state,
    )
    assert groups == 4
    *updated, norm = update(own_plan, info, squares, unit_sum, head_sum, second_sum, states)
    return (merged, input_grad, norm[0, 0], *updated)


def solution(mesh):
    in_specs = (
        P("dp", None),
        P("dp", None),
        P("dp", None),
        P(None, None, "dp", "mp"),
        P(None, None, ("mp", "dp"), None),
        P(None, None, "dp", "mp"),
        P(None, None, ("mp", "dp")),
        P(None, None, ("mp", "dp"), None),
        P(None, None, None, "dp"),
        P(None, None, "dp"),
    )
    out_specs = (
        P("dp", None),
        P("dp", None),
        P(),
        P(None, "dp", "mp"),
        P(None, ("mp", "dp"), None),
        P(None, "dp", "mp"),
        P(None, ("mp", "dp")),
        P(None, ("mp", "dp"), None),
        P(None, None, "dp"),
        P(None, "dp"),
        P(None, "dp", "mp"),
        P(None, ("mp", "dp"), None),
        P(None, "dp", "mp"),
        P(None, ("mp", "dp")),
        P(None, ("mp", "dp"), None),
        P(None, None, "dp"),
        P(None, "dp"),
        P(None, "dp", "mp"),
        P(None, ("mp", "dp"), None),
        P(None, "dp", "mp"),
        P(None, ("mp", "dp")),
        P(None, ("mp", "dp"), None),
        P(None, None, "dp"),
        P(None, "dp"),
    )
    return jax.shard_map(shards, mesh=mesh, in_specs=in_specs, out_specs=out_specs, check_vma=False)
```
